32 devices in a mesh: tm: 8 (over y, x, core), unit: 4 (over z).
Axes of the slice: x: 2, y: 2, z: 4, core: 2. Of those that a mesh axis runs over, the one named last changes fastest.
Arguments:
- recording: bfloat16 [65536, 384], P(('tm', 'unit')), may hold values from -6 to 6
- spike_times: int32 [1024], P(('tm', 'unit')), may hold values from 30 to 65505, as said below
- unit_labels: int32 [1024], P(('tm', 'unit')), may hold values from 0 to 255, as said below
- old_templates: bfloat16 [256, 23424], P('unit'), may hold values from -3 to 3
Outputs:
- templates: bfloat16 [256, 23424], P('unit', 'tm')
- scores: float32 [256, 32768], P('unit', 'tm')
The draws below stay inside these ranges and needn't reach their ends.
Inputs may be any that keep to these rules, and one draw needn't show every extreme that they name: `spike_times`: the spikes lie in blocks of 32, block b on the device of flattened index b over tm and unit; the times of block b lie in b * 2048 + 30 to (b + 1) * 2048 - 31, and both ends are reached in every block. `unit_labels`: labels lie in 0 to 255; the panel of a label is label // 64. In each block of 32 spikes at most 8 labels fall in one panel, and on each index of tm one panel receives exactly 8 from every block of that index.
All inputs are finite; a program needn't handle non-finite values.
Results may differ from the reference program's by a relative error of at most 0.0027.
Values may be sent and summed in bfloat16 or wider, within the bound.
No kernel may reach another device: no remote copies, remote signals or barrier semaphores. Data moves between devices by JAX's collectives and lax.ppermute only.
A program may use at most 64 MiB of HBM per device.

```python
import jax
import jax.numpy as jnp
from jax import lax

C = 384
TAPS = 61
PANEL = 64
STRIDE = 2
SPK_DEV = 32
CAP = 8
OWNERS = 4
UNITS = 256
FEAT = 23424
HALF = 30
SLAB = 8192
SAMPLES = 65536
WINDOWS = 32768
SPIKES = 1024


def draw_spike_times(key, part):
    blocks = SPIKES // SPK_DEV
    sub = SLAB // OWNERS

    def one_block(index):
        lower = index * sub + HALF
        upper = index * sub + sub - HALF
        values = jax.random.randint(jax.random.fold_in(key, index), (SPK_DEV,), lower, upper)
        places = jnp.arange(SPK_DEV)
        values = jnp.where(places == 0, upper - 1, values)
        values = jnp.where(places == 1, lower, values)
        return values
    return jax.vmap(one_block)(jnp.arange(blocks)).reshape(-1).astype(jnp.int32)


def draw_unit_labels(key, part):
    blocks = SPIKES // SPK_DEV
    hot_key = jax.random.fold_in(key, 7)
    base_key = jax.random.fold_in(key, 11)

    def one_block(index):
        row = index // OWNERS
        hot = jax.random.randint(jax.random.fold_in(hot_key, row), (), 0, OWNERS)
        block_key = jax.random.fold_in(base_key, index)
        first_key, second_key, third_key = jax.random.split(block_key, 3)
        others = jnp.arange((OWNERS - 1) * CAP) // CAP
        others = others + (others >= hot).astype(others.dtype)
        taken = jax.random.permutation(first_key, others)[:SPK_DEV - CAP]
        owner_list = jnp.concatenate([jnp.full((CAP,), hot, others.dtype), taken])
        owner_list = jax.random.permutation(second_key, owner_list)
        within = jax.random.randint(third_key, (SPK_DEV,), 0, PANEL)
        return owner_list * PANEL + within
    return jax.vmap(one_block)(jnp.arange(blocks)).reshape(-1).astype(jnp.int32)


def block_scale(rng, shape, pieces, low, largest):
    def one(position, shards_of):
        heights = jax.random.uniform(jax.random.fold_in(jax.random.fold_in(rng, 6), position), (shards_of,), jnp.float32, low / len(pieces), largest / len(pieces))
        return jnp.repeat(jnp.exp(heights), shape[position] // shards_of).reshape((-1,) + (1,) * (len(shape) - position - 1))

    loudness = one(*pieces[0])
    for cut in pieces[1:]:
        loudness = loudness * one(*cut)
    return loudness


def gaussian(own_key, shape, width, bound, cuts=(), kind=jnp.bfloat16):
    drawn = jax.random.normal(own_key, shape, jnp.float32) * width
    if len(cuts) > 0:
        drawn = block_scale(own_key, shape, cuts, -0.22, 0.18) * drawn
    return jnp.clip(drawn, min=-bound, max=bound).astype(kind)


def setup_inputs(seed: int = 0) -> dict:
    arg_keys = jax.random.split(jax.random.key(seed), 5)
    recording = gaussian(arg_keys[0], (SAMPLES, C), 1.0, 6.0, ((0, 32),))
    spike_times = draw_spike_times(jax.random.fold_in(arg_keys[4], 71), 0)
    unit_labels = draw_unit_labels(jax.random.fold_in(arg_keys[4], 71), 0)
    old_templates = gaussian(arg_keys[3], (UNITS, FEAT), 0.5, 3.0, ((0, 4),))
    return dict(recording=recording, spike_times=spike_times, unit_labels=unit_labels, old_templates=old_templates)


def reference(recording, spike_times, unit_labels, old_templates):
    feat = C * TAPS

    def add_one(i, carry):
        sums, counts = carry
        start = (spike_times[i] - HALF).astype(jnp.int32)
        snip = lax.dynamic_slice(recording, (start, jnp.int32(0)), (TAPS, C))
        row = snip.T.reshape(1, feat).astype(jnp.float32)
        label = unit_labels[i].astype(jnp.int32)
        current = lax.dynamic_slice(sums, (label, jnp.int32(0)), (1, feat))
        sums = lax.dynamic_update_slice(sums, current + row, (label, jnp.int32(0)))
        counts = counts.at[label].add(jnp.float32(1.0))
        return (sums, counts)
    sums0 = jnp.zeros((UNITS, feat), jnp.float32)
    counts0 = jnp.zeros((UNITS,), jnp.float32)
    sums, counts = lax.fori_loop(0, SPIKES, add_one, (sums0, counts0))
    weight = counts / (counts + 4.0)
    mean = sums / jnp.maximum(counts, 1.0)[:, None]
    old = old_templates.astype(jnp.float32)
    templates = (old + weight[:, None] * (mean - old)).astype(jnp.bfloat16)
    extended = jnp.concatenate([recording, jnp.zeros((TAPS - 1, C), jnp.bfloat16)], axis=0)
    signal = extended.astype(jnp.float32)[None]
    kernels = templates.astype(jnp.float32).reshape(OWNERS, PANEL, C, TAPS)

    def one_panel(kernel):
        out = lax.conv_general_dilated(signal, kernel, (STRIDE,), 'VALID', dimension_numbers=('NWC', 'OIW', 'NCW'), precision=lax.Precision.HIGHEST)
        return out[0]
    scores = lax.map(one_panel, kernels).reshape(UNITS, WINDOWS)
    scores = scores * (1.0 / jnp.sqrt(jnp.float32(feat)))
    return (templates, scores)
```

```python
import functools

import jax
import jax.numpy as jnp
from jax import lax
from jax.experimental import pallas as pl
from jax.experimental.pallas import tpu as pltpu
from jax.sharding import PartitionSpec as P

STRIDE = 2
CAP = 8
FOLD = 4
ROWS = STRIDE * FOLD
AXES = ("tm", "unit")
VMEM_LIMIT = 56 * 1024 * 1024
NT = (((1,), (1,)), ((), ()))


def params():
    return pltpu.CompilerParams(vmem_limit_bytes=VMEM_LIMIT)


def pack_kernel(
    taps, panel, owners, tm_count, tpd, times_ref, labels_ref, base_ref, rec_ref, send_ref, buf, cnt
):
    spikes = times_ref.shape[0]
    sub_rows = rec_ref.shape[0]
    padded = tm_count * tpd
    win = padded + 16
    base = base_ref[0]
    for o in range(owners):
        cnt[o] = 0
    if owners * CAP > spikes:
        buf[...] = jnp.zeros_like(buf)
    tap = lax.broadcasted_iota(jnp.int32, (padded, win), 0)
    col = lax.broadcasted_iota(jnp.int32, (padded, win), 1)
    gap = jnp.where(tap < taps, col - tap, -1)

    def one(s):
        first = times_ref[s] - base
        start = jnp.minimum((first // 16) * 16, sub_rows - win)
        owner = labels_ref[s] // panel
        slot = cnt[owner]
        cnt[owner] = slot + 1
        pick = (gap == first - start).astype(jnp.bfloat16)
        window = rec_ref[pl.ds(pl.multiple_of(start, 16), win), :]
        snip = jnp.dot(pick, window, preferred_element_type=jnp.float32)
        for t in range(tm_count):
            row = (t * owners + owner) * (CAP * tpd) + slot * tpd
            buf[pl.ds(pl.multiple_of(row, tpd), tpd), :] = snip[t * tpd : (t + 1) * tpd]

    def group(g, carry):
        for i in range(8):
            one(g * 8 + i)
        return carry

    lax.fori_loop(0, spikes // 8, group, 0)
    send_ref[...] = buf[...].astype(jnp.bfloat16)


def pack(times, labels, base, rec, taps, panel, owners, tm_count, tpd):
    chans = rec.shape[1]
    rows = owners * tm_count * CAP * tpd
    smem = pl.BlockSpec(memory_space=pltpu.SMEM)
    vmem = pl.BlockSpec(memory_space=pltpu.VMEM)
    return pl.pallas_call(
        functools.partial(pack_kernel, taps, panel, owners, tm_count, tpd),
        out_shape=jax.ShapeDtypeStruct((rows, chans), jnp.bfloat16),
        in_specs=[smem, smem, smem, vmem],
        out_specs=vmem,
        scratch_shapes=[
            pltpu.VMEM((rows, chans), jnp.float32),
            pltpu.SMEM((owners,), jnp.int32),
        ],
        compiler_params=params(),
        cost_estimate=pl.CostEstimate(flops=10**8, bytes_accessed=4 * 10**6, transcendentals=0),
        name="pack",
    )(times, labels, base, rec)


def fold_kernel(rec_ref, out_ref):
    rows, chans = rec_ref.shape
    block = 16 * ROWS
    new = lax.broadcasted_iota(jnp.int32, (block, block), 0)
    old = lax.broadcasted_iota(jnp.int32, (block, block), 1)
    perm = (old == (new % 16) * ROWS + new // 16).astype(jnp.bfloat16)
    for b in range(rows // block):
        part = jnp.dot(perm, rec_ref[b * block : (b + 1) * block, :], preferred_element_type=jnp.float32)
        part = part.astype(jnp.bfloat16)
        for r in range(ROWS):
            out_ref[b * 16 : (b + 1) * 16, r * chans : (r + 1) * chans] = part[r * 16 : (r + 1) * 16]


def fold(rec):
    rows, chans = rec.shape
    vmem = pl.BlockSpec(memory_space=pltpu.VMEM)
    return pl.pallas_call(
        fold_kernel,
        out_shape=jax.ShapeDtypeStruct((rows // ROWS, ROWS * chans), jnp.bfloat16),
        in_specs=[vmem],
        out_specs=vmem,
        compiler_params=params(),
        cost_estimate=pl.CostEstimate(flops=2 * 10**8, bytes_accessed=4 * 10**6, transcendentals=0),
        name="fold",
    )(rec)


def refine_kernel(tpd, key_ref, got_ref, old_ref, out_ref, sums):
    panel = old_ref.shape[0]
    rows, chans = got_ref.shape
    step = min(rows, 2048)
    count = jnp.zeros((panel, 1), jnp.float32)
    for b in range(rows // step):
        key = key_ref[:, b * step : (b + 1) * step]
        wanted = lax.broadcasted_iota(jnp.int32, (tpd * panel, step), 0)
        wanted = (wanted % panel) * tpd + wanted // panel
        hit = (wanted == key).astype(jnp.float32)
        count = count + jnp.sum(hit[:panel], axis=1, keepdims=True)
        part = jnp.dot(
            hit.astype(jnp.bfloat16),
            got_ref[b * step : (b + 1) * step, :],
            preferred_element_type=jnp.float32,
        )
        if b == 0:
            sums[...] = part
        else:
            sums[...] += part
    weight = count / (count + 4.0)
    most = jnp.maximum(count, 1.0)
    for t in range(tpd):
        base = old_ref[:, t * chans : (t + 1) * chans].astype(jnp.float32)
        mean = sums[t * panel : (t + 1) * panel, :] / most
        out_ref[:, t * chans : (t + 1) * chans] = (base + weight * (mean - base)).astype(jnp.bfloat16)


def refine(key, got, old, tpd):
    vmem = pl.BlockSpec(memory_space=pltpu.VMEM)
    panel = old.shape[0]
    return pl.pallas_call(
        functools.partial(refine_kernel, tpd),
        out_shape=jax.ShapeDtypeStruct(old.shape, jnp.bfloat16),
        in_specs=[vmem] * 3,
        out_specs=vmem,
        scratch_shapes=[pltpu.VMEM((tpd * panel, got.shape[1]), jnp.float32)],
        compiler_params=params(),
        cost_estimate=pl.CostEstimate(flops=8 * 10**8, bytes_accessed=3 * 10**6, transcendentals=0),
        name="refine",
    )(key, got, old)


def correlate_kernel(chans, scale, odd_ref, t_ref, e_ref, out_ref, rhs, part, acc):
    blocks, panel, lanes = t_ref.shape
    height = e_ref.shape[0] // 2
    keep = acc.shape[0] // 2
    shift = STRIDE * chans
    for a in range(blocks + 1):
        used = lanes if a < blocks else lanes // 2
        for q in range(FOLD):
            rows = slice(q * panel, (q + 1) * panel)
            cut = q * shift
            if cut > 0:
                low = min(cut, used)
                if a > 0:
                    rhs[rows, 0:low] = t_ref[a - 1, :, lanes - cut : lanes - cut + low]
                else:
                    rhs[rows, 0:low] = jnp.zeros((panel, low), jnp.bfloat16)
            if cut < used:
                if a < blocks:
                    rhs[rows, cut:used] = t_ref[a, :, 0 : used - cut]
                else:
                    rhs[rows, cut:used] = jnp.zeros((panel, used - cut), jnp.bfloat16)
        part[...] = lax.dot_general(
            e_ref[:, 0:used], rhs[:, 0:used], NT, preferred_element_type=jnp.float32
        )
        for h in range(2):
            found = part[h * height + a : h * height + a + keep, :]
            if a == 0:
                acc[h * keep : (h + 1) * keep, :] = found
            else:
                acc[h * keep : (h + 1) * keep, :] += found
    width = 128
    place = lax.broadcasted_iota(jnp.int32, (FOLD * width, FOLD * width), 0)
    lane = lax.broadcasted_iota(jnp.int32, (FOLD * width, FOLD * width), 1)
    weave = (lane == (place % width) * FOLD + place // width).astype(jnp.bfloat16)
    per_half = keep // width
    odd = odd_ref[0]
    for h in range(2):
        side = odd if h == 0 else 1 - odd
        for b in range(per_half):
            first = h * keep + b * width
            turned = acc[first : first + width, :].T * scale
            row = jnp.concatenate([turned[q * panel : (q + 1) * panel] for q in range(FOLD)], axis=1)
            high = row.astype(jnp.bfloat16)
            found = jnp.dot(high, weave, preferred_element_type=jnp.float32)
            if out_ref.dtype == jnp.float32:
                rest = (row - high.astype(jnp.float32)).astype(jnp.bfloat16)
                found = found + jnp.dot(rest, weave, preferred_element_type=jnp.float32)
            at = pl.multiple_of((side * per_half + b) * (FOLD * width), FOLD * width)
            out_ref[:, pl.ds(at, FOLD * width)] = found.astype(out_ref.dtype)


def correlate(odd, t_all, e_two, keep, chans, scale, dtype):
    panel = t_all.shape[1]
    smem = pl.BlockSpec(memory_space=pltpu.SMEM)
    vmem = pl.BlockSpec(memory_space=pltpu.VMEM)
    return pl.pallas_call(
        functools.partial(correlate_kernel, chans, scale),
        out_shape=jax.ShapeDtypeStruct((panel, 2 * keep * FOLD), dtype),
        in_specs=[smem, vmem, vmem],
        out_specs=vmem,
        scratch_shapes=[
            pltpu.VMEM((FOLD * panel, ROWS * chans), jnp.bfloat16),
            pltpu.VMEM((e_two.shape[0], FOLD * panel), jnp.float32),
            pltpu.VMEM((2 * keep, FOLD * panel), jnp.float32),
        ],
        compiler_params=params(),
        cost_estimate=pl.CostEstimate(flops=8 * 10**9, bytes_accessed=8 * 10**6, transcendentals=0),
        name="correlate",
    )(odd, t_all, e_two)


def by_tap(parts, chans):
    count, panel, lanes = parts.shape
    per = ROWS * chans // lanes
    if per == 1:
        return parts
    parts = parts.reshape(count // per, per, panel, lanes)
    return jnp.transpose(parts, (0, 2, 1, 3)).reshape(count // per, panel, per * lanes)


def body(recording, spike_times, unit_labels, old_templates):
    sub_rows, chans = recording.shape
    panel, feat = old_templates.shape
    taps = feat // chans
    half = (taps - 1) // 2
    owners = lax.axis_size("unit")
    tm_count = lax.axis_size("tm")
    devices = owners * tm_count
    spikes = spike_times.shape[0]
    tm_pos = lax.axis_index("tm")
    unit_pos = lax.axis_index("unit")
    flat_pos = tm_pos * owners + unit_pos
    tpd = -(-taps // tm_count)
    padded = tpd * tm_count
    keep = sub_rows // ROWS
    scale = 1.0 / (float(feat) ** 0.5)

    base = (flat_pos * sub_rows + half).astype(jnp.int32).reshape(1)
    groups = padded // ROWS
    send = pack(spike_times, unit_labels, base, recording, taps, panel, owners, groups, ROWS)
    if tpd != ROWS:
        send = send.reshape(groups, owners, CAP, ROWS // tpd, tpd, chans)
        send = jnp.transpose(send, (0, 3, 1, 2, 4, 5))
    got = lax.all_to_all(
        send.reshape(devices, CAP * tpd, chans), AXES, split_axis=0, concat_axis=0, tiled=True
    ).reshape(devices * CAP * tpd, chans)

    labels = lax.all_gather(unit_labels, AXES, axis=0, tiled=True).reshape(devices, spikes)
    mine = labels // panel == unit_pos
    counted = mine.astype(jnp.int32)
    rank = jnp.cumsum(counted, axis=1) - counted
    here = mine[:, :, None] & (rank[:, :, None] == jnp.arange(CAP)[None, None, :])
    within = jnp.sum(jnp.where(here, (labels % panel + 1)[:, :, None], 0), axis=1) - 1
    key = (within[:, :, None] * tpd + jnp.arange(tpd)[None, None, :]).reshape(1, -1)

    cube = old_templates.reshape(panel, chans, taps)
    cube = jnp.pad(cube, ((0, 0), (0, 0), (0, padded - taps)))
    cube = lax.dynamic_slice_in_dim(cube, tm_pos * tpd, tpd, 2)
    old = jnp.transpose(cube, (0, 2, 1)).reshape(panel, tpd * chans)

    folded = fold(recording)
    halo = padded // ROWS
    following = lax.ppermute(folded[:halo], AXES, [(i, i - 1) for i in range(1, devices)])
    spare = jnp.zeros((16 - halo % 16, ROWS * chans), jnp.bfloat16)
    mine_rows = jnp.concatenate([folded, following, spare], axis=0)
    their_rows = lax.ppermute(mine_rows, "unit", [(i, i ^ 1) for i in range(owners)])
    e_two = jnp.concatenate([mine_rows, their_rows], axis=0)

    fresh = refine(key, got, old, tpd)
    odd = (unit_pos % 2).astype(jnp.int32).reshape(1)
    own_panel = lax.all_gather(fresh, "tm", axis=0, tiled=False)
    width = 2 * keep * FOLD
    scores = jnp.zeros((panel, owners // 2 * width), jnp.float32)
    found = []
    for m in range(1, owners // 2):
        ahead = [(i, (i + 2 * m) % owners) for i in range(owners)]
        back = [(j, i) for i, j in ahead]
        other = lax.all_gather(lax.ppermute(fresh, "unit", ahead), "tm", axis=0, tiled=False)
        out = correlate(odd, by_tap(other, chans), e_two, keep, chans, scale, jnp.bfloat16)
        found.append((lax.ppermute(out, "unit", back), ((unit_pos + 2 * m) % owners) // 2))
    found.append((correlate(odd, by_tap(own_panel, chans), e_two, keep, chans, scale, jnp.float32), unit_pos // 2))
    for out, pair in found:
        scores = lax.dynamic_update_slice_in_dim(
            scores, out.astype(jnp.float32), pair * width, 1
        )

    share = chans // tm_count
    part = own_panel.reshape(tm_count, panel, tpd, chans)
    part = lax.dynamic_slice_in_dim(part, tm_pos * share, share, 3)
    part = jnp.transpose(part, (1, 3, 0, 2)).reshape(panel, share, padded)[:, :, :taps]
    return (part.reshape(panel, share * taps), scores)


def solution(mesh):
    in_specs = (P(AXES, None), P(AXES), P(AXES), P("unit", None))
    out_specs = (P("unit", "tm"), P("unit", "tm"))
    return jax.shard_map(body, mesh=mesh, in_specs=in_specs, out_specs=out_specs, check_vma=False)
```

```python
import functools

import jax
import jax.numpy as jnp
from jax import lax
from jax.experimental import pallas as pl
from jax.experimental.pallas import tpu as pltpu
from jax.sharding import PartitionSpec as P

STRIDE = 2
CAP = 8
FOLD = 4
ROWS = STRIDE * FOLD
AXES = ("tm", "unit")
VMEM_LIMIT = 56 * 1024 * 1024
NT = (((1,), (1,)), ((), ()))


def params():
    return pltpu.CompilerParams(vmem_limit_bytes=VMEM_LIMIT)


def pack_kernel(
    taps, panel, owners, tm_count, tpd, times_ref, labels_ref, base_ref, rec_ref, send_ref, buf, cnt
):
    spikes = times_ref.shape[0]
    sub_rows = rec_ref.shape[0]
    padded = tm_count * tpd
    win = padded + 16
    base = base_ref[0]
    for o in range(owners):
        cnt[o] = 0
    if owners * CAP > spikes:
        buf[...] = jnp.zeros_like(buf)
    tap = lax.broadcasted_iota(jnp.int32, (padded, win), 0)
    col = lax.broadcasted_iota(jnp.int32, (padded, win), 1)
    gap = jnp.where(tap < taps, col - tap, -1)

    def one(s):
        first = times_ref[s] - base
        start = jnp.minimum((first // 16) * 16, sub_rows - win)
        owner = labels_ref[s] // panel
        slot = cnt[owner]
        cnt[owner] = slot + 1
        pick = (gap == first - start).astype(jnp.bfloat16)
        window = rec_ref[pl.ds(pl.multiple_of(start, 16), win), :]
        snip = jnp.dot(pick, window, preferred_element_type=jnp.float32)
        for t in range(tm_count):
            row = (t * owners + owner) * (CAP * tpd) + slot * tpd
            buf[pl.ds(pl.multiple_of(row, tpd), tpd), :] = snip[t * tpd : (t + 1) * tpd]

    def group(g, carry):
        for i in range(8):
            one(g * 8 + i)
        return carry

    lax.fori_loop(0, spikes // 8, group, 0)
    send_ref[...] = buf[...].astype(jnp.bfloat16)


def pack(times, labels, base, rec, taps, panel, owners, tm_count, tpd):
    chans = rec.shape[1]
    rows = owners * tm_count * CAP * tpd
    smem = pl.BlockSpec(memory_space=pltpu.SMEM)
    vmem = pl.BlockSpec(memory_space=pltpu.VMEM)
    return pl.pallas_call(
        functools.partial(pack_kernel, taps, panel, owners, tm_count, tpd),
        out_shape=jax.ShapeDtypeStruct((rows, chans), jnp.bfloat16),
        in_specs=[smem, smem, smem, vmem],
        out_specs=vmem,
        scratch_shapes=[
            pltpu.VMEM((rows, chans), jnp.float32),
            pltpu.SMEM((owners,), jnp.int32),
        ],
        compiler_params=params(),
        cost_estimate=pl.CostEstimate(flops=10**8, bytes_accessed=4 * 10**6, transcendentals=0),
        name="pack",
    )(times, labels, base, rec)


def fold_kernel(rec_ref, out_ref):
    rows, chans = rec_ref.shape
    block = 16 * ROWS
    new = lax.broadcasted_iota(jnp.int32, (block, block), 0)
    old = lax.broadcasted_iota(jnp.int32, (block, block), 1)
    perm = (old == (new % 16) * ROWS + new // 16).astype(jnp.bfloat16)
    for b in range(rows // block):
        part = jnp.dot(perm, rec_ref[b * block : (b + 1) * block, :], preferred_element_type=jnp.float32)
        part = part.astype(jnp.bfloat16)
        for r in range(ROWS):
            out_ref[b * 16 : (b + 1) * 16, r * chans : (r + 1) * chans] = part[r * 16 : (r + 1) * 16]


def fold(rec):
    rows, chans = rec.shape
    vmem = pl.BlockSpec(memory_space=pltpu.VMEM)
    return pl.pallas_call(
        fold_kernel,
        out_shape=jax.ShapeDtypeStruct((rows // ROWS, ROWS * chans), jnp.bfloat16),
        in_specs=[vmem],
        out_specs=vmem,
        compiler_params=params(),
        cost_estimate=pl.CostEstimate(flops=2 * 10**8, bytes_accessed=4 * 10**6, transcendentals=0),
        name="fold",
    )(rec)


def refine_kernel(tpd, key_ref, got_ref, old_ref, out_ref, sums):
    panel = old_ref.shape[0]
    rows, chans = got_ref.shape
    step = min(rows, 2048)
    count = jnp.zeros((panel, 1), jnp.float32)
    for b in range(rows // step):
        key = key_ref[:, b * step : (b + 1) * step]
        wanted = lax.broadcasted_iota(jnp.int32, (tpd * panel, step), 0)
        wanted = (wanted % panel) * tpd + wanted // panel
        hit = (wanted == key).astype(jnp.float32)
        count = count + jnp.sum(hit[:panel], axis=1, keepdims=True)
        part = jnp.dot(
            hit.astype(jnp.bfloat16),
            got_ref[b * step : (b + 1) * step, :],
            preferred_element_type=jnp.float32,
        )
        if b == 0:
            sums[...] = part
        else:
            sums[...] += part
    weight = count / (count + 4.0)
    most = jnp.maximum(count, 1.0)
    for t in range(tpd):
        base = old_ref[:, t * chans : (t + 1) * chans].astype(jnp.float32)
        mean = sums[t * panel : (t + 1) * panel, :] / most
        out_ref[:, t * chans : (t + 1) * chans] = (base + weight * (mean - base)).astype(jnp.bfloat16)


def refine(key, got, old, tpd):
    vmem = pl.BlockSpec(memory_space=pltpu.VMEM)
    panel = old.shape[0]
    return pl.pallas_call(
        functools.partial(refine_kernel, tpd),
        out_shape=jax.ShapeDtypeStruct(old.shape, jnp.bfloat16),
        in_specs=[vmem] * 3,
        out_specs=vmem,
        scratch_shapes=[pltpu.VMEM((tpd * panel, got.shape[1]), jnp.float32)],
        compiler_params=params(),
        cost_estimate=pl.CostEstimate(flops=8 * 10**8, bytes_accessed=3 * 10**6, transcendentals=0),
        name="refine",
    )(key, got, old)


def correlate_kernel(
    chans, tpd, scale, place_ref, same_ref, cross_ref, mine_ref, theirs_ref, out_ref, t_buf, e_buf, t_sem, e_sem, rhs, part, acc
):
    pairs = same_ref.shape[0]
    blocks, panel, lanes = t_buf.shape
    height = mine_ref.shape[0]
    keep = acc.shape[0] // 2
    shift = STRIDE * chans
    core, odd, pair = place_ref[0], place_ref[1], place_ref[2]
    e_copies = [
        pltpu.make_async_copy(ref, e_buf.at[h * height : (h + 1) * height, :], e_sem.at[h])
        for h, ref in enumerate((mine_ref, theirs_ref))
    ]
    t_copies = []
    for i in range(pairs):
        for n, ref, side in ((0, same_ref, core), (1, cross_ref, 1 - core)):
            chunk = 2 * i + side
            if tpd == ROWS:
                target = t_buf.at[chunk]
            else:
                first = pl.multiple_of(chunk * tpd % ROWS * chans, 128)
                target = t_buf.at[chunk * tpd // ROWS, :, pl.ds(first, tpd * chans)]
            t_copies.append(pltpu.make_async_copy(ref.at[i], target, t_sem.at[2 * i + n]))
    for copy in t_copies[:2] + e_copies + t_copies[2:]:
        copy.start()
    for copy in e_copies:
        copy.wait()
    waited = 0
    for a in range(blocks + 1):
        while a < blocks and waited < len(t_copies) and waited // 2 * 2 * tpd < (a + 1) * ROWS:
            t_copies[waited].wait()
            waited += 1
        used = lanes if a < blocks else lanes // 2
        for q in range(FOLD):
            rows = slice(q * panel, (q + 1) * panel)
            cut = q * shift
            if cut > 0:
                low = min(cut, used)
                if a > 0:
                    rhs[rows, 0:low] = t_buf[a - 1, :, lanes - cut : lanes - cut + low]
                else:
                    rhs[rows, 0:low] = jnp.zeros((panel, low), jnp.bfloat16)
            if cut < used:
                if a < blocks:
                    rhs[rows, cut:used] = t_buf[a, :, 0 : used - cut]
                else:
                    rhs[rows, cut:used] = jnp.zeros((panel, used - cut), jnp.bfloat16)
        part[...] = lax.dot_general(
            e_buf[:, 0:used], rhs[:, 0:used], NT, preferred_element_type=jnp.float32
        )
        for h in range(2):
            found = part[h * height + a : h * height + a + keep, :]
            if a == 0:
                acc[h * keep : (h + 1) * keep, :] = found
            else:
                acc[h * keep : (h + 1) * keep, :] += found
    width = 128
    place = lax.broadcasted_iota(jnp.int32, (FOLD * width, FOLD * width), 0)
    lane = lax.broadcasted_iota(jnp.int32, (FOLD * width, FOLD * width), 1)
    weave = (lane == (place % width) * FOLD + place // width).astype(jnp.bfloat16)
    per_half = keep // width
    for h in range(2):
        side = odd if h == 0 else 1 - odd
        for b in range(per_half):
            first = h * keep + b * width
            turned = acc[first : first + width, :].T * scale
            row = jnp.concatenate([turned[q * panel : (q + 1) * panel] for q in range(FOLD)], axis=1)
            high = row.astype(jnp.bfloat16)
            found = jnp.dot(high, weave, preferred_element_type=jnp.float32)
            if out_ref.dtype == jnp.float32:
                rest = (row - high.astype(jnp.float32)).astype(jnp.bfloat16)
                found = found + jnp.dot(rest, weave, preferred_element_type=jnp.float32)
            at = ((2 * pair + side) * per_half + b) * (FOLD * width)
            at = pl.multiple_of(at, FOLD * width)
            out_ref[:, pl.ds(at, FOLD * width)] = found.astype(out_ref.dtype)


def correlate(place, same, cross, mine, theirs, keep, chans, tpd, scale, width, dtype):
    panel = same.shape[1]
    height = mine.shape[0]
    blocks = 2 * same.shape[0] * tpd // ROWS
    anywhere = pl.BlockSpec(memory_space=pl.ANY)
    return pl.pallas_call(
        functools.partial(correlate_kernel, chans, tpd, scale),
        out_shape=jax.ShapeDtypeStruct((panel, width), dtype),
        in_specs=[pl.BlockSpec(memory_space=pltpu.SMEM)] + [anywhere] * 4,
        out_specs=pl.BlockSpec(memory_space=pltpu.VMEM),
        scratch_shapes=[
            pltpu.VMEM((blocks, panel, ROWS * chans), jnp.bfloat16),
            pltpu.VMEM((2 * height, ROWS * chans), jnp.bfloat16),
            pltpu.SemaphoreType.DMA((2 * same.shape[0],)),
            pltpu.SemaphoreType.DMA((2,)),
            pltpu.VMEM((FOLD * panel, ROWS * chans), jnp.bfloat16),
            pltpu.VMEM((2 * height, FOLD * panel), jnp.float32),
            pltpu.VMEM((2 * keep, FOLD * panel), jnp.float32),
        ],
        compiler_params=params(),
        cost_estimate=pl.CostEstimate(flops=8 * 10**9, bytes_accessed=8 * 10**6, transcendentals=0),
        name="correlate",
    )(place, same, cross, mine, theirs)


def gather_panel(value):
    size = lax.axis_size("tm")
    groups = [list(range(c, size, 2)) for c in range(2)]
    same = lax.all_gather(value, "tm", axis=0, tiled=False, axis_index_groups=groups)
    return same, lax.ppermute(same, "tm", [(i, i ^ 1) for i in range(size)])


def body(recording, spike_times, unit_labels, old_templates):
    sub_rows, chans = recording.shape
    panel, feat = old_templates.shape
    taps = feat // chans
    half = (taps - 1) // 2
    owners = lax.axis_size("unit")
    tm_count = lax.axis_size("tm")
    devices = owners * tm_count
    spikes = spike_times.shape[0]
    tm_pos = lax.axis_index("tm")
    unit_pos = lax.axis_index("unit")
    flat_pos = tm_pos * owners + unit_pos
    tpd = -(-taps // tm_count)
    padded = tpd * tm_count
    keep = sub_rows // ROWS
    scale = 1.0 / (float(feat) ** 0.5)

    base = (flat_pos * sub_rows + half).astype(jnp.int32).reshape(1)
    groups = padded // ROWS
    send = pack(spike_times, unit_labels, base, recording, taps, panel, owners, groups, ROWS)
    if tpd != ROWS:
        send = send.reshape(groups, owners, CAP, ROWS // tpd, tpd, chans)
        send = jnp.transpose(send, (0, 3, 1, 2, 4, 5))
    got = lax.all_to_all(
        send.reshape(devices, CAP * tpd, chans), AXES, split_axis=0, concat_axis=0, tiled=True
    ).reshape(devices * CAP * tpd, chans)

    wide = jnp.pad(unit_labels.reshape(1, spikes), ((0, 7), (0, -spikes % 128)))
    labels = lax.all_gather(wide, AXES, axis=0, tiled=False)[:, 0, :spikes]
    mine = labels // panel == unit_pos
    counted = mine.astype(jnp.int32)
    rank = jnp.cumsum(counted, axis=1) - counted
    here = mine[:, :, None] & (rank[:, :, None] == jnp.arange(CAP)[None, None, :])
    within = jnp.sum(jnp.where(here, (labels % panel + 1)[:, :, None], 0), axis=1) - 1
    key = (within[:, :, None] * tpd + jnp.arange(tpd)[None, None, :]).reshape(1, -1)

    cube = old_templates.reshape(panel, chans, taps)
    cube = jnp.pad(cube, ((0, 0), (0, 0), (0, padded - taps)))
    cube = lax.dynamic_slice_in_dim(cube, tm_pos * tpd, tpd, 2)
    old = jnp.transpose(cube, (0, 2, 1)).reshape(panel, tpd * chans)

    folded = fold(lax.optimization_barrier((recording, send))[0])
    halo = padded // ROWS
    following = lax.ppermute(folded[:halo], AXES, [(i, i - 1) for i in range(1, devices)])
    spare = jnp.zeros((16 - halo % 16, ROWS * chans), jnp.bfloat16)
    mine_rows = jnp.concatenate([folded, following, spare], axis=0)
    their_rows = lax.ppermute(mine_rows, "unit", [(i, i ^ 1) for i in range(owners)])
    got, their_rows = lax.optimization_barrier((got, their_rows))

    fresh = refine(key, got, old, tpd)
    core = tm_pos % 2
    own = gather_panel(fresh)
    width = 2 * keep * FOLD

    share = chans // tm_count
    near, far = [
        lax.dynamic_slice_in_dim(
            value.reshape(tm_count // 2, panel, tpd, chans), tm_pos * share, share, 3
        )
        for value in own
    ]
    part = jnp.stack([jnp.where(core == 0, near, far), jnp.where(core == 0, far, near)], axis=1)
    part = part.reshape(tm_count, panel, tpd, share)
    part = jnp.transpose(part, (1, 3, 0, 2)).reshape(panel, share, padded)[:, :, :taps]
    part = part.reshape(panel, share * taps)

    odd = unit_pos % 2
    found = []
    for m in range(1, owners // 2):
        ahead = [(i, (i + 2 * m) % owners) for i in range(owners)]
        back = [(j, i) for i, j in ahead]
        other = gather_panel(lax.ppermute(fresh, "unit", ahead))
        if m == 1:
            part, other = lax.optimization_barrier((part, other))
        place = jnp.stack([core, odd, 0 * core]).astype(jnp.int32)
        out = correlate(
            place, *other, mine_rows, their_rows, keep, chans, tpd, scale, width, jnp.bfloat16
        )
        found.append((lax.ppermute(out, "unit", back), ((unit_pos + 2 * m) % owners) // 2))
    place = jnp.stack([core, odd, unit_pos // 2]).astype(jnp.int32)
    scores = correlate(
        place, *own, mine_rows, their_rows, keep, chans, tpd, scale, owners // 2 * width, jnp.float32
    )
    for out, pair in found:
        scores = lax.dynamic_update_slice_in_dim(
            scores, out.astype(jnp.float32), pair * width, 1
        )
    return (part, scores)


def solution(mesh):
    in_specs = (P(AXES, None), P(AXES), P(AXES), P("unit", None))
    out_specs = (P("unit", "tm"), P("unit", "tm"))
    return jax.shard_map(body, mesh=mesh, in_specs=in_specs, out_specs=out_specs, check_vma=False)
```

```python
import functools

import jax
import jax.numpy as jnp
from jax import lax
from jax.experimental import pallas as pl
from jax.experimental.pallas import tpu as pltpu
from jax.sharding import PartitionSpec as P

STRIDE = 2
CAP = 8
FOLD = 4
ROWS = STRIDE * FOLD
AXES = ("tm", "unit")
VMEM_LIMIT = 56 * 1024 * 1024
NT = (((1,), (1,)), ((), ()))


def params():
    return pltpu.CompilerParams(vmem_limit_bytes=VMEM_LIMIT)


def pack_kernel(
    taps, panel, owners, tm_count, tpd, times_ref, labels_ref, base_ref, rec_ref, send_ref, buf, cnt
):
    spikes = times_ref.shape[0]
    sub_rows = rec_ref.shape[0]
    padded = tm_count * tpd
    win = padded + 16
    base = base_ref[0]
    for o in range(owners):
        cnt[o] = 0
    if owners * CAP > spikes:
        buf[...] = jnp.zeros_like(buf)
    tap = lax.broadcasted_iota(jnp.int32, (padded, win), 0)
    col = lax.broadcasted_iota(jnp.int32, (padded, win), 1)
    gap = jnp.where(tap < taps, col - tap, -1)

    def one(s):
        first = times_ref[s] - base
        start = jnp.minimum((first // 16) * 16, sub_rows - win)
        owner = labels_ref[s] // panel
        slot = cnt[owner]
        cnt[owner] = slot + 1
        pick = (gap == first - start).astype(jnp.bfloat16)
        window = rec_ref[pl.ds(pl.multiple_of(start, 16), win), :]
        snip = jnp.dot(pick, window, preferred_element_type=jnp.float32)
        for t in range(tm_count):
            row = (t * owners + owner) * (CAP * tpd) + slot * tpd
            buf[pl.ds(pl.multiple_of(row, tpd), tpd), :] = snip[t * tpd : (t + 1) * tpd]

    def group(g, carry):
        for i in range(8):
            one(g * 8 + i)
        return carry

    lax.fori_loop(0, spikes // 8, group, 0)
    send_ref[...] = buf[...].astype(jnp.bfloat16)


def pack(times, labels, base, rec, taps, panel, owners, tm_count, tpd):
    chans = rec.shape[1]
    rows = owners * tm_count * CAP * tpd
    smem = pl.BlockSpec(memory_space=pltpu.SMEM)
    vmem = pl.BlockSpec(memory_space=pltpu.VMEM)
    return pl.pallas_call(
        functools.partial(pack_kernel, taps, panel, owners, tm_count, tpd),
        out_shape=jax.ShapeDtypeStruct((rows, chans), jnp.bfloat16),
        in_specs=[smem, smem, smem, vmem],
        out_specs=vmem,
        scratch_shapes=[
            pltpu.VMEM((rows, chans), jnp.float32),
            pltpu.SMEM((owners,), jnp.int32),
        ],
        compiler_params=params(),
        cost_estimate=pl.CostEstimate(flops=10**8, bytes_accessed=4 * 10**6, transcendentals=0),
        name="pack",
    )(times, labels, base, rec)


def fold_kernel(rec_ref, out_ref):
    rows, chans = rec_ref.shape
    block = 16 * ROWS
    new = lax.broadcasted_iota(jnp.int32, (block, block), 0)
    old = lax.broadcasted_iota(jnp.int32, (block, block), 1)
    perm = (old == (new % 16) * ROWS + new // 16).astype(jnp.bfloat16)
    for b in range(rows // block):
        part = jnp.dot(perm, rec_ref[b * block : (b + 1) * block, :], preferred_element_type=jnp.float32)
        part = part.astype(jnp.bfloat16)
        for r in range(ROWS):
            out_ref[b * 16 : (b + 1) * 16, r * chans : (r + 1) * chans] = part[r * 16 : (r + 1) * 16]


def fold(rec):
    rows, chans = rec.shape
    vmem = pl.BlockSpec(memory_space=pltpu.VMEM)
    return pl.pallas_call(
        fold_kernel,
        out_shape=jax.ShapeDtypeStruct((rows // ROWS, ROWS * chans), jnp.bfloat16),
        in_specs=[vmem],
        out_specs=vmem,
        compiler_params=params(),
        cost_estimate=pl.CostEstimate(flops=2 * 10**8, bytes_accessed=4 * 10**6, transcendentals=0),
        name="fold",
    )(rec)


def refine_kernel(tpd, key_ref, got_ref, old_ref, out_ref, sums):
    panel = old_ref.shape[0]
    rows, chans = got_ref.shape
    step = min(rows, 2048)
    count = jnp.zeros((panel, 1), jnp.float32)
    for b in range(rows // step):
        key = key_ref[:, b * step : (b + 1) * step]
        wanted = lax.broadcasted_iota(jnp.int32, (tpd * panel, step), 0)
        wanted = (wanted % panel) * tpd + wanted // panel
        hit = (wanted == key).astype(jnp.float32)
        count = count + jnp.sum(hit[:panel], axis=1, keepdims=True)
        part = jnp.dot(
            hit.astype(jnp.bfloat16),
            got_ref[b * step : (b + 1) * step, :],
            preferred_element_type=jnp.float32,
        )
        if b == 0:
            sums[...] = part
        else:
            sums[...] += part
    weight = count / (count + 4.0)
    most = jnp.maximum(count, 1.0)
    for t in range(tpd):
        base = old_ref[:, t * chans : (t + 1) * chans].astype(jnp.float32)
        mean = sums[t * panel : (t + 1) * panel, :] / most
        out_ref[:, t * chans : (t + 1) * chans] = (base + weight * (mean - base)).astype(jnp.bfloat16)


def refine(key, got, old, tpd):
    vmem = pl.BlockSpec(memory_space=pltpu.VMEM)
    panel = old.shape[0]
    return pl.pallas_call(
        functools.partial(refine_kernel, tpd),
        out_shape=jax.ShapeDtypeStruct(old.shape, jnp.bfloat16),
        in_specs=[vmem] * 3,
        out_specs=vmem,
        scratch_shapes=[pltpu.VMEM((tpd * panel, got.shape[1]), jnp.float32)],
        compiler_params=params(),
        cost_estimate=pl.CostEstimate(flops=8 * 10**8, bytes_accessed=3 * 10**6, transcendentals=0),
        name="refine",
    )(key, got, old)


def correlate_kernel(chans, tpd, scale, masks, place_ref, *refs):
    count = len(masks)
    pieces, rest = refs[:count], refs[count:]
    mine_ref, my_halo, theirs_ref, their_halo, out_ref, rhs, e_buf, t_sem, e_sem, part, acc = rest
    half_rows = pieces[0].shape[1]
    panel = 2 * half_rows
    lanes = tpd * chans
    chunks = t_sem.shape[0]
    whole = chunks * lanes
    height = e_buf.shape[0] // 2
    keep = acc.shape[0] // 2
    shift = STRIDE * chans
    me, odd, pair = place_ref[0], place_ref[1], place_ref[2]

    def spot(chunk, part_of, q):
        first = chunk * lanes + q * shift
        if not isinstance(chunk, int):
            first = pl.multiple_of(first, 128)
        return rhs.at[pl.ds(q * panel + part_of * half_rows, half_rows), pl.ds(first, lanes)]

    e_copies = []
    for n, (body_ref, halo_ref) in enumerate(((mine_ref, my_halo), (theirs_ref, their_halo))):
        low = n * height
        e_copies.append(
            pltpu.make_async_copy(body_ref, e_buf.at[low : low + keep, :], e_sem.at[2 * n])
        )
        e_copies.append(
            pltpu.make_async_copy(halo_ref, e_buf.at[low + keep : low + height, :], e_sem.at[2 * n + 1])
        )
    for copy in e_copies:
        copy.start()
    for ref, (part_of, items) in zip(pieces, masks):
        for at, mask in enumerate(items):
            chunk = jnp.bitwise_xor(me, mask)
            for q in range(FOLD):
                sem = t_sem.at[chunk, part_of * FOLD + q]
                pltpu.make_async_copy(ref.at[at], spot(chunk, part_of, q), sem).start()
    for q in range(FOLD):
        rows = slice(q * panel, (q + 1) * panel)
        if q > 0:
            rhs[rows, 0 : q * shift] = jnp.zeros((panel, q * shift), jnp.bfloat16)
        tail = rhs.shape[1] - whole - q * shift
        if tail > 0:
            rhs[rows, whole + q * shift :] = jnp.zeros((panel, tail), jnp.bfloat16)
    for copy in e_copies:
        copy.wait()
    depth = ROWS * chans
    per = depth // lanes
    for a in range(chunks // per + 1):
        for chunk in range(a * per, min((a + 1) * per, chunks)):
            for part_of in range(2):
                for q in range(FOLD):
                    sem = t_sem.at[chunk, part_of * FOLD + q]
                    pltpu.make_async_copy(pieces[0].at[0], spot(chunk, part_of, q), sem).wait()
        used = min(depth, rhs.shape[1] - a * depth)
        part[...] = lax.dot_general(
            e_buf[:, 0:used],
            rhs[:, a * depth : a * depth + used],
            NT,
            preferred_element_type=jnp.float32,
        )
        for h in range(2):
            found = part[h * height + a : h * height + a + keep, :]
            if a == 0:
                acc[h * keep : (h + 1) * keep, :] = found
            else:
                acc[h * keep : (h + 1) * keep, :] += found
    width = 128
    place = lax.broadcasted_iota(jnp.int32, (FOLD * width, FOLD * width), 0)
    lane = lax.broadcasted_iota(jnp.int32, (FOLD * width, FOLD * width), 1)
    weave = (lane == (place % width) * FOLD + place // width).astype(jnp.bfloat16)
    per_half = keep // width
    for h in range(2):
        side = odd if h == 0 else 1 - odd
        for b in range(per_half):
            first = h * keep + b * width
            turned = acc[first : first + width, :].T * scale
            row = jnp.concatenate([turned[q * panel : (q + 1) * panel] for q in range(FOLD)], axis=1)
            high = row.astype(jnp.bfloat16)
            found = jnp.dot(high, weave, preferred_element_type=jnp.float32)
            if out_ref.dtype == jnp.float32:
                rest = (row - high.astype(jnp.float32)).astype(jnp.bfloat16)
                found = found + jnp.dot(rest, weave, preferred_element_type=jnp.float32)
            at = ((2 * pair + side) * per_half + b) * (FOLD * width)
            at = pl.multiple_of(at, FOLD * width)
            out_ref[:, pl.ds(at, FOLD * width)] = found.astype(out_ref.dtype)


def correlate(place, gathered, windows, chans, tpd, scale, width, dtype):
    pieces = [value for value, _, _ in gathered]
    masks = [(part_of, items) for _, part_of, items in gathered]
    panel = 2 * pieces[0].shape[1]
    chunks = sum(len(items) for _, items in masks) // 2
    keep = windows[0].shape[0]
    height = keep + windows[1].shape[0]
    depth = ROWS * chans
    anywhere = pl.BlockSpec(memory_space=pl.ANY)
    return pl.pallas_call(
        functools.partial(correlate_kernel, chans, tpd, scale, masks),
        out_shape=jax.ShapeDtypeStruct((panel, width), dtype),
        in_specs=[pl.BlockSpec(memory_space=pltpu.SMEM)] + [anywhere] * (len(pieces) + 4),
        out_specs=pl.BlockSpec(memory_space=pltpu.VMEM),
        scratch_shapes=[
            pltpu.VMEM((FOLD * panel, chunks * tpd * chans + (FOLD - 1) * STRIDE * chans), jnp.bfloat16),
            pltpu.VMEM((2 * height, depth), jnp.bfloat16),
            pltpu.SemaphoreType.DMA((chunks, 2 * FOLD)),
            pltpu.SemaphoreType.DMA((4,)),
            pltpu.VMEM((2 * height, FOLD * panel), jnp.float32),
            pltpu.VMEM((2 * keep, FOLD * panel), jnp.float32),
        ],
        compiler_params=params(),
        cost_estimate=pl.CostEstimate(flops=8 * 10**9, bytes_accessed=16 * 10**6, transcendentals=0),
        name="correlate",
    )(place, *pieces, *windows)


def swap(value, bit):
    size = lax.axis_size("tm")
    return lax.ppermute(value, "tm", [(i, i ^ bit) for i in range(size)])


def gather_panel(value):
    bits = []
    while 2 << len(bits) < lax.axis_size("tm"):
        bits.append(2 << len(bits))
    rows = value.shape[0] // 2
    out = []
    for part_of, order in enumerate((bits[::-1], bits)):
        parts = [(value[part_of * rows : (part_of + 1) * rows][None], [0])]
        for bit in order:
            held = jnp.concatenate([v for v, _ in parts], axis=0) if len(parts) > 1 else parts[0][0]
            items = [m for _, ms in parts for m in ms]
            parts = [(held, items), (swap(held, bit), [m ^ bit for m in items])]
        out += [(v, part_of, ms) for v, ms in parts]
    return out + [(swap(v, 1), part_of, [m ^ 1 for m in ms]) for v, part_of, ms in out]


def body(recording, spike_times, unit_labels, old_templates):
    sub_rows, chans = recording.shape
    panel, feat = old_templates.shape
    taps = feat // chans
    half = (taps - 1) // 2
    owners = lax.axis_size("unit")
    tm_count = lax.axis_size("tm")
    devices = owners * tm_count
    spikes = spike_times.shape[0]
    tm_pos = lax.axis_index("tm")
    unit_pos = lax.axis_index("unit")
    flat_pos = tm_pos * owners + unit_pos
    tpd = -(-taps // tm_count)
    padded = tpd * tm_count
    keep = sub_rows // ROWS
    scale = 1.0 / (float(feat) ** 0.5)

    base = (flat_pos * sub_rows + half).astype(jnp.int32).reshape(1)
    groups = padded // ROWS
    send = pack(spike_times, unit_labels, base, recording, taps, panel, owners, groups, ROWS)
    if tpd != ROWS:
        send = send.reshape(groups, owners, CAP, ROWS // tpd, tpd, chans)
        send = jnp.transpose(send, (0, 3, 1, 2, 4, 5))
    owner = unit_labels // panel
    hits = (owner[:, None] == jnp.arange(owners)[None, :]).astype(jnp.int32)
    rank = jnp.sum((jnp.cumsum(hits, axis=0) - hits) * hits, axis=1)
    placing = jnp.arange(owners * CAP)[:, None] == (owner * CAP + rank)[None, :]
    tags = jnp.sum(jnp.where(placing, (unit_labels % panel + 1)[None, :], 0), axis=1) - 1
    tags = jnp.broadcast_to(tags.reshape(1, owners, CAP), (tm_count, owners, CAP))
    tags = tags.reshape(devices, CAP)
    tags = lax.all_to_all(tags, AXES, split_axis=0, concat_axis=0, tiled=True)
    key = (tags[:, :, None] * tpd + jnp.arange(tpd)[None, None, :]).reshape(1, -1)
    send, key = lax.optimization_barrier((send, key))
    got = lax.all_to_all(
        send.reshape(devices, CAP * tpd, chans), AXES, split_axis=0, concat_axis=0, tiled=True
    ).reshape(devices * CAP * tpd, chans)

    cube = old_templates.reshape(panel, chans, taps)
    cube = jnp.pad(cube, ((0, 0), (0, 0), (0, padded - taps)))
    cube = lax.dynamic_slice_in_dim(cube, tm_pos * tpd, tpd, 2)
    old = jnp.transpose(cube, (0, 2, 1)).reshape(panel, tpd * chans)

    folded = fold(lax.optimization_barrier((recording, send))[0])
    folded, got = lax.optimization_barrier((folded, got))
    halo = padded // ROWS
    head = folded[:halo]
    follow = lax.ppermute(head, AXES, [(i, i - 1) for i in range(1, devices)])
    skip = lax.ppermute(head, AXES, [(i, i - 2) for i in range(2, devices, 2)])
    theirs = lax.ppermute(folded, "unit", [(i, i ^ 1) for i in range(owners)])
    odd = unit_pos % 2
    spare = ((0, -halo % 16), (0, 0))
    windows = (
        folded,
        jnp.pad(follow, spare),
        theirs,
        jnp.pad(jnp.where(odd == 1, head, skip), spare),
    )

    fresh = refine(key, got, old, tpd)
    own = gather_panel(fresh)
    width = 2 * keep * FOLD

    share = chans // tm_count
    order = []
    pieces = [[], []]
    for value, part_of, items in own:
        value = value.reshape(len(items), panel // 2, tpd, chans)
        pieces[part_of].append(lax.dynamic_slice_in_dim(value, tm_pos * share, share, 3))
        order += items if part_of == 0 else []
    order_b = [m for _, part_of, items in own if part_of == 1 for m in items]
    part = []
    for found, masks in ((pieces[0], order), (pieces[1], order_b)):
        spots = jnp.array([masks.index(m) for m in range(tm_count)])
        stacked = jnp.concatenate(found, axis=0)
        picks = spots[jnp.bitwise_xor(jnp.arange(tm_count), tm_pos)]
        part.append(jnp.take(stacked, picks, axis=0))
    part = jnp.concatenate(part, axis=1)
    part = jnp.transpose(part, (1, 3, 0, 2)).reshape(panel, share, padded)[:, :, :taps]
    part = part.reshape(panel, share * taps)

    found = []
    for m in range(1, owners // 2):
        ahead = [(i, (i + 2 * m) % owners) for i in range(owners)]
        back = [(j, i) for i, j in ahead]
        other = gather_panel(lax.ppermute(fresh, "unit", ahead))
        place = jnp.stack([tm_pos, odd, 0 * odd]).astype(jnp.int32)
        out = correlate(place, other, windows, chans, tpd, scale, width, jnp.bfloat16)
        found.append((lax.ppermute(out, "unit", back), ((unit_pos + 2 * m) % owners) // 2))
    place = jnp.stack([tm_pos, odd, unit_pos // 2]).astype(jnp.int32)
    scores = correlate(place, own, windows, chans, tpd, scale, owners // 2 * width, jnp.float32)
    for out, pair in found:
        scores = lax.dynamic_update_slice_in_dim(
            scores, out.astype(jnp.float32), pair * width, 1
        )
    return (part, scores)


def solution(mesh):
    in_specs = (P(AXES, None), P(AXES), P(AXES), P("unit", None))
    out_specs = (P("unit", "tm"), P("unit", "tm"))
    return jax.shard_map(body, mesh=mesh, in_specs=in_specs, out_specs=out_specs, check_vma=False)
```

```python
import functools

import jax
import jax.numpy as jnp
from jax import lax
from jax.experimental import pallas as pl
from jax.experimental.pallas import tpu as pltpu
from jax.sharding import PartitionSpec as P

STRIDE = 2
CAP = 8
FOLD = 4
ROWS = STRIDE * FOLD
AXES = ("tm", "unit")
VMEM_LIMIT = 56 * 1024 * 1024
NT = (((1,), (1,)), ((), ()))


def params():
    return pltpu.CompilerParams(vmem_limit_bytes=VMEM_LIMIT)


def pack_kernel(
    taps, panel, owners, tm_count, tpd, times_ref, labels_ref, base_ref, rec_ref, send_ref, buf, cnt
):
    spikes = times_ref.shape[0]
    sub_rows = rec_ref.shape[0]
    padded = tm_count * tpd
    win = padded + 16
    base = base_ref[0]
    for o in range(owners):
        cnt[o] = 0
    if owners * CAP > spikes:
        buf[...] = jnp.zeros_like(buf)
    tap = lax.broadcasted_iota(jnp.int32, (padded, win), 0)
    col = lax.broadcasted_iota(jnp.int32, (padded, win), 1)
    gap = jnp.where(tap < taps, col - tap, -1)

    def one(s):
        first = times_ref[s] - base
        start = jnp.minimum((first // 16) * 16, sub_rows - win)
        owner = labels_ref[s] // panel
        slot = cnt[owner]
        cnt[owner] = slot + 1
        pick = (gap == first - start).astype(jnp.bfloat16)
        window = rec_ref[pl.ds(pl.multiple_of(start, 16), win), :]
        snip = jnp.dot(pick, window, preferred_element_type=jnp.float32)
        for t in range(tm_count):
            row = (t * owners + owner) * (CAP * tpd) + slot * tpd
            buf[pl.ds(pl.multiple_of(row, tpd), tpd), :] = snip[t * tpd : (t + 1) * tpd]

    def group(g, carry):
        for i in range(8):
            one(g * 8 + i)
        return carry

    lax.fori_loop(0, spikes // 8, group, 0)
    send_ref[...] = buf[...].astype(jnp.bfloat16)


def pack(times, labels, base, rec, taps, panel, owners, tm_count, tpd):
    chans = rec.shape[1]
    rows = owners * tm_count * CAP * tpd
    smem = pl.BlockSpec(memory_space=pltpu.SMEM)
    vmem = pl.BlockSpec(memory_space=pltpu.VMEM)
    return pl.pallas_call(
        functools.partial(pack_kernel, taps, panel, owners, tm_count, tpd),
        out_shape=jax.ShapeDtypeStruct((rows, chans), jnp.bfloat16),
        in_specs=[smem, smem, smem, vmem],
        out_specs=vmem,
        scratch_shapes=[
            pltpu.VMEM((rows, chans), jnp.float32),
            pltpu.SMEM((owners,), jnp.int32),
        ],
        compiler_params=params(),
        cost_estimate=pl.CostEstimate(flops=10**8, bytes_accessed=4 * 10**6, transcendentals=0),
        name="pack",
    )(times, labels, base, rec)


def fold_kernel(rec_ref, halo_ref, out_ref):
    rows, chans = rec_ref.shape
    extra = halo_ref.shape[0]
    block = 16 * ROWS
    new = lax.broadcasted_iota(jnp.int32, (block, block), 0)
    old = lax.broadcasted_iota(jnp.int32, (block, block), 1)
    perm = (old == (new % 16) * ROWS + new // 16).astype(jnp.bfloat16)
    for b in range(rows // block + 1):
        if b < rows // block:
            part = jnp.dot(perm, rec_ref[b * block : (b + 1) * block, :], preferred_element_type=jnp.float32)
        else:
            part = jnp.dot(perm[:, :extra], halo_ref[...], preferred_element_type=jnp.float32)
        part = part.astype(jnp.bfloat16)
        for r in range(ROWS):
            out_ref[b * 16 : (b + 1) * 16, r * chans : (r + 1) * chans] = part[r * 16 : (r + 1) * 16]


def fold(rec, halo):
    rows, chans = rec.shape
    vmem = pl.BlockSpec(memory_space=pltpu.VMEM)
    return pl.pallas_call(
        fold_kernel,
        out_shape=jax.ShapeDtypeStruct((rows // ROWS + 16, ROWS * chans), jnp.bfloat16),
        in_specs=[vmem, vmem],
        out_specs=vmem,
        compiler_params=params(),
        cost_estimate=pl.CostEstimate(flops=2 * 10**8, bytes_accessed=4 * 10**6, transcendentals=0),
        name="fold",
    )(rec, halo)


def refine_kernel(tpd, key_ref, got_ref, old_ref, out_ref, sums):
    panel = old_ref.shape[0]
    rows, chans = got_ref.shape
    step = min(rows, 2048)
    count = jnp.zeros((panel, 1), jnp.float32)
    for b in range(rows // step):
        key = key_ref[:, b * step : (b + 1) * step]
        wanted = lax.broadcasted_iota(jnp.int32, (tpd * panel, step), 0)
        wanted = (wanted % panel) * tpd + wanted // panel
        hit = (wanted == key).astype(jnp.float32)
        count = count + jnp.sum(hit[:panel], axis=1, keepdims=True)
        part = jnp.dot(
            hit.astype(jnp.bfloat16),
            got_ref[b * step : (b + 1) * step, :],
            preferred_element_type=jnp.float32,
        )
        if b == 0:
            sums[...] = part
        else:
            sums[...] += part
    weight = count / (count + 4.0)
    most = jnp.maximum(count, 1.0)
    for t in range(tpd):
        base = old_ref[:, t * chans : (t + 1) * chans].astype(jnp.float32)
        mean = sums[t * panel : (t + 1) * panel, :] / most
        out_ref[:, t * chans : (t + 1) * chans] = (base + weight * (mean - base)).astype(jnp.bfloat16)


def refine(key, got, old, tpd):
    vmem = pl.BlockSpec(memory_space=pltpu.VMEM)
    panel = old.shape[0]
    return pl.pallas_call(
        functools.partial(refine_kernel, tpd),
        out_shape=jax.ShapeDtypeStruct(old.shape, jnp.bfloat16),
        in_specs=[vmem] * 3,
        out_specs=vmem,
        scratch_shapes=[pltpu.VMEM((tpd * panel, got.shape[1]), jnp.float32)],
        compiler_params=params(),
        cost_estimate=pl.CostEstimate(flops=8 * 10**8, bytes_accessed=3 * 10**6, transcendentals=0),
        name="refine",
    )(key, got, old)


def correlate_kernel(chans, tpd, scale, masks, place_ref, *refs):
    count = len(masks)
    pieces, rest = refs[:count], refs[count:]
    mine_ref, theirs_ref, out_ref, t_buf, e_buf, t_sem, e_sem, rhs, part, acc = rest
    half_rows = pieces[0].shape[1]
    lanes = tpd * chans
    chunks = t_sem.shape[0]
    blocks, panel, depth = t_buf.shape
    per = depth // lanes
    height = e_buf.shape[0] // 2
    keep = acc.shape[0] // 2
    shift = STRIDE * chans
    me, odd, pair = place_ref[0], place_ref[1], place_ref[2]

    def spot(chunk, part_of):
        rows = pl.ds(part_of * half_rows, half_rows)
        if per == 1:
            return t_buf.at[chunk, rows]
        first = chunk % per * lanes
        if not isinstance(chunk, int):
            first = pl.multiple_of(first, 128)
        return t_buf.at[chunk // per, rows, pl.ds(first, lanes)]

    e_copies = [
        pltpu.make_async_copy(ref, e_buf.at[n * height : (n + 1) * height, :], e_sem.at[n])
        for n, ref in enumerate((mine_ref, theirs_ref))
    ]
    for copy in e_copies:
        copy.start()
    for ref, (part_of, items) in zip(pieces, masks):
        for at, mask in enumerate(items):
            chunk = jnp.bitwise_xor(me, mask)
            pltpu.make_async_copy(ref.at[at], spot(chunk, part_of), t_sem.at[chunk, part_of]).start()
    for copy in e_copies:
        copy.wait()
    for a in range(blocks + 1):
        if a < blocks:
            for chunk in range(a * per, (a + 1) * per):
                for part_of in range(2):
                    sem = t_sem.at[chunk, part_of]
                    pltpu.make_async_copy(pieces[0].at[0], spot(chunk, part_of), sem).wait()
        used = depth if a < blocks else depth // 2
        turn = a % 2
        for q in range(FOLD):
            rows = slice(q * panel, (q + 1) * panel)
            cut = q * shift
            low = min(cut, used)
            if low > 0:
                if a > 0:
                    rhs[turn, rows, 0:low] = t_buf[a - 1, :, depth - cut : depth - cut + low]
                else:
                    rhs[turn, rows, 0:low] = jnp.zeros((panel, low), jnp.bfloat16)
            if cut < used:
                if a < blocks:
                    rhs[turn, rows, cut:used] = t_buf[a, :, 0 : used - cut]
                else:
                    rhs[turn, rows, cut:used] = jnp.zeros((panel, used - cut), jnp.bfloat16)
        part[turn] = lax.dot_general(
            e_buf[:, 0:used], rhs[turn, :, 0:used], NT, preferred_element_type=jnp.float32
        )
        for h in range(2):
            found = part[turn, h * height + a : h * height + a + keep, :]
            if a == 0:
                acc[h * keep : (h + 1) * keep, :] = found
            else:
                acc[h * keep : (h + 1) * keep, :] += found
    width = 128
    place = lax.broadcasted_iota(jnp.int32, (FOLD * width, FOLD * width), 0)
    lane = lax.broadcasted_iota(jnp.int32, (FOLD * width, FOLD * width), 1)
    weave = (lane == (place % width) * FOLD + place // width).astype(jnp.bfloat16)
    per_half = keep // width
    for h in range(2):
        side = odd if h == 0 else 1 - odd
        for b in range(per_half):
            first = h * keep + b * width
            turned = acc[first : first + width, :].T * scale
            row = jnp.concatenate([turned[q * panel : (q + 1) * panel] for q in range(FOLD)], axis=1)
            high = row.astype(jnp.bfloat16)
            found = jnp.dot(high, weave, preferred_element_type=jnp.float32)
            if out_ref.dtype == jnp.float32:
                rest = (row - high.astype(jnp.float32)).astype(jnp.bfloat16)
                found = found + jnp.dot(rest, weave, preferred_element_type=jnp.float32)
            at = ((2 * pair + side) * per_half + b) * (FOLD * width)
            at = pl.multiple_of(at, FOLD * width)
            out_ref[:, pl.ds(at, FOLD * width)] = found.astype(out_ref.dtype)


def correlate(place, gathered, windows, chans, tpd, scale, width, dtype):
    pieces = [value for value, _, _ in gathered]
    masks = [(part_of, items) for _, part_of, items in gathered]
    panel = 2 * pieces[0].shape[1]
    chunks = sum(len(items) for _, items in masks) // 2
    height = windows[0].shape[0]
    keep = height - 16
    depth = ROWS * chans
    anywhere = pl.BlockSpec(memory_space=pl.ANY)
    return pl.pallas_call(
        functools.partial(correlate_kernel, chans, tpd, scale, masks),
        out_shape=jax.ShapeDtypeStruct((panel, width), dtype),
        in_specs=[pl.BlockSpec(memory_space=pltpu.SMEM)] + [anywhere] * (len(pieces) + 2),
        out_specs=pl.BlockSpec(memory_space=pltpu.VMEM),
        scratch_shapes=[
            pltpu.VMEM((chunks * tpd // ROWS, panel, depth), jnp.bfloat16),
            pltpu.VMEM((2 * height, depth), jnp.bfloat16),
            pltpu.SemaphoreType.DMA((chunks, 2)),
            pltpu.SemaphoreType.DMA((2,)),
            pltpu.VMEM((2, FOLD * panel, depth), jnp.bfloat16),
            pltpu.VMEM((2, 2 * height, FOLD * panel), jnp.float32),
            pltpu.VMEM((2 * keep, FOLD * panel), jnp.float32),
        ],
        compiler_params=params(),
        cost_estimate=pl.CostEstimate(flops=8 * 10**9, bytes_accessed=8 * 10**6, transcendentals=0),
        name="correlate",
    )(place, *pieces, *windows)


def swap(value, bit):
    size = lax.axis_size("tm")
    return lax.ppermute(value, "tm", [(i, i ^ bit) for i in range(size)])


def gather_panel(value):
    bits = []
    while 2 << len(bits) < lax.axis_size("tm"):
        bits.append(2 << len(bits))
    rows = value.shape[0] // 2
    out = []
    for part_of, order in enumerate((bits[::-1], bits)):
        parts = [(value[part_of * rows : (part_of + 1) * rows][None], [0])]
        for bit in order:
            held = jnp.concatenate([v for v, _ in parts], axis=0) if len(parts) > 1 else parts[0][0]
            items = [m for _, ms in parts for m in ms]
            parts = [(held, items), (swap(held, bit), [m ^ bit for m in items])]
        out += [(v, part_of, ms) for v, ms in parts]
    return out + [(swap(v, 1), part_of, [m ^ 1 for m in ms]) for v, part_of, ms in out]


def body(recording, spike_times, unit_labels, old_templates):
    sub_rows, chans = recording.shape
    panel, feat = old_templates.shape
    taps = feat // chans
    half = (taps - 1) // 2
    owners = lax.axis_size("unit")
    tm_count = lax.axis_size("tm")
    devices = owners * tm_count
    spikes = spike_times.shape[0]
    tm_pos = lax.axis_index("tm")
    unit_pos = lax.axis_index("unit")
    flat_pos = tm_pos * owners + unit_pos
    tpd = -(-taps // tm_count)
    padded = tpd * tm_count
    keep = sub_rows // ROWS
    scale = 1.0 / (float(feat) ** 0.5)

    base = (flat_pos * sub_rows + half).astype(jnp.int32).reshape(1)
    groups = padded // ROWS
    send = pack(spike_times, unit_labels, base, recording, taps, panel, owners, groups, ROWS)
    if tpd != ROWS:
        send = send.reshape(groups, owners, CAP, ROWS // tpd, tpd, chans)
        send = jnp.transpose(send, (0, 3, 1, 2, 4, 5))
    owner = unit_labels // panel
    hits = (owner[:, None] == jnp.arange(owners)[None, :]).astype(jnp.int32)
    rank = jnp.sum((jnp.cumsum(hits, axis=0) - hits) * hits, axis=1)
    placing = jnp.arange(owners * CAP)[:, None] == (owner * CAP + rank)[None, :]
    tags = jnp.sum(jnp.where(placing, (unit_labels % panel + 1)[None, :], 0), axis=1) - 1
    tags = jnp.broadcast_to(tags.reshape(1, owners, CAP), (tm_count, owners, CAP))
    tags = tags.reshape(devices, CAP)
    tags = lax.all_to_all(tags, AXES, split_axis=0, concat_axis=0, tiled=True)
    key = (tags[:, :, None] * tpd + jnp.arange(tpd)[None, None, :]).reshape(1, -1)
    send, key = lax.optimization_barrier((send, key))
    got = lax.all_to_all(
        send.reshape(devices, CAP * tpd, chans), AXES, split_axis=0, concat_axis=0, tiled=True
    ).reshape(devices * CAP * tpd, chans)

    cube = old_templates.reshape(panel, chans, taps)
    cube = jnp.pad(cube, ((0, 0), (0, 0), (0, padded - taps)))
    cube = lax.dynamic_slice_in_dim(cube, tm_pos * tpd, tpd, 2)
    old = jnp.transpose(cube, (0, 2, 1)).reshape(panel, tpd * chans)

    head = recording[:padded]
    follow = lax.ppermute(head, AXES, [(i, i - 1) for i in range(1, devices)])
    skip = lax.ppermute(head, AXES, [(i, i - 2) for i in range(2, devices, 2)])
    theirs = lax.ppermute(recording, "unit", [(i, i ^ 1) for i in range(owners)])
    got, theirs, follow, skip = lax.optimization_barrier((got, theirs, follow, skip))
    odd = unit_pos % 2

    fresh = refine(key, got, old, tpd)
    late, theirs, fresh = lax.optimization_barrier((recording, theirs, fresh))
    windows = (fold(late, follow), fold(theirs, jnp.where(odd == 1, head, skip)))
    own = gather_panel(fresh)
    width = 2 * keep * FOLD

    share = chans // tm_count
    order = []
    pieces = [[], []]
    for value, part_of, items in own:
        value = value.reshape(len(items), panel // 2, tpd, chans)
        pieces[part_of].append(lax.dynamic_slice_in_dim(value, tm_pos * share, share, 3))
        order += items if part_of == 0 else []
    order_b = [m for _, part_of, items in own if part_of == 1 for m in items]
    part = []
    for found, masks in ((pieces[0], order), (pieces[1], order_b)):
        spots = jnp.array([masks.index(m) for m in range(tm_count)])
        stacked = jnp.concatenate(found, axis=0)
        picks = spots[jnp.bitwise_xor(jnp.arange(tm_count), tm_pos)]
        part.append(jnp.take(stacked, picks, axis=0))
    part = jnp.concatenate(part, axis=1)
    part = jnp.transpose(part, (1, 3, 0, 2)).reshape(panel, share, padded)[:, :, :taps]
    part = part.reshape(panel, share * taps)

    found = []
    for m in range(1, owners // 2):
        ahead = [(i, (i + 2 * m) % owners) for i in range(owners)]
        back = [(j, i) for i, j in ahead]
        other = gather_panel(lax.ppermute(fresh, "unit", ahead))
        place = jnp.stack([tm_pos, odd, 0 * odd]).astype(jnp.int32)
        out = correlate(place, other, windows, chans, tpd, scale, width, jnp.bfloat16)
        found.append((lax.ppermute(out, "unit", back), ((unit_pos + 2 * m) % owners) // 2))
    place = jnp.stack([tm_pos, odd, unit_pos // 2]).astype(jnp.int32)
    scores = correlate(place, own, windows, chans, tpd, scale, owners // 2 * width, jnp.float32)
    for out, pair in found:
        scores = lax.dynamic_update_slice_in_dim(
            scores, out.astype(jnp.float32), pair * width, 1
        )
    return (part, scores)


def solution(mesh):
    in_specs = (P(AXES, None), P(AXES), P(AXES), P("unit", None))
    out_specs = (P("unit", "tm"), P("unit", "tm"))
    return jax.shard_map(body, mesh=mesh, in_specs=in_specs, out_specs=out_specs, check_vma=False)
```

```python
import functools

import jax
import jax.numpy as jnp
from jax import lax
from jax.experimental import pallas as pl
from jax.experimental.pallas import tpu as pltpu
from jax.sharding import PartitionSpec as P

STRIDE = 2
CAP = 8
FOLD = 4
ROWS = STRIDE * FOLD
AXES = ("tm", "unit")
VMEM_LIMIT = 56 * 1024 * 1024
NT = (((1,), (1,)), ((), ()))


def params():
    return pltpu.CompilerParams(vmem_limit_bytes=VMEM_LIMIT)


def pack_kernel(
    taps, panel, owners, tm_count, tpd, times_ref, labels_ref, base_ref, rec_ref, send_ref, buf, cnt
):
    spikes = times_ref.shape[0]
    sub_rows = rec_ref.shape[0]
    padded = tm_count * tpd
    win = padded + 16
    base = base_ref[0]
    for o in range(owners):
        cnt[o] = 0
    if owners * CAP > spikes:
        buf[...] = jnp.zeros_like(buf)
    tap = lax.broadcasted_iota(jnp.int32, (padded, win), 0)
    col = lax.broadcasted_iota(jnp.int32, (padded, win), 1)
    gap = jnp.where(tap < taps, col - tap, -1)

    def one(s):
        first = times_ref[s] - base
        start = jnp.minimum((first // 16) * 16, sub_rows - win)
        owner = labels_ref[s] // panel
        slot = cnt[owner]
        cnt[owner] = slot + 1
        pick = (gap == first - start).astype(jnp.bfloat16)
        window = rec_ref[pl.ds(pl.multiple_of(start, 16), win), :]
        snip = jnp.dot(pick, window, preferred_element_type=jnp.float32)
        for t in range(tm_count):
            row = (t * owners + owner) * (CAP * tpd) + slot * tpd
            buf[pl.ds(pl.multiple_of(row, tpd), tpd), :] = snip[t * tpd : (t + 1) * tpd]

    def group(g, carry):
        for i in range(8):
            one(g * 8 + i)
        return carry

    lax.fori_loop(0, spikes // 8, group, 0)
    send_ref[...] = buf[...].astype(jnp.bfloat16)


def pack(times, labels, base, rec, taps, panel, owners, tm_count, tpd):
    chans = rec.shape[1]
    rows = owners * tm_count * CAP * tpd
    smem = pl.BlockSpec(memory_space=pltpu.SMEM)
    vmem = pl.BlockSpec(memory_space=pltpu.VMEM)
    return pl.pallas_call(
        functools.partial(pack_kernel, taps, panel, owners, tm_count, tpd),
        out_shape=jax.ShapeDtypeStruct((rows, chans), jnp.bfloat16),
        in_specs=[smem, smem, smem, vmem],
        out_specs=vmem,
        scratch_shapes=[
            pltpu.VMEM((rows, chans), jnp.float32),
            pltpu.SMEM((owners,), jnp.int32),
        ],
        compiler_params=params(),
        cost_estimate=pl.CostEstimate(flops=10**8, bytes_accessed=4 * 10**6, transcendentals=0),
        name="pack",
    )(times, labels, base, rec)


def fold_kernel(*refs):
    out_ref = refs[-1]
    chans = refs[0].shape[1]
    block = 16 * ROWS
    new = lax.broadcasted_iota(jnp.int32, (block, block), 0)
    old = lax.broadcasted_iota(jnp.int32, (block, block), 1)
    perm = (old == (new % 16) * ROWS + new // 16).astype(jnp.bfloat16)
    at = 0
    for ref in refs[:-1]:
        for low in range(0, ref.shape[0], block):
            size = min(block, ref.shape[0] - low)
            part = jnp.dot(perm[:, :size], ref[low : low + size, :], preferred_element_type=jnp.float32)
            part = part.astype(jnp.bfloat16)
            for r in range(ROWS):
                out_ref[at : at + 16, r * chans : (r + 1) * chans] = part[r * 16 : (r + 1) * 16]
            at += 16


def fold(*parts):
    chans = parts[0].shape[1]
    blocks = sum(-(-p.shape[0] // (16 * ROWS)) for p in parts)
    vmem = pl.BlockSpec(memory_space=pltpu.VMEM)
    return pl.pallas_call(
        fold_kernel,
        out_shape=jax.ShapeDtypeStruct((blocks * 16, ROWS * chans), jnp.bfloat16),
        in_specs=[vmem] * len(parts),
        out_specs=vmem,
        compiler_params=params(),
        cost_estimate=pl.CostEstimate(flops=2 * 10**8, bytes_accessed=4 * 10**6, transcendentals=0),
        name="fold",
    )(*parts)


def refine_kernel(tpd, key_ref, got_ref, old_ref, out_ref, sums):
    panel = old_ref.shape[0]
    rows, chans = got_ref.shape
    step = min(rows, 2048)
    count = jnp.zeros((panel, 1), jnp.float32)
    for b in range(rows // step):
        key = key_ref[:, b * step : (b + 1) * step]
        wanted = lax.broadcasted_iota(jnp.int32, (tpd * panel, step), 0)
        wanted = (wanted % panel) * tpd + wanted // panel
        hit = (wanted == key).astype(jnp.float32)
        count = count + jnp.sum(hit[:panel], axis=1, keepdims=True)
        part = jnp.dot(
            hit.astype(jnp.bfloat16),
            got_ref[b * step : (b + 1) * step, :],
            preferred_element_type=jnp.float32,
        )
        if b == 0:
            sums[...] = part
        else:
            sums[...] += part
    weight = count / (count + 4.0)
    most = jnp.maximum(count, 1.0)
    for t in range(tpd):
        base = old_ref[:, t * chans : (t + 1) * chans].astype(jnp.float32)
        mean = sums[t * panel : (t + 1) * panel, :] / most
        out_ref[:, t * chans : (t + 1) * chans] = (base + weight * (mean - base)).astype(jnp.bfloat16)


def refine(key, got, old, tpd):
    vmem = pl.BlockSpec(memory_space=pltpu.VMEM)
    panel = old.shape[0]
    return pl.pallas_call(
        functools.partial(refine_kernel, tpd),
        out_shape=jax.ShapeDtypeStruct(old.shape, jnp.bfloat16),
        in_specs=[vmem] * 3,
        out_specs=vmem,
        scratch_shapes=[pltpu.VMEM((tpd * panel, got.shape[1]), jnp.float32)],
        compiler_params=params(),
        cost_estimate=pl.CostEstimate(flops=8 * 10**8, bytes_accessed=3 * 10**6, transcendentals=0),
        name="refine",
    )(key, got, old)


def correlate_kernel(chans, tpd, scale, masks, place_ref, *refs):
    count = len(masks)
    pieces, rest = refs[:count], refs[count:]
    mine_ref, early_ref, late_ref, out_ref, t_buf, e_buf, t_sem, e_sem, rhs, part, acc = rest
    half_rows = pieces[0].shape[1]
    lanes = tpd * chans
    chunks = t_sem.shape[0]
    blocks, panel, depth = t_buf.shape
    per = depth // lanes
    height = e_buf.shape[0] // 2
    keep = acc.shape[0] // 2
    shift = STRIDE * chans
    me, odd, pair = place_ref[0], place_ref[1], place_ref[2]

    def spot(chunk, part_of):
        rows = pl.ds(part_of * half_rows, half_rows)
        if per == 1:
            return t_buf.at[chunk, rows]
        first = chunk % per * lanes
        if not isinstance(chunk, int):
            first = pl.multiple_of(first, 128)
        return t_buf.at[chunk // per, rows, pl.ds(first, lanes)]

    e_copies = []
    low = 0
    for n, ref in enumerate((mine_ref, early_ref, late_ref)):
        size = ref.shape[0]
        e_copies.append(pltpu.make_async_copy(ref, e_buf.at[low : low + size, :], e_sem.at[n]))
        low += size
    for copy in e_copies:
        copy.start()
    for ref, (part_of, items) in zip(pieces, masks):
        for at, mask in enumerate(items):
            chunk = jnp.bitwise_xor(me, mask)
            pltpu.make_async_copy(ref.at[at], spot(chunk, part_of), t_sem.at[chunk, part_of]).start()
    for copy in e_copies:
        copy.wait()
    for a in range(blocks + 1):
        if a < blocks:
            for chunk in range(a * per, (a + 1) * per):
                for part_of in range(2):
                    sem = t_sem.at[chunk, part_of]
                    pltpu.make_async_copy(pieces[0].at[0], spot(chunk, part_of), sem).wait()
        used = depth if a < blocks else depth // 2
        for q in range(FOLD):
            rows = slice(q * panel, (q + 1) * panel)
            cut = q * shift
            low = min(cut, used)
            if low > 0:
                if a > 0:
                    rhs[rows, 0:low] = t_buf[a - 1, :, depth - cut : depth - cut + low]
                else:
                    rhs[rows, 0:low] = jnp.zeros((panel, low), jnp.bfloat16)
            if cut < used:
                if a < blocks:
                    rhs[rows, cut:used] = t_buf[a, :, 0 : used - cut]
                else:
                    rhs[rows, cut:used] = jnp.zeros((panel, used - cut), jnp.bfloat16)
        part[...] = lax.dot_general(
            e_buf[:, 0:used], rhs[:, 0:used], NT, preferred_element_type=jnp.float32
        )
        for h in range(2):
            found = part[h * height + a : h * height + a + keep, :]
            if a == 0:
                acc[h * keep : (h + 1) * keep, :] = found
            else:
                acc[h * keep : (h + 1) * keep, :] += found
    width = 128
    place = lax.broadcasted_iota(jnp.int32, (FOLD * width, FOLD * width), 0)
    lane = lax.broadcasted_iota(jnp.int32, (FOLD * width, FOLD * width), 1)
    weave = (lane == (place % width) * FOLD + place // width).astype(jnp.bfloat16)
    per_half = keep // width
    for h in range(2):
        side = odd if h == 0 else 1 - odd
        for b in range(per_half):
            first = h * keep + b * width
            turned = acc[first : first + width, :].T * scale
            row = jnp.concatenate([turned[q * panel : (q + 1) * panel] for q in range(FOLD)], axis=1)
            high = row.astype(jnp.bfloat16)
            found = jnp.dot(high, weave, preferred_element_type=jnp.float32)
            if out_ref.dtype == jnp.float32:
                rest = (row - high.astype(jnp.float32)).astype(jnp.bfloat16)
                found = found + jnp.dot(rest, weave, preferred_element_type=jnp.float32)
            at = ((2 * pair + side) * per_half + b) * (FOLD * width)
            at = pl.multiple_of(at, FOLD * width)
            out_ref[:, pl.ds(at, FOLD * width)] = found.astype(out_ref.dtype)


def correlate(place, gathered, windows, chans, tpd, scale, width, dtype):
    pieces = [value for value, _, _ in gathered]
    masks = [(part_of, items) for _, part_of, items in gathered]
    panel = 2 * pieces[0].shape[1]
    chunks = sum(len(items) for _, items in masks) // 2
    height = windows[0].shape[0]
    keep = height - 16
    depth = ROWS * chans
    anywhere = pl.BlockSpec(memory_space=pl.ANY)
    return pl.pallas_call(
        functools.partial(correlate_kernel, chans, tpd, scale, masks),
        out_shape=jax.ShapeDtypeStruct((panel, width), dtype),
        in_specs=[pl.BlockSpec(memory_space=pltpu.SMEM)] + [anywhere] * (len(pieces) + 3),
        out_specs=pl.BlockSpec(memory_space=pltpu.VMEM),
        scratch_shapes=[
            pltpu.VMEM((chunks * tpd // ROWS, panel, depth), jnp.bfloat16),
            pltpu.VMEM((2 * height, depth), jnp.bfloat16),
            pltpu.SemaphoreType.DMA((chunks, 2)),
            pltpu.SemaphoreType.DMA((3,)),
            pltpu.VMEM((FOLD * panel, depth), jnp.bfloat16),
            pltpu.VMEM((2 * height, FOLD * panel), jnp.float32),
            pltpu.VMEM((2 * keep, FOLD * panel), jnp.float32),
        ],
        compiler_params=params(),
        cost_estimate=pl.CostEstimate(flops=8 * 10**9, bytes_accessed=8 * 10**6, transcendentals=0),
        name="correlate",
    )(place, *pieces, *windows)


def swap(value, bit):
    size = lax.axis_size("tm")
    return lax.ppermute(value, "tm", [(i, i ^ bit) for i in range(size)])


def gather_panel(value):
    bits = []
    while 2 << len(bits) < lax.axis_size("tm"):
        bits.append(2 << len(bits))
    rows = value.shape[0] // 2
    out = []
    for part_of, order in enumerate((bits[::-1], bits)):
        parts = [(value[part_of * rows : (part_of + 1) * rows][None], [0])]
        for bit in order:
            held = jnp.concatenate([v for v, _ in parts], axis=0) if len(parts) > 1 else parts[0][0]
            items = [m for _, ms in parts for m in ms]
            parts = [(held, items), (swap(held, bit), [m ^ bit for m in items])]
        out += [(v, part_of, ms) for v, ms in parts]
    return out + [(swap(v, 1), part_of, [m ^ 1 for m in ms]) for v, part_of, ms in out]


def body(recording, spike_times, unit_labels, old_templates):
    sub_rows, chans = recording.shape
    panel, feat = old_templates.shape
    taps = feat // chans
    half = (taps - 1) // 2
    owners = lax.axis_size("unit")
    tm_count = lax.axis_size("tm")
    devices = owners * tm_count
    spikes = spike_times.shape[0]
    tm_pos = lax.axis_index("tm")
    unit_pos = lax.axis_index("unit")
    flat_pos = tm_pos * owners + unit_pos
    tpd = -(-taps // tm_count)
    padded = tpd * tm_count
    keep = sub_rows // ROWS
    scale = 1.0 / (float(feat) ** 0.5)

    base = (flat_pos * sub_rows + half).astype(jnp.int32).reshape(1)
    groups = padded // ROWS
    send = pack(spike_times, unit_labels, base, recording, taps, panel, owners, groups, ROWS)
    if tpd != ROWS:
        send = send.reshape(groups, owners, CAP, ROWS // tpd, tpd, chans)
        send = jnp.transpose(send, (0, 3, 1, 2, 4, 5))
    owner = unit_labels // panel
    hits = (owner[:, None] == jnp.arange(owners)[None, :]).astype(jnp.int32)
    rank = jnp.sum((jnp.cumsum(hits, axis=0) - hits) * hits, axis=1)
    placing = jnp.arange(owners * CAP)[:, None] == (owner * CAP + rank)[None, :]
    tags = jnp.sum(jnp.where(placing, (unit_labels % panel + 1)[None, :], 0), axis=1) - 1
    tags = jnp.broadcast_to(tags.reshape(1, owners, CAP), (tm_count, owners, CAP))
    tags = tags.reshape(devices, CAP)
    tags = lax.all_to_all(tags, AXES, split_axis=0, concat_axis=0, tiled=True)
    key = (tags[:, :, None] * tpd + jnp.arange(tpd)[None, None, :]).reshape(1, -1)
    pairs = [(i, i ^ 1) for i in range(owners)]
    first = sub_rows * 7 // 16 // (16 * ROWS) * (16 * ROWS)
    early = lax.ppermute(recording[:first], "unit", pairs)
    send, key, early, before = lax.optimization_barrier((send, key, early, old_templates))
    got = lax.all_to_all(
        send.reshape(devices, CAP * tpd, chans), AXES, split_axis=0, concat_axis=0, tiled=True
    ).reshape(devices * CAP * tpd, chans)

    cube = before.reshape(panel, chans, taps)
    cube = jnp.pad(cube, ((0, 0), (0, 0), (0, padded - taps)))
    cube = lax.dynamic_slice_in_dim(cube, tm_pos * tpd, tpd, 2)
    old = jnp.transpose(cube, (0, 2, 1)).reshape(panel, tpd * chans)

    got, rest = lax.optimization_barrier((got, recording))
    head = rest[:padded]
    follow = lax.ppermute(head, AXES, [(i, i - 1) for i in range(1, devices)])
    skip = lax.ppermute(head, AXES, [(i, i - 2) for i in range(2, devices, 2)])
    late = lax.ppermute(rest[first:], "unit", pairs)
    odd = unit_pos % 2

    fresh = refine(key, got, old, tpd)
    early, rest, fresh = lax.optimization_barrier((early, rest, fresh))
    mine = fold(rest, follow)
    early = fold(early)
    own = gather_panel(fresh)
    width = 2 * keep * FOLD

    share = chans // tm_count
    order = []
    pieces = [[], []]
    for value, part_of, items in own:
        value = value.reshape(len(items), panel // 2, tpd, chans)
        pieces[part_of].append(lax.dynamic_slice_in_dim(value, tm_pos * share, share, 3))
        order += items if part_of == 0 else []
    order_b = [m for _, part_of, items in own if part_of == 1 for m in items]
    part = []
    for found, masks in ((pieces[0], order), (pieces[1], order_b)):
        spots = jnp.array([masks.index(m) for m in range(tm_count)])
        stacked = jnp.concatenate(found, axis=0)
        picks = spots[jnp.bitwise_xor(jnp.arange(tm_count), tm_pos)]
        part.append(jnp.take(stacked, picks, axis=0))
    part = jnp.concatenate(part, axis=1)
    part = jnp.transpose(part, (1, 3, 0, 2)).reshape(panel, share, padded)[:, :, :taps]
    part = part.reshape(panel, share * taps)

    found = []
    for m in range(1, owners // 2):
        ahead = [(i, (i + 2 * m) % owners) for i in range(owners)]
        back = [(j, i) for i, j in ahead]
        chunk = lax.ppermute(fresh, "unit", ahead)
        if m == 1:
            chunk, mine, early = lax.optimization_barrier((chunk, mine, early))
        other = gather_panel(chunk)
        if m == 1:
            windows = (mine, early, fold(late, jnp.where(odd == 1, head, skip)))
            tied = lax.optimization_barrier((part, *[v for v, _, _ in other]))
            part = tied[0]
            other = [(v, n, ms) for v, (_, n, ms) in zip(tied[1:], other)]
        place = jnp.stack([tm_pos, odd, 0 * odd]).astype(jnp.int32)
        out = correlate(place, other, windows, chans, tpd, scale, width, jnp.bfloat16)
        found.append((lax.ppermute(out, "unit", back), ((unit_pos + 2 * m) % owners) // 2))
    place = jnp.stack([tm_pos, odd, unit_pos // 2]).astype(jnp.int32)
    place, _ = lax.optimization_barrier((place, out))
    scores = correlate(place, own, windows, chans, tpd, scale, owners // 2 * width, jnp.float32)
    for out, pair in found:
        scores = lax.dynamic_update_slice_in_dim(
            scores, out.astype(jnp.float32), pair * width, 1
        )
    return (part, scores)


def solution(mesh):
    in_specs = (P(AXES, None), P(AXES), P(AXES), P("unit", None))
    out_specs = (P("unit", "tm"), P("unit", "tm"))
    return jax.shard_map(body, mesh=mesh, in_specs=in_specs, out_specs=out_specs, check_vma=False)
```

```python
import functools

import jax
import jax.numpy as jnp
from jax import lax
from jax.experimental import pallas as pl
from jax.experimental.pallas import tpu as pltpu
from jax.sharding import PartitionSpec as P

STRIDE = 2
CAP = 8
FOLD = 4
ROWS = STRIDE * FOLD
AXES = ("tm", "unit")
MIB = 1024 * 1024
NT = (((1,), (1,)), ((), ()))


def params(mib):
    return pltpu.CompilerParams(vmem_limit_bytes=mib * MIB)


def pack_kernel(
    taps, panel, owners, tm_count, tpd, times_ref, labels_ref, base_ref, rec_ref, send_ref, buf, cnt
):
    spikes = times_ref.shape[0]
    sub_rows = rec_ref.shape[0]
    padded = tm_count * tpd
    win = padded + 16
    base = base_ref[0]
    for o in range(owners):
        cnt[o] = 0
    if owners * CAP > spikes:
        buf[...] = jnp.zeros_like(buf)
    tap = lax.broadcasted_iota(jnp.int32, (padded, win), 0)
    col = lax.broadcasted_iota(jnp.int32, (padded, win), 1)
    gap = jnp.where(tap < taps, col - tap, -1)

    def one(s):
        first = times_ref[s] - base
        start = jnp.minimum((first // 16) * 16, sub_rows - win)
        owner = labels_ref[s] // panel
        slot = cnt[owner]
        cnt[owner] = slot + 1
        pick = (gap == first - start).astype(jnp.bfloat16)
        window = rec_ref[pl.ds(pl.multiple_of(start, 16), win), :]
        snip = jnp.dot(pick, window, preferred_element_type=jnp.float32)
        for t in range(tm_count):
            row = (t * owners + owner) * (CAP * tpd) + slot * tpd
            buf[pl.ds(pl.multiple_of(row, tpd), tpd), :] = snip[t * tpd : (t + 1) * tpd]

    def group(g, carry):
        for i in range(8):
            one(g * 8 + i)
        return carry

    lax.fori_loop(0, spikes // 8, group, 0)
    send_ref[...] = buf[...].astype(jnp.bfloat16)


def pack(times, labels, base, rec, taps, panel, owners, tm_count, tpd):
    chans = rec.shape[1]
    rows = owners * tm_count * CAP * tpd
    smem = pl.BlockSpec(memory_space=pltpu.SMEM)
    vmem = pl.BlockSpec(memory_space=pltpu.VMEM)
    return pl.pallas_call(
        functools.partial(pack_kernel, taps, panel, owners, tm_count, tpd),
        out_shape=jax.ShapeDtypeStruct((rows, chans), jnp.bfloat16),
        in_specs=[smem, smem, smem, vmem],
        out_specs=vmem,
        scratch_shapes=[
            pltpu.VMEM((rows, chans), jnp.float32),
            pltpu.SMEM((owners,), jnp.int32),
        ],
        compiler_params=params(24),
        cost_estimate=pl.CostEstimate(flops=10**8, bytes_accessed=4 * 10**6, transcendentals=0),
        name="pack",
    )(times, labels, base, rec)


def fold_kernel(*refs):
    out_ref = refs[-1]
    chans = refs[0].shape[1]
    block = 16 * ROWS
    new = lax.broadcasted_iota(jnp.int32, (block, block), 0)
    old = lax.broadcasted_iota(jnp.int32, (block, block), 1)
    perm = (old == (new % 16) * ROWS + new // 16).astype(jnp.bfloat16)
    at = 0
    for ref in refs[:-1]:
        for low in range(0, ref.shape[0], block):
            size = min(block, ref.shape[0] - low)
            part = jnp.dot(perm[:, :size], ref[low : low + size, :], preferred_element_type=jnp.float32)
            part = part.astype(jnp.bfloat16)
            for r in range(ROWS):
                out_ref[at : at + 16, r * chans : (r + 1) * chans] = part[r * 16 : (r + 1) * 16]
            at += 16


def fold(*parts):
    chans = parts[0].shape[1]
    blocks = sum(-(-p.shape[0] // (16 * ROWS)) for p in parts)
    vmem = pl.BlockSpec(memory_space=pltpu.VMEM)
    return pl.pallas_call(
        fold_kernel,
        out_shape=jax.ShapeDtypeStruct((blocks * 16, ROWS * chans), jnp.bfloat16),
        in_specs=[vmem] * len(parts),
        out_specs=vmem,
        compiler_params=params(14),
        cost_estimate=pl.CostEstimate(flops=2 * 10**8, bytes_accessed=4 * 10**6, transcendentals=0),
        name="fold",
    )(*parts)


def refine_kernel(tpd, key_ref, got_ref, old_ref, out_ref, sums):
    panel = old_ref.shape[0]
    rows, chans = got_ref.shape
    step = min(rows, 2048)
    count = jnp.zeros((panel, 1), jnp.float32)
    for b in range(rows // step):
        key = key_ref[:, b * step : (b + 1) * step]
        wanted = lax.broadcasted_iota(jnp.int32, (tpd * panel, step), 0)
        wanted = (wanted % panel) * tpd + wanted // panel
        hit = (wanted == key).astype(jnp.float32)
        count = count + jnp.sum(hit[:panel], axis=1, keepdims=True)
        part = jnp.dot(
            hit.astype(jnp.bfloat16),
            got_ref[b * step : (b + 1) * step, :],
            preferred_element_type=jnp.float32,
        )
        if b == 0:
            sums[...] = part
        else:
            sums[...] += part
    weight = count / (count + 4.0)
    most = jnp.maximum(count, 1.0)
    for t in range(tpd):
        base = old_ref[:, t * chans : (t + 1) * chans].astype(jnp.float32)
        mean = sums[t * panel : (t + 1) * panel, :] / most
        out_ref[:, t * chans : (t + 1) * chans] = (base + weight * (mean - base)).astype(jnp.bfloat16)


def refine(key, got, old, tpd):
    vmem = pl.BlockSpec(memory_space=pltpu.VMEM)
    panel = old.shape[0]
    return pl.pallas_call(
        functools.partial(refine_kernel, tpd),
        out_shape=jax.ShapeDtypeStruct(old.shape, jnp.bfloat16),
        in_specs=[vmem] * 3,
        out_specs=vmem,
        scratch_shapes=[pltpu.VMEM((tpd * panel, got.shape[1]), jnp.float32)],
        compiler_params=params(32),
        cost_estimate=pl.CostEstimate(flops=8 * 10**8, bytes_accessed=3 * 10**6, transcendentals=0),
        name="refine",
    )(key, got, old)


def correlate_kernel(chans, tpd, scale, masks, place_ref, *refs):
    count = len(masks)
    pieces, rest = refs[:count], refs[count:]
    mine_ref, early_ref, late_ref, out_ref, t_buf, e_buf, rhs, part, acc = rest
    half_rows = pieces[0].shape[1]
    lanes = tpd * chans
    blocks, panel, depth = t_buf.shape
    per = depth // lanes
    height = e_buf.shape[0] // 2
    keep = acc.shape[0] // 2
    shift = STRIDE * chans
    me, odd, pair = place_ref[0], place_ref[1], place_ref[2]
    early = early_ref.shape[0]
    e_buf[0:keep, :] = mine_ref[...]
    e_buf[keep:height, :] = late_ref[0 : height - keep, :]
    e_buf[height : height + early, :] = early_ref[...]
    e_buf[height + early :, :] = late_ref[height - keep :, :]
    for ref, (part_of, items) in zip(pieces, masks):
        rows = slice(part_of * half_rows, (part_of + 1) * half_rows)
        for at, mask in enumerate(items):
            chunk = jnp.bitwise_xor(me, mask)
            if per == 1:
                t_buf[chunk, rows, :] = ref[at]
            else:
                first = pl.multiple_of(chunk % per * lanes, 128)
                t_buf[chunk // per, rows, pl.ds(first, lanes)] = ref[at]
    for a in range(blocks + 1):
        used = depth if a < blocks else depth // 2
        for q in range(FOLD):
            rows = slice(q * panel, (q + 1) * panel)
            cut = q * shift
            low = min(cut, used)
            if low > 0:
                if a > 0:
                    rhs[rows, 0:low] = t_buf[a - 1, :, depth - cut : depth - cut + low]
                else:
                    rhs[rows, 0:low] = jnp.zeros((panel, low), jnp.bfloat16)
            if cut < used:
                if a < blocks:
                    rhs[rows, cut:used] = t_buf[a, :, 0 : used - cut]
                else:
                    rhs[rows, cut:used] = jnp.zeros((panel, used - cut), jnp.bfloat16)
        part[...] = lax.dot_general(
            e_buf[:, 0:used], rhs[:, 0:used], NT, preferred_element_type=jnp.float32
        )
        for h in range(2):
            found = part[h * height + a : h * height + a + keep, :]
            if a == 0:
                acc[h * keep : (h + 1) * keep, :] = found
            else:
                acc[h * keep : (h + 1) * keep, :] += found
    width = 128
    place = lax.broadcasted_iota(jnp.int32, (FOLD * width, FOLD * width), 0)
    lane = lax.broadcasted_iota(jnp.int32, (FOLD * width, FOLD * width), 1)
    weave = (lane == (place % width) * FOLD + place // width).astype(jnp.bfloat16)
    per_half = keep // width
    for h in range(2):
        side = odd if h == 0 else 1 - odd
        for b in range(per_half):
            first = h * keep + b * width
            turned = acc[first : first + width, :].T * scale
            row = jnp.concatenate([turned[q * panel : (q + 1) * panel] for q in range(FOLD)], axis=1)
            high = row.astype(jnp.bfloat16)
            found = jnp.dot(high, weave, preferred_element_type=jnp.float32)
            if out_ref.dtype == jnp.float32:
                rest = (row - high.astype(jnp.float32)).astype(jnp.bfloat16)
                found = found + jnp.dot(rest, weave, preferred_element_type=jnp.float32)
            at = ((2 * pair + side) * per_half + b) * (FOLD * width)
            at = pl.multiple_of(at, FOLD * width)
            out_ref[:, pl.ds(at, FOLD * width)] = found.astype(out_ref.dtype)


def correlate(place, gathered, windows, chans, tpd, scale, width, dtype):
    pieces = [value for value, _, _ in gathered]
    masks = [(part_of, items) for _, part_of, items in gathered]
    panel = 2 * pieces[0].shape[1]
    chunks = sum(len(items) for _, items in masks) // 2
    keep = windows[0].shape[0]
    height = keep + 16
    depth = ROWS * chans
    vmem = pl.BlockSpec(memory_space=pltpu.VMEM)
    return pl.pallas_call(
        functools.partial(correlate_kernel, chans, tpd, scale, masks),
        out_shape=jax.ShapeDtypeStruct((panel, width), dtype),
        in_specs=[pl.BlockSpec(memory_space=pltpu.SMEM)] + [vmem] * (len(pieces) + 3),
        out_specs=vmem,
        scratch_shapes=[
            pltpu.VMEM((chunks * tpd // ROWS, panel, depth), jnp.bfloat16),
            pltpu.VMEM((2 * height, depth), jnp.bfloat16),
            pltpu.VMEM((FOLD * panel, depth), jnp.bfloat16),
            pltpu.VMEM((2 * height, FOLD * panel), jnp.float32),
            pltpu.VMEM((2 * keep, FOLD * panel), jnp.float32),
        ],
        compiler_params=params(30),
        cost_estimate=pl.CostEstimate(flops=8 * 10**9, bytes_accessed=8 * 10**6, transcendentals=0),
        name="correlate",
    )(place, *pieces, *windows)


def swap(value, bit):
    size = lax.axis_size("tm")
    return lax.ppermute(value, "tm", [(i, i ^ bit) for i in range(size)])


def gather_panel(value):
    bits = []
    while 2 << len(bits) < lax.axis_size("tm"):
        bits.append(2 << len(bits))
    rows = value.shape[0] // 2
    out = []
    for part_of, order in enumerate((bits[::-1], bits)):
        parts = [(value[part_of * rows : (part_of + 1) * rows][None], [0])]
        for bit in order:
            held = jnp.concatenate([v for v, _ in parts], axis=0) if len(parts) > 1 else parts[0][0]
            items = [m for _, ms in parts for m in ms]
            parts = [(held, items), (swap(held, bit), [m ^ bit for m in items])]
        out += [(v, part_of, ms) for v, ms in parts]
    return out + [(swap(v, 1), part_of, [m ^ 1 for m in ms]) for v, part_of, ms in out]


def body(recording, spike_times, unit_labels, old_templates):
    sub_rows, chans = recording.shape
    panel, feat = old_templates.shape
    taps = feat // chans
    half = (taps - 1) // 2
    owners = lax.axis_size("unit")
    tm_count = lax.axis_size("tm")
    devices = owners * tm_count
    spikes = spike_times.shape[0]
    tm_pos = lax.axis_index("tm")
    unit_pos = lax.axis_index("unit")
    flat_pos = tm_pos * owners + unit_pos
    tpd = -(-taps // tm_count)
    padded = tpd * tm_count
    keep = sub_rows // ROWS
    scale = 1.0 / (float(feat) ** 0.5)

    base = (flat_pos * sub_rows + half).astype(jnp.int32).reshape(1)
    groups = padded // ROWS
    send = pack(spike_times, unit_labels, base, recording, taps, panel, owners, groups, ROWS)
    if tpd != ROWS:
        send = send.reshape(groups, owners, CAP, ROWS // tpd, tpd, chans)
        send = jnp.transpose(send, (0, 3, 1, 2, 4, 5))
    owner = unit_labels // panel
    hits = (owner[:, None] == jnp.arange(owners)[None, :]).astype(jnp.int32)
    rank = jnp.sum((jnp.cumsum(hits, axis=0) - hits) * hits, axis=1)
    placing = jnp.arange(owners * CAP)[:, None] == (owner * CAP + rank)[None, :]
    tags = jnp.sum(jnp.where(placing, (unit_labels % panel + 1)[None, :], 0), axis=1) - 1
    tags = jnp.broadcast_to(tags.reshape(1, owners, CAP), (tm_count, owners, CAP))
    tags = tags.reshape(devices, CAP)
    tags = lax.all_to_all(tags, AXES, split_axis=0, concat_axis=0, tiled=True)
    key = (tags[:, :, None] * tpd + jnp.arange(tpd)[None, None, :]).reshape(1, -1)
    pairs = [(i, i ^ 1) for i in range(owners)]
    first = sub_rows // 4 // (16 * ROWS) * (16 * ROWS)
    early = lax.ppermute(recording[:first], "unit", pairs)
    send, key, early, before = lax.optimization_barrier((send, key, early, old_templates))
    got = lax.all_to_all(
        send.reshape(devices, CAP * tpd, chans), AXES, split_axis=0, concat_axis=0, tiled=True
    ).reshape(devices * CAP * tpd, chans)

    cube = before.reshape(panel, chans, taps)
    cube = jnp.pad(cube, ((0, 0), (0, 0), (0, padded - taps)))
    cube = lax.dynamic_slice_in_dim(cube, tm_pos * tpd, tpd, 2)
    old = jnp.transpose(cube, (0, 2, 1)).reshape(panel, tpd * chans)

    got, rest = lax.optimization_barrier((got, recording))
    head = rest[:padded]
    follow = lax.ppermute(head, AXES, [(i, i - 1) for i in range(1, devices)])
    skip = lax.ppermute(head, AXES, [(i, i - 2) for i in range(2, devices, 2)])
    late = lax.ppermute(rest[first:], "unit", pairs)
    odd = unit_pos % 2

    fresh = refine(key, got, old, tpd)
    early, rest, fresh = lax.optimization_barrier((early, rest, fresh))
    mine = fold(rest)
    early = fold(early)
    own = gather_panel(fresh)
    width = 2 * keep * FOLD

    share = chans // tm_count
    order = []
    pieces = [[], []]
    for value, part_of, items in own:
        value = value.reshape(len(items), panel // 2, tpd, chans)
        pieces[part_of].append(lax.dynamic_slice_in_dim(value, tm_pos * share, share, 3))
        order += items if part_of == 0 else []
    order_b = [m for _, part_of, items in own if part_of == 1 for m in items]
    part = []
    for found, masks in ((pieces[0], order), (pieces[1], order_b)):
        spots = jnp.array([masks.index(m) for m in range(tm_count)])
        stacked = jnp.concatenate(found, axis=0)
        picks = spots[jnp.bitwise_xor(jnp.arange(tm_count), tm_pos)]
        part.append(jnp.take(stacked, picks, axis=0))
    part = jnp.concatenate(part, axis=1)
    part = jnp.transpose(part, (1, 3, 0, 2)).reshape(panel, share, padded)[:, :, :taps]
    part = part.reshape(panel, share * taps)

    found = []
    for m in range(1, owners // 2):
        ahead = [(i, (i + 2 * m) % owners) for i in range(owners)]
        back = [(j, i) for i, j in ahead]
        chunk = lax.ppermute(fresh, "unit", ahead)
        if m == 1:
            chunk, mine, early = lax.optimization_barrier((chunk, mine, early))
        other = gather_panel(chunk)
        if m == 1:
            windows = (mine, early, fold(follow, late, jnp.where(odd == 1, head, skip)))
            tied = lax.optimization_barrier((part, *[v for v, _, _ in other]))
            part = tied[0]
            other = [(v, n, ms) for v, (_, n, ms) in zip(tied[1:], other)]
        place = jnp.stack([tm_pos, odd, 0 * odd]).astype(jnp.int32)
        out = correlate(place, other, windows, chans, tpd, scale, width, jnp.bfloat16)
        found.append((lax.ppermute(out, "unit", back), ((unit_pos + 2 * m) % owners) // 2))
    place = jnp.stack([tm_pos, odd, unit_pos // 2]).astype(jnp.int32)
    place, _ = lax.optimization_barrier((place, out))
    scores = correlate(place, own, windows, chans, tpd, scale, owners // 2 * width, jnp.float32)
    for out, pair in found:
        scores = lax.dynamic_update_slice_in_dim(
            scores, out.astype(jnp.float32), pair * width, 1
        )
    return (part, scores)


def solution(mesh):
    in_specs = (P(AXES, None), P(AXES), P(AXES), P("unit", None))
    out_specs = (P("unit", "tm"), P("unit", "tm"))
    return jax.shard_map(body, mesh=mesh, in_specs=in_specs, out_specs=out_specs, check_vma=False)
```

```python
import functools

import jax
import jax.numpy as jnp
from jax import lax
from jax.experimental import pallas as pl
from jax.experimental.pallas import tpu as pltpu
from jax.sharding import PartitionSpec as P

STRIDE = 2
CAP = 8
FOLD = 4
ROWS = STRIDE * FOLD
AXES = ("tm", "unit")
MIB = 1024 * 1024
NT = (((1,), (1,)), ((), ()))


def params(mib):
    return pltpu.CompilerParams(vmem_limit_bytes=mib * MIB)


def pack_kernel(
    taps, panel, owners, tm_count, tpd, times_ref, labels_ref, base_ref, rec_ref, send_ref, buf, cnt
):
    spikes = times_ref.shape[0]
    sub_rows = rec_ref.shape[0]
    padded = tm_count * tpd
    win = padded + 16
    base = base_ref[0]
    for o in range(owners):
        cnt[o] = 0
    if owners * CAP > spikes:
        buf[...] = jnp.zeros_like(buf)
    tap = lax.broadcasted_iota(jnp.int32, (padded, win), 0)
    col = lax.broadcasted_iota(jnp.int32, (padded, win), 1)
    gap = jnp.where(tap < taps, col - tap, -1)

    def one(s):
        first = times_ref[s] - base
        start = jnp.minimum((first // 16) * 16, sub_rows - win)
        owner = labels_ref[s] // panel
        slot = cnt[owner]
        cnt[owner] = slot + 1
        pick = (gap == first - start).astype(jnp.bfloat16)
        window = rec_ref[pl.ds(pl.multiple_of(start, 16), win), :]
        snip = jnp.dot(pick, window, preferred_element_type=jnp.float32)
        for t in range(tm_count):
            row = (t * owners + owner) * (CAP * tpd) + slot * tpd
            buf[pl.ds(pl.multiple_of(row, tpd), tpd), :] = snip[t * tpd : (t + 1) * tpd]

    def group(g, carry):
        for i in range(8):
            one(g * 8 + i)
        return carry

    lax.fori_loop(0, spikes // 8, group, 0)
    send_ref[...] = buf[...].astype(jnp.bfloat16)


def pack(times, labels, base, rec, taps, panel, owners, tm_count, tpd):
    chans = rec.shape[1]
    rows = owners * tm_count * CAP * tpd
    smem = pl.BlockSpec(memory_space=pltpu.SMEM)
    vmem = pl.BlockSpec(memory_space=pltpu.VMEM)
    return pl.pallas_call(
        functools.partial(pack_kernel, taps, panel, owners, tm_count, tpd),
        out_shape=jax.ShapeDtypeStruct((rows, chans), jnp.bfloat16),
        in_specs=[smem, smem, smem, vmem],
        out_specs=vmem,
        scratch_shapes=[
            pltpu.VMEM((rows, chans), jnp.float32),
            pltpu.SMEM((owners,), jnp.int32),
        ],
        compiler_params=params(24),
        cost_estimate=pl.CostEstimate(flops=10**8, bytes_accessed=4 * 10**6, transcendentals=0),
        name="pack",
    )(times, labels, base, rec)


def fold_kernel(*refs):
    out_ref = refs[-1]
    chans = refs[0].shape[1]
    block = 16 * ROWS
    new = lax.broadcasted_iota(jnp.int32, (block, block), 0)
    old = lax.broadcasted_iota(jnp.int32, (block, block), 1)
    perm = (old == (new % 16) * ROWS + new // 16).astype(jnp.bfloat16)
    at = 0
    for ref in refs[:-1]:
        for low in range(0, ref.shape[0], block):
            size = min(block, ref.shape[0] - low)
            part = jnp.dot(perm[:, :size], ref[low : low + size, :], preferred_element_type=jnp.float32)
            part = part.astype(jnp.bfloat16)
            for r in range(ROWS):
                out_ref[at : at + 16, r * chans : (r + 1) * chans] = part[r * 16 : (r + 1) * 16]
            at += 16


def fold(*parts):
    chans = parts[0].shape[1]
    blocks = sum(-(-p.shape[0] // (16 * ROWS)) for p in parts)
    vmem = pl.BlockSpec(memory_space=pltpu.VMEM)
    return pl.pallas_call(
        fold_kernel,
        out_shape=jax.ShapeDtypeStruct((blocks * 16, ROWS * chans), jnp.bfloat16),
        in_specs=[vmem] * len(parts),
        out_specs=vmem,
        compiler_params=params(14),
        cost_estimate=pl.CostEstimate(flops=2 * 10**8, bytes_accessed=4 * 10**6, transcendentals=0),
        name="fold",
    )(*parts)


def refine_kernel(tpd, key_ref, got_ref, old_ref, out_ref, sums):
    panel = old_ref.shape[0]
    rows, chans = got_ref.shape
    step = min(rows, 2048)
    count = jnp.zeros((panel, 1), jnp.float32)
    for b in range(rows // step):
        key = key_ref[:, b * step : (b + 1) * step]
        wanted = lax.broadcasted_iota(jnp.int32, (tpd * panel, step), 0)
        wanted = (wanted % panel) * tpd + wanted // panel
        hit = (wanted == key).astype(jnp.float32)
        count = count + jnp.sum(hit[:panel], axis=1, keepdims=True)
        part = jnp.dot(
            hit.astype(jnp.bfloat16),
            got_ref[b * step : (b + 1) * step, :],
            preferred_element_type=jnp.float32,
        )
        if b == 0:
            sums[...] = part
        else:
            sums[...] += part
    weight = count / (count + 4.0)
    most = jnp.maximum(count, 1.0)
    for t in range(tpd):
        base = old_ref[:, t * chans : (t + 1) * chans].astype(jnp.float32)
        mean = sums[t * panel : (t + 1) * panel, :] / most
        out_ref[:, t * chans : (t + 1) * chans] = (base + weight * (mean - base)).astype(jnp.bfloat16)


def refine(key, got, old, tpd):
    vmem = pl.BlockSpec(memory_space=pltpu.VMEM)
    panel = old.shape[0]
    return pl.pallas_call(
        functools.partial(refine_kernel, tpd),
        out_shape=jax.ShapeDtypeStruct(old.shape, jnp.bfloat16),
        in_specs=[vmem] * 3,
        out_specs=vmem,
        scratch_shapes=[pltpu.VMEM((tpd * panel, got.shape[1]), jnp.float32)],
        compiler_params=params(32),
        cost_estimate=pl.CostEstimate(flops=8 * 10**8, bytes_accessed=3 * 10**6, transcendentals=0),
        name="refine",
    )(key, got, old)


def correlate_kernel(chans, tpd, scale, masks, share, place_ref, *refs):
    count = len(masks)
    pieces, rest = refs[:count], refs[count:]
    mine_ref, early_ref, late_ref, out_ref = rest[:4]
    t_buf, e_buf, rhs, part, acc = rest[-5:]
    half_rows = pieces[0].shape[1]
    lanes = tpd * chans
    blocks, panel, depth = t_buf.shape
    per = depth // lanes
    height = e_buf.shape[0] // 2
    keep = acc.shape[0] // 2
    shift = STRIDE * chans
    me, odd, pair = place_ref[0], place_ref[1], place_ref[2]
    early = early_ref.shape[0]
    e_buf[0:keep, :] = mine_ref[...]
    e_buf[keep:height, :] = late_ref[0 : height - keep, :]
    e_buf[height : height + early, :] = early_ref[...]
    e_buf[height + early :, :] = late_ref[height - keep :, :]
    for ref, (part_of, items) in zip(pieces, masks):
        rows = slice(part_of * half_rows, (part_of + 1) * half_rows)
        for at, mask in enumerate(items):
            chunk = jnp.bitwise_xor(me, mask)
            if per == 1:
                t_buf[chunk, rows, :] = ref[at]
            else:
                first = pl.multiple_of(chunk % per * lanes, 128)
                t_buf[chunk // per, rows, pl.ds(first, lanes)] = ref[at]
    if share:
        pick_ref = rest[4]
        wide = pick_ref.shape[2]
        channel = lax.broadcasted_iota(jnp.int32, (chans, wide), 0)
        lane = lax.broadcasted_iota(jnp.int32, (chans, wide), 1)
        pick = ((channel == me * share + lane) & (lane < share)).astype(jnp.bfloat16)
        for b in range(blocks):
            for r in range(ROWS):
                taken = t_buf[b, :, r * chans : (r + 1) * chans]
                taken = jnp.dot(taken, pick, preferred_element_type=jnp.float32)
                pick_ref[b * ROWS + r] = taken.astype(jnp.bfloat16)
    for a in range(blocks + 1):
        used = depth if a < blocks else depth // 2
        for q in range(FOLD):
            rows = slice(q * panel, (q + 1) * panel)
            cut = q * shift
            low = min(cut, used)
            if low > 0:
                if a > 0:
                    rhs[rows, 0:low] = t_buf[a - 1, :, depth - cut : depth - cut + low]
                else:
                    rhs[rows, 0:low] = jnp.zeros((panel, low), jnp.bfloat16)
            if cut < used:
                if a < blocks:
                    rhs[rows, cut:used] = t_buf[a, :, 0 : used - cut]
                else:
                    rhs[rows, cut:used] = jnp.zeros((panel, used - cut), jnp.bfloat16)
        part[...] = lax.dot_general(
            e_buf[:, 0:used], rhs[:, 0:used], NT, preferred_element_type=jnp.float32
        )
        for h in range(2):
            found = part[h * height + a : h * height + a + keep, :]
            if a == 0:
                acc[h * keep : (h + 1) * keep, :] = found
            else:
                acc[h * keep : (h + 1) * keep, :] += found
    width = 128
    place = lax.broadcasted_iota(jnp.int32, (FOLD * width, FOLD * width), 0)
    lane = lax.broadcasted_iota(jnp.int32, (FOLD * width, FOLD * width), 1)
    weave = (lane == (place % width) * FOLD + place // width).astype(jnp.bfloat16)
    per_half = keep // width
    for h in range(2):
        side = odd if h == 0 else 1 - odd
        for b in range(per_half):
            first = h * keep + b * width
            turned = acc[first : first + width, :].T * scale
            row = jnp.concatenate([turned[q * panel : (q + 1) * panel] for q in range(FOLD)], axis=1)
            high = row.astype(jnp.bfloat16)
            found = jnp.dot(high, weave, preferred_element_type=jnp.float32)
            if out_ref.dtype == jnp.float32:
                rest = (row - high.astype(jnp.float32)).astype(jnp.bfloat16)
                found = found + jnp.dot(rest, weave, preferred_element_type=jnp.float32)
            at = ((2 * pair + side) * per_half + b) * (FOLD * width)
            at = pl.multiple_of(at, FOLD * width)
            out_ref[:, pl.ds(at, FOLD * width)] = found.astype(out_ref.dtype)


def correlate(place, gathered, windows, chans, tpd, scale, width, dtype, share=0):
    pieces = [value for value, _, _ in gathered]
    masks = [(part_of, items) for _, part_of, items in gathered]
    panel = 2 * pieces[0].shape[1]
    chunks = sum(len(items) for _, items in masks) // 2
    keep = windows[0].shape[0]
    height = keep + 16
    depth = ROWS * chans
    vmem = pl.BlockSpec(memory_space=pltpu.VMEM)
    outs = [
        jax.ShapeDtypeStruct((panel, width), dtype),
        jax.ShapeDtypeStruct((chunks * tpd, panel, -(-share // 128) * 128), jnp.bfloat16),
    ]
    return pl.pallas_call(
        functools.partial(correlate_kernel, chans, tpd, scale, masks, share),
        out_shape=outs if share else outs[0],
        in_specs=[pl.BlockSpec(memory_space=pltpu.SMEM)] + [vmem] * (len(pieces) + 3),
        out_specs=[vmem] * 2 if share else vmem,
        scratch_shapes=[
            pltpu.VMEM((chunks * tpd // ROWS, panel, depth), jnp.bfloat16),
            pltpu.VMEM((2 * height, depth), jnp.bfloat16),
            pltpu.VMEM((FOLD * panel, depth), jnp.bfloat16),
            pltpu.VMEM((2 * height, FOLD * panel), jnp.float32),
            pltpu.VMEM((2 * keep, FOLD * panel), jnp.float32),
        ],
        compiler_params=params(30),
        cost_estimate=pl.CostEstimate(flops=8 * 10**9, bytes_accessed=8 * 10**6, transcendentals=0),
        name="correlate",
    )(place, *pieces, *windows)


def swap(value, bit):
    size = lax.axis_size("tm")
    return lax.ppermute(value, "tm", [(i, i ^ bit) for i in range(size)])


def gather_panel(value, beside=None):
    bits = []
    while 2 << len(bits) < lax.axis_size("tm"):
        bits.append(2 << len(bits))
    rows = value.shape[0] // 2
    out = []
    for part_of, order in enumerate((bits[::-1], bits)):
        parts = [(value[part_of * rows : (part_of + 1) * rows][None], [0])]
        for bit in order:
            held = jnp.concatenate([v for v, _ in parts], axis=0) if len(parts) > 1 else parts[0][0]
            items = [m for _, ms in parts for m in ms]
            parts = [(held, items), (swap(held, bit), [m ^ bit for m in items])]
        out += [(v, part_of, ms) for v, ms in parts]
    if beside is not None:
        beside, *tied = lax.optimization_barrier((beside, *[v for v, _, _ in out]))
        out = [(v, n, ms) for v, (_, n, ms) in zip(tied, out)]
    return beside, out + [(swap(v, 1), part_of, [m ^ 1 for m in ms]) for v, part_of, ms in out]


def body(recording, spike_times, unit_labels, old_templates):
    sub_rows, chans = recording.shape
    panel, feat = old_templates.shape
    taps = feat // chans
    half = (taps - 1) // 2
    owners = lax.axis_size("unit")
    tm_count = lax.axis_size("tm")
    devices = owners * tm_count
    spikes = spike_times.shape[0]
    tm_pos = lax.axis_index("tm")
    unit_pos = lax.axis_index("unit")
    flat_pos = tm_pos * owners + unit_pos
    tpd = -(-taps // tm_count)
    padded = tpd * tm_count
    keep = sub_rows // ROWS
    scale = 1.0 / (float(feat) ** 0.5)

    base = (flat_pos * sub_rows + half).astype(jnp.int32).reshape(1)
    groups = padded // ROWS
    send = pack(spike_times, unit_labels, base, recording, taps, panel, owners, groups, ROWS)
    if tpd != ROWS:
        send = send.reshape(groups, owners, CAP, ROWS // tpd, tpd, chans)
        send = jnp.transpose(send, (0, 3, 1, 2, 4, 5))
    owner = unit_labels // panel
    hits = (owner[:, None] == jnp.arange(owners)[None, :]).astype(jnp.int32)
    rank = jnp.sum((jnp.cumsum(hits, axis=0) - hits) * hits, axis=1)
    placing = jnp.arange(owners * CAP)[:, None] == (owner * CAP + rank)[None, :]
    tags = jnp.sum(jnp.where(placing, (unit_labels % panel + 1)[None, :], 0), axis=1) - 1
    tags = jnp.broadcast_to(tags.reshape(1, owners, CAP), (tm_count, owners, CAP))
    tags = tags.reshape(devices, CAP)
    tags = lax.all_to_all(tags, AXES, split_axis=0, concat_axis=0, tiled=True)
    key = (tags[:, :, None] * tpd + jnp.arange(tpd)[None, None, :]).reshape(1, -1)
    send, key, before = lax.optimization_barrier((send, key, old_templates))
    got = lax.all_to_all(
        send.reshape(devices, CAP * tpd, chans), AXES, split_axis=0, concat_axis=0, tiled=True
    ).reshape(devices * CAP * tpd, chans)

    cube = before.reshape(panel, chans, taps)
    cube = jnp.pad(cube, ((0, 0), (0, 0), (0, padded - taps)))
    cube = lax.dynamic_slice_in_dim(cube, tm_pos * tpd, tpd, 2)
    old = jnp.transpose(cube, (0, 2, 1)).reshape(panel, tpd * chans)

    got, rest = lax.optimization_barrier((got, recording))
    head = rest[:padded]
    follow = lax.ppermute(head, AXES, [(i, i - 1) for i in range(1, devices)])
    skip = lax.ppermute(head, AXES, [(i, i - 2) for i in range(2, devices, 2)])
    pairs = [(i, i ^ 1) for i in range(owners)]
    first = sub_rows * 5 // 16 // (16 * ROWS) * (16 * ROWS)
    early = lax.ppermute(rest[:first], "unit", pairs)
    late = lax.ppermute(rest[first:], "unit", pairs)
    odd = unit_pos % 2

    fresh = refine(key, got, old, tpd)
    rest, fresh = lax.optimization_barrier((rest, fresh))
    mine = fold(rest)
    _, own = gather_panel(fresh)
    width = 2 * keep * FOLD

    found = []
    for m in range(1, owners // 2):
        ahead = [(i, (i + 2 * m) % owners) for i in range(owners)]
        back = [(j, i) for i, j in ahead]
        chunk = lax.ppermute(fresh, "unit", ahead)
        if m == 1:
            chunk, mine, early = lax.optimization_barrier((chunk, mine, early))
            late, other = gather_panel(chunk, late)
            windows = (mine, fold(early), fold(follow, late, jnp.where(odd == 1, head, skip)))
        else:
            _, other = gather_panel(chunk)
        place = jnp.stack([tm_pos, odd, 0 * odd]).astype(jnp.int32)
        out = correlate(place, other, windows, chans, tpd, scale, width, jnp.bfloat16)
        found.append((lax.ppermute(out, "unit", back), ((unit_pos + 2 * m) % owners) // 2))
    place = jnp.stack([tm_pos, odd, unit_pos // 2]).astype(jnp.int32)
    place, _ = lax.optimization_barrier((place, out))
    share = chans // tm_count
    scores, part = correlate(
        place, own, windows, chans, tpd, scale, owners // 2 * width, jnp.float32, share
    )
    for out, pair in found:
        scores = lax.dynamic_update_slice_in_dim(
            scores, out.astype(jnp.float32), pair * width, 1
        )
    part = jnp.transpose(part[:taps, :, :share], (1, 2, 0)).reshape(panel, share * taps)
    return (part, scores)


def solution(mesh):
    in_specs = (P(AXES, None), P(AXES), P(AXES), P("unit", None))
    out_specs = (P("unit", "tm"), P("unit", "tm"))
    return jax.shard_map(body, mesh=mesh, in_specs=in_specs, out_specs=out_specs, check_vma=False)
```

```python
import functools

import jax
import jax.numpy as jnp
from jax import lax
from jax.experimental import pallas as pl
from jax.experimental.pallas import tpu as pltpu
from jax.sharding import PartitionSpec as P

STRIDE = 2
CAP = 8
FOLD = 4
ROWS = STRIDE * FOLD
AXES = ("tm", "unit")
MIB = 1024 * 1024
NT = (((1,), (1,)), ((), ()))


def params(mib):
    return pltpu.CompilerParams(vmem_limit_bytes=mib * MIB)


def pack_kernel(
    taps, panel, owners, tm_count, tpd, times_ref, labels_ref, base_ref, rec_ref, send_ref, buf, cnt
):
    spikes = times_ref.shape[0]
    sub_rows = rec_ref.shape[0]
    padded = tm_count * tpd
    win = padded + 16
    base = base_ref[0]
    for o in range(owners):
        cnt[o] = 0
    if owners * CAP > spikes:
        buf[...] = jnp.zeros_like(buf)
    tap = lax.broadcasted_iota(jnp.int32, (padded, win), 0)
    col = lax.broadcasted_iota(jnp.int32, (padded, win), 1)
    gap = jnp.where(tap < taps, col - tap, -1)

    def one(s):
        first = times_ref[s] - base
        start = jnp.minimum((first // 16) * 16, sub_rows - win)
        owner = labels_ref[s] // panel
        slot = cnt[owner]
        cnt[owner] = slot + 1
        pick = (gap == first - start).astype(jnp.bfloat16)
        window = rec_ref[pl.ds(pl.multiple_of(start, 16), win), :]
        snip = jnp.dot(pick, window, preferred_element_type=jnp.float32)
        for t in range(tm_count):
            row = (t * owners + owner) * (CAP * tpd) + slot * tpd
            buf[pl.ds(pl.multiple_of(row, tpd), tpd), :] = snip[t * tpd : (t + 1) * tpd]

    def group(g, carry):
        for i in range(8):
            one(g * 8 + i)
        return carry

    lax.fori_loop(0, spikes // 8, group, 0)
    send_ref[...] = buf[...].astype(jnp.bfloat16)


def pack(times, labels, base, rec, taps, panel, owners, tm_count, tpd):
    chans = rec.shape[1]
    rows = owners * tm_count * CAP * tpd
    smem = pl.BlockSpec(memory_space=pltpu.SMEM)
    vmem = pl.BlockSpec(memory_space=pltpu.VMEM)
    return pl.pallas_call(
        functools.partial(pack_kernel, taps, panel, owners, tm_count, tpd),
        out_shape=jax.ShapeDtypeStruct((rows, chans), jnp.bfloat16),
        in_specs=[smem, smem, smem, vmem],
        out_specs=vmem,
        scratch_shapes=[
            pltpu.VMEM((rows, chans), jnp.float32),
            pltpu.SMEM((owners,), jnp.int32),
        ],
        compiler_params=params(24),
        cost_estimate=pl.CostEstimate(flops=10**8, bytes_accessed=4 * 10**6, transcendentals=0),
        name="pack",
    )(times, labels, base, rec)


def fold_kernel(*refs):
    out_ref = refs[-1]
    chans = refs[0].shape[1]
    block = 16 * ROWS
    new = lax.broadcasted_iota(jnp.int32, (block, block), 0)
    old = lax.broadcasted_iota(jnp.int32, (block, block), 1)
    perm = (old == (new % 16) * ROWS + new // 16).astype(jnp.bfloat16)
    at = 0
    for ref in refs[:-1]:
        for low in range(0, ref.shape[0], block):
            size = min(block, ref.shape[0] - low)
            part = jnp.dot(perm[:, :size], ref[low : low + size, :], preferred_element_type=jnp.float32)
            part = part.astype(jnp.bfloat16)
            for r in range(ROWS):
                out_ref[at : at + 16, r * chans : (r + 1) * chans] = part[r * 16 : (r + 1) * 16]
            at += 16


def fold(*parts):
    chans = parts[0].shape[1]
    blocks = sum(-(-p.shape[0] // (16 * ROWS)) for p in parts)
    vmem = pl.BlockSpec(memory_space=pltpu.VMEM)
    return pl.pallas_call(
        fold_kernel,
        out_shape=jax.ShapeDtypeStruct((blocks * 16, ROWS * chans), jnp.bfloat16),
        in_specs=[vmem] * len(parts),
        out_specs=vmem,
        compiler_params=params(14),
        cost_estimate=pl.CostEstimate(flops=2 * 10**8, bytes_accessed=4 * 10**6, transcendentals=0),
        name="fold",
    )(*parts)


def refine_kernel(tpd, key_ref, got_ref, old_ref, out_ref, sums):
    panel = old_ref.shape[0]
    rows, chans = got_ref.shape
    step = min(rows, 2048)
    count = jnp.zeros((panel, 1), jnp.float32)
    for b in range(rows // step):
        key = key_ref[:, b * step : (b + 1) * step]
        wanted = lax.broadcasted_iota(jnp.int32, (tpd * panel, step), 0)
        wanted = (wanted % panel) * tpd + wanted // panel
        hit = (wanted == key).astype(jnp.float32)
        count = count + jnp.sum(hit[:panel], axis=1, keepdims=True)
        part = jnp.dot(
            hit.astype(jnp.bfloat16),
            got_ref[b * step : (b + 1) * step, :],
            preferred_element_type=jnp.float32,
        )
        if b == 0:
            sums[...] = part
        else:
            sums[...] += part
    weight = count / (count + 4.0)
    most = jnp.maximum(count, 1.0)
    for t in range(tpd):
        base = old_ref[:, t * chans : (t + 1) * chans].astype(jnp.float32)
        mean = sums[t * panel : (t + 1) * panel, :] / most
        out_ref[:, t * chans : (t + 1) * chans] = (base + weight * (mean - base)).astype(jnp.bfloat16)


def refine(key, got, old, tpd):
    vmem = pl.BlockSpec(memory_space=pltpu.VMEM)
    panel = old.shape[0]
    return pl.pallas_call(
        functools.partial(refine_kernel, tpd),
        out_shape=jax.ShapeDtypeStruct(old.shape, jnp.bfloat16),
        in_specs=[vmem] * 3,
        out_specs=vmem,
        scratch_shapes=[pltpu.VMEM((tpd * panel, got.shape[1]), jnp.float32)],
        compiler_params=params(32),
        cost_estimate=pl.CostEstimate(flops=8 * 10**8, bytes_accessed=3 * 10**6, transcendentals=0),
        name="refine",
    )(key, got, old)


def extract_kernel(chans, tpd, share, masks, place_ref, *refs):
    pieces, out_ref = refs[:-1], refs[-1]
    half_rows = pieces[0].shape[1]
    wide = out_ref.shape[2]
    me = place_ref[0]
    channel = lax.broadcasted_iota(jnp.int32, (chans, wide), 0)
    lane = lax.broadcasted_iota(jnp.int32, (chans, wide), 1)
    pick = ((channel == me * share + lane) & (lane < share)).astype(jnp.bfloat16)
    for ref, (part_of, items) in zip(pieces, masks):
        rows = slice(part_of * half_rows, (part_of + 1) * half_rows)
        for at, mask in enumerate(items):
            first = jnp.bitwise_xor(me, mask) * tpd
            for t in range(tpd):
                taken = jnp.dot(
                    ref[at, :, t * chans : (t + 1) * chans], pick, preferred_element_type=jnp.float32
                )
                out_ref[first + t, rows, :] = taken.astype(jnp.bfloat16)


def extract(me, gathered, chans, tpd, share):
    pieces = [value for value, _, _ in gathered]
    masks = [(part_of, items) for _, part_of, items in gathered]
    taps = sum(len(items) for _, items in masks) // 2 * tpd
    vmem = pl.BlockSpec(memory_space=pltpu.VMEM)
    return pl.pallas_call(
        functools.partial(extract_kernel, chans, tpd, share, masks),
        out_shape=jax.ShapeDtypeStruct((taps, 2 * pieces[0].shape[1], -(-share // 128) * 128), jnp.bfloat16),
        in_specs=[pl.BlockSpec(memory_space=pltpu.SMEM)] + [vmem] * len(pieces),
        out_specs=vmem,
        compiler_params=params(14),
        cost_estimate=pl.CostEstimate(flops=4 * 10**8, bytes_accessed=4 * 10**6, transcendentals=0),
        name="extract",
    )(me, *pieces)


def correlate_kernel(chans, tpd, scale, masks, place_ref, *refs):
    count = len(masks)
    pieces, rest = refs[:count], refs[count:]
    mine_ref, early_ref, late_ref, out_ref, t_buf, e_buf, rhs, part, acc = rest
    half_rows = pieces[0].shape[1]
    lanes = tpd * chans
    blocks, panel, depth = t_buf.shape
    per = depth // lanes
    height = e_buf.shape[0] // 2
    keep = acc.shape[0] // 2
    shift = STRIDE * chans
    me, odd, pair = place_ref[0], place_ref[1], place_ref[2]
    early = early_ref.shape[0]
    e_buf[0:keep, :] = mine_ref[...]
    e_buf[keep:height, :] = late_ref[0 : height - keep, :]
    e_buf[height : height + early, :] = early_ref[...]
    e_buf[height + early :, :] = late_ref[height - keep :, :]
    for ref, (part_of, items) in zip(pieces, masks):
        rows = slice(part_of * half_rows, (part_of + 1) * half_rows)
        for at, mask in enumerate(items):
            chunk = jnp.bitwise_xor(me, mask)
            if per == 1:
                t_buf[chunk, rows, :] = ref[at]
            else:
                first = pl.multiple_of(chunk % per * lanes, 128)
                t_buf[chunk // per, rows, pl.ds(first, lanes)] = ref[at]
    for a in range(blocks + 1):
        used = depth if a < blocks else depth // 2
        for q in range(FOLD):
            rows = slice(q * panel, (q + 1) * panel)
            cut = q * shift
            low = min(cut, used)
            if low > 0:
                if a > 0:
                    rhs[rows, 0:low] = t_buf[a - 1, :, depth - cut : depth - cut + low]
                else:
                    rhs[rows, 0:low] = jnp.zeros((panel, low), jnp.bfloat16)
            if cut < used:
                if a < blocks:
                    rhs[rows, cut:used] = t_buf[a, :, 0 : used - cut]
                else:
                    rhs[rows, cut:used] = jnp.zeros((panel, used - cut), jnp.bfloat16)
        part[...] = lax.dot_general(
            e_buf[:, 0:used], rhs[:, 0:used], NT, preferred_element_type=jnp.float32
        )
        for h in range(2):
            found = part[h * height + a : h * height + a + keep, :]
            if a == 0:
                acc[h * keep : (h + 1) * keep, :] = found
            else:
                acc[h * keep : (h + 1) * keep, :] += found
    width = 128
    place = lax.broadcasted_iota(jnp.int32, (FOLD * width, FOLD * width), 0)
    lane = lax.broadcasted_iota(jnp.int32, (FOLD * width, FOLD * width), 1)
    weave = (lane == (place % width) * FOLD + place // width).astype(jnp.bfloat16)
    per_half = keep // width
    for h in range(2):
        side = odd if h == 0 else 1 - odd
        for b in range(per_half):
            first = h * keep + b * width
            turned = acc[first : first + width, :].T * scale
            row = jnp.concatenate([turned[q * panel : (q + 1) * panel] for q in range(FOLD)], axis=1)
            high = row.astype(jnp.bfloat16)
            found = jnp.dot(high, weave, preferred_element_type=jnp.float32)
            if out_ref.dtype == jnp.float32:
                rest = (row - high.astype(jnp.float32)).astype(jnp.bfloat16)
                found = found + jnp.dot(rest, weave, preferred_element_type=jnp.float32)
            at = ((2 * pair + side) * per_half + b) * (FOLD * width)
            at = pl.multiple_of(at, FOLD * width)
            out_ref[:, pl.ds(at, FOLD * width)] = found.astype(out_ref.dtype)


def correlate(place, gathered, windows, chans, tpd, scale, width, dtype):
    pieces = [value for value, _, _ in gathered]
    masks = [(part_of, items) for _, part_of, items in gathered]
    panel = 2 * pieces[0].shape[1]
    chunks = sum(len(items) for _, items in masks) // 2
    keep = windows[0].shape[0]
    height = keep + 16
    depth = ROWS * chans
    vmem = pl.BlockSpec(memory_space=pltpu.VMEM)
    return pl.pallas_call(
        functools.partial(correlate_kernel, chans, tpd, scale, masks),
        out_shape=jax.ShapeDtypeStruct((panel, width), dtype),
        in_specs=[pl.BlockSpec(memory_space=pltpu.SMEM)] + [vmem] * (len(pieces) + 3),
        out_specs=vmem,
        scratch_shapes=[
            pltpu.VMEM((chunks * tpd // ROWS, panel, depth), jnp.bfloat16),
            pltpu.VMEM((2 * height, depth), jnp.bfloat16),
            pltpu.VMEM((FOLD * panel, depth), jnp.bfloat16),
            pltpu.VMEM((2 * height, FOLD * panel), jnp.float32),
            pltpu.VMEM((2 * keep, FOLD * panel), jnp.float32),
        ],
        compiler_params=params(30),
        cost_estimate=pl.CostEstimate(flops=8 * 10**9, bytes_accessed=8 * 10**6, transcendentals=0),
        name="correlate",
    )(place, *pieces, *windows)


def swap(value, bit):
    size = lax.axis_size("tm")
    return lax.ppermute(value, "tm", [(i, i ^ bit) for i in range(size)])


def spread(value):
    bits = []
    while 2 << len(bits) < lax.axis_size("tm"):
        bits.append(2 << len(bits))
    rows = value.shape[0] // 2
    out = []
    for part_of, order in enumerate((bits[::-1], bits)):
        parts = [(value[part_of * rows : (part_of + 1) * rows][None], [0])]
        for bit in order:
            held = jnp.concatenate([v for v, _ in parts], axis=0) if len(parts) > 1 else parts[0][0]
            items = [m for _, ms in parts for m in ms]
            parts = [(held, items), (swap(held, bit), [m ^ bit for m in items])]
        out += [(v, part_of, ms) for v, ms in parts]
    return out


def across(parts):
    return parts + [(swap(v, 1), part_of, [m ^ 1 for m in ms]) for v, part_of, ms in parts]


def tie(parts, *beside):
    done = lax.optimization_barrier((*beside, *[v for v, _, _ in parts]))
    tied = [(v, n, ms) for v, (_, n, ms) in zip(done[len(beside) :], parts)]
    return tied, *done[: len(beside)]


def body(recording, spike_times, unit_labels, old_templates):
    sub_rows, chans = recording.shape
    panel, feat = old_templates.shape
    taps = feat // chans
    half = (taps - 1) // 2
    owners = lax.axis_size("unit")
    tm_count = lax.axis_size("tm")
    devices = owners * tm_count
    spikes = spike_times.shape[0]
    tm_pos = lax.axis_index("tm")
    unit_pos = lax.axis_index("unit")
    flat_pos = tm_pos * owners + unit_pos
    tpd = -(-taps // tm_count)
    padded = tpd * tm_count
    keep = sub_rows // ROWS
    scale = 1.0 / (float(feat) ** 0.5)

    base = (flat_pos * sub_rows + half).astype(jnp.int32).reshape(1)
    groups = padded // ROWS
    send = pack(spike_times, unit_labels, base, recording, taps, panel, owners, groups, ROWS)
    if tpd != ROWS:
        send = send.reshape(groups, owners, CAP, ROWS // tpd, tpd, chans)
        send = jnp.transpose(send, (0, 3, 1, 2, 4, 5))
    owner = unit_labels // panel
    hits = (owner[:, None] == jnp.arange(owners)[None, :]).astype(jnp.int32)
    rank = jnp.sum((jnp.cumsum(hits, axis=0) - hits) * hits, axis=1)
    placing = jnp.arange(owners * CAP)[:, None] == (owner * CAP + rank)[None, :]
    tags = jnp.sum(jnp.where(placing, (unit_labels % panel + 1)[None, :], 0), axis=1) - 1
    tags = jnp.broadcast_to(tags.reshape(1, owners, CAP), (tm_count, owners, CAP))
    tags = tags.reshape(devices, CAP)
    tags = lax.all_to_all(tags, AXES, split_axis=0, concat_axis=0, tiled=True)
    key = (tags[:, :, None] * tpd + jnp.arange(tpd)[None, None, :]).reshape(1, -1)
    send, key, before = lax.optimization_barrier((send, key, old_templates))
    got = lax.all_to_all(
        send.reshape(devices, CAP * tpd, chans), AXES, split_axis=0, concat_axis=0, tiled=True
    ).reshape(devices * CAP * tpd, chans)

    cube = before.reshape(panel, chans, taps)
    cube = jnp.pad(cube, ((0, 0), (0, 0), (0, padded - taps)))
    cube = lax.dynamic_slice_in_dim(cube, tm_pos * tpd, tpd, 2)
    old = jnp.transpose(cube, (0, 2, 1)).reshape(panel, tpd * chans)

    got, rest, old = lax.optimization_barrier((got, recording, old))
    head = rest[:padded]
    follow = lax.ppermute(head, AXES, [(i, i - 1) for i in range(1, devices)])
    skip = lax.ppermute(head, AXES, [(i, i - 2) for i in range(2, devices, 2)])
    pairs = [(i, i ^ 1) for i in range(owners)]
    first = sub_rows // 2 // (16 * ROWS) * (16 * ROWS)
    early = lax.ppermute(rest[:first], "unit", pairs)
    late = lax.ppermute(rest[first:], "unit", pairs)
    odd = unit_pos % 2

    fresh = refine(key, got, old, tpd)
    rest, fresh = lax.optimization_barrier((rest, fresh))
    mine = fold(rest)
    own = spread(fresh)
    share = chans // tm_count
    width = 2 * keep * FOLD

    found = []
    for m in range(1, owners // 2):
        ahead = [(i, (i + 2 * m) % owners) for i in range(owners)]
        back = [(j, i) for i, j in ahead]
        chunk = lax.ppermute(fresh, "unit", ahead)
        if m == 1:
            own, chunk, mine, early = tie(own, chunk, mine, early)
            own = across(own)
            part = extract(tm_pos.astype(jnp.int32).reshape(1), own, chans, tpd, share)
            part = jnp.transpose(part[:taps, :, :share], (1, 2, 0)).reshape(panel, share * taps)
            other, late, part = tie(spread(chunk), late, part)
            windows = (mine, fold(early), fold(follow, late, jnp.where(odd == 1, head, skip)))
        else:
            other = spread(chunk)
        other = across(other)
        place = jnp.stack([tm_pos, odd, 0 * odd]).astype(jnp.int32)
        out = correlate(place, other, windows, chans, tpd, scale, width, jnp.bfloat16)
        found.append((lax.ppermute(out, "unit", back), ((unit_pos + 2 * m) % owners) // 2))
    place = jnp.stack([tm_pos, odd, unit_pos // 2]).astype(jnp.int32)
    place, _ = lax.optimization_barrier((place, out))
    scores = correlate(place, own, windows, chans, tpd, scale, owners // 2 * width, jnp.float32)
    for out, pair in found:
        scores = lax.dynamic_update_slice_in_dim(
            scores, out.astype(jnp.float32), pair * width, 1
        )
    return (part, scores)


def solution(mesh):
    in_specs = (P(AXES, None), P(AXES), P(AXES), P("unit", None))
    out_specs = (P("unit", "tm"), P("unit", "tm"))
    return jax.shard_map(body, mesh=mesh, in_specs=in_specs, out_specs=out_specs, check_vma=False)
```

```python
import functools

import jax
import jax.numpy as jnp
from jax import lax
from jax.experimental import pallas as pl
from jax.experimental.pallas import tpu as pltpu
from jax.sharding import PartitionSpec as P

STRIDE = 2
CAP = 8
FOLD = 4
ROWS = STRIDE * FOLD
AXES = ("tm", "unit")
MIB = 1024 * 1024
NT = (((1,), (1,)), ((), ()))


def params(mib):
    return pltpu.CompilerParams(vmem_limit_bytes=mib * MIB)


def pack_kernel(
    taps, panel, owners, tm_count, tpd, times_ref, labels_ref, base_ref, rec_ref, send_ref, buf, cnt
):
    spikes = times_ref.shape[0]
    sub_rows = rec_ref.shape[0]
    padded = tm_count * tpd
    win = padded + 16
    base = base_ref[0]
    for o in range(owners):
        cnt[o] = 0
    if owners * CAP > spikes:
        buf[...] = jnp.zeros_like(buf)
    tap = lax.broadcasted_iota(jnp.int32, (padded, win), 0)
    col = lax.broadcasted_iota(jnp.int32, (padded, win), 1)
    gap = jnp.where(tap < taps, col - tap, -1)

    def one(s):
        first = times_ref[s] - base
        start = jnp.minimum((first // 16) * 16, sub_rows - win)
        owner = labels_ref[s] // panel
        slot = cnt[owner]
        cnt[owner] = slot + 1
        pick = (gap == first - start).astype(jnp.bfloat16)
        window = rec_ref[pl.ds(pl.multiple_of(start, 16), win), :]
        snip = jnp.dot(pick, window, preferred_element_type=jnp.float32)
        for t in range(tm_count):
            row = (t * owners + owner) * (CAP * tpd) + slot * tpd
            buf[pl.ds(pl.multiple_of(row, tpd), tpd), :] = snip[t * tpd : (t + 1) * tpd]

    def group(g, carry):
        for i in range(8):
            one(g * 8 + i)
        return carry

    lax.fori_loop(0, spikes // 8, group, 0)
    send_ref[...] = buf[...].astype(jnp.bfloat16)


def pack(times, labels, base, rec, taps, panel, owners, tm_count, tpd):
    chans = rec.shape[1]
    rows = owners * tm_count * CAP * tpd
    smem = pl.BlockSpec(memory_space=pltpu.SMEM)
    vmem = pl.BlockSpec(memory_space=pltpu.VMEM)
    return pl.pallas_call(
        functools.partial(pack_kernel, taps, panel, owners, tm_count, tpd),
        out_shape=jax.ShapeDtypeStruct((rows, chans), jnp.bfloat16),
        in_specs=[smem, smem, smem, vmem],
        out_specs=vmem,
        scratch_shapes=[
            pltpu.VMEM((rows, chans), jnp.float32),
            pltpu.SMEM((owners,), jnp.int32),
        ],
        compiler_params=params(24),
        cost_estimate=pl.CostEstimate(flops=10**8, bytes_accessed=4 * 10**6, transcendentals=0),
        name="pack",
    )(times, labels, base, rec)


def fold_kernel(*refs):
    out_ref = refs[-1]
    chans = refs[0].shape[1]
    block = 16 * ROWS
    new = lax.broadcasted_iota(jnp.int32, (block, block), 0)
    old = lax.broadcasted_iota(jnp.int32, (block, block), 1)
    perm = (old == (new % 16) * ROWS + new // 16).astype(jnp.bfloat16)
    at = 0
    for ref in refs[:-1]:
        for low in range(0, ref.shape[0], block):
            size = min(block, ref.shape[0] - low)
            part = jnp.dot(perm[:, :size], ref[low : low + size, :], preferred_element_type=jnp.float32)
            part = part.astype(jnp.bfloat16)
            for r in range(ROWS):
                out_ref[at : at + 16, r * chans : (r + 1) * chans] = part[r * 16 : (r + 1) * 16]
            at += 16


def fold(*parts):
    chans = parts[0].shape[1]
    blocks = sum(-(-p.shape[0] // (16 * ROWS)) for p in parts)
    vmem = pl.BlockSpec(memory_space=pltpu.VMEM)
    return pl.pallas_call(
        fold_kernel,
        out_shape=jax.ShapeDtypeStruct((blocks * 16, ROWS * chans), jnp.bfloat16),
        in_specs=[vmem] * len(parts),
        out_specs=vmem,
        compiler_params=params(14),
        cost_estimate=pl.CostEstimate(flops=2 * 10**8, bytes_accessed=4 * 10**6, transcendentals=0),
        name="fold",
    )(*parts)


def refine_kernel(tpd, key_ref, got_ref, old_ref, out_ref, sums):
    panel = old_ref.shape[0]
    rows, chans = got_ref.shape
    step = min(rows, 2048)
    count = jnp.zeros((panel, 1), jnp.float32)
    for b in range(rows // step):
        key = key_ref[:, b * step : (b + 1) * step]
        wanted = lax.broadcasted_iota(jnp.int32, (tpd * panel, step), 0)
        wanted = (wanted % panel) * tpd + wanted // panel
        hit = (wanted == key).astype(jnp.float32)
        count = count + jnp.sum(hit[:panel], axis=1, keepdims=True)
        part = jnp.dot(
            hit.astype(jnp.bfloat16),
            got_ref[b * step : (b + 1) * step, :],
            preferred_element_type=jnp.float32,
        )
        if b == 0:
            sums[...] = part
        else:
            sums[...] += part
    weight = count / (count + 4.0)
    most = jnp.maximum(count, 1.0)
    for t in range(tpd):
        base = old_ref[:, t * chans : (t + 1) * chans].astype(jnp.float32)
        mean = sums[t * panel : (t + 1) * panel, :] / most
        out_ref[:, t * chans : (t + 1) * chans] = (base + weight * (mean - base)).astype(jnp.bfloat16)


def refine(key, got, old, tpd):
    vmem = pl.BlockSpec(memory_space=pltpu.VMEM)
    panel = old.shape[0]
    return pl.pallas_call(
        functools.partial(refine_kernel, tpd),
        out_shape=jax.ShapeDtypeStruct(old.shape, jnp.bfloat16),
        in_specs=[vmem] * 3,
        out_specs=vmem,
        scratch_shapes=[pltpu.VMEM((tpd * panel, got.shape[1]), jnp.float32)],
        compiler_params=params(32),
        cost_estimate=pl.CostEstimate(flops=8 * 10**8, bytes_accessed=3 * 10**6, transcendentals=0),
        name="refine",
    )(key, got, old)


def extract_kernel(chans, tpd, share, masks, place_ref, *refs):
    pieces, out_ref = refs[:-1], refs[-1]
    half_rows = pieces[0].shape[1]
    wide = out_ref.shape[2]
    me = place_ref[0]
    channel = lax.broadcasted_iota(jnp.int32, (chans, wide), 0)
    lane = lax.broadcasted_iota(jnp.int32, (chans, wide), 1)
    pick = ((channel == me * share + lane) & (lane < share)).astype(jnp.bfloat16)
    for ref, (part_of, items) in zip(pieces, masks):
        rows = slice(part_of * half_rows, (part_of + 1) * half_rows)
        for at, mask in enumerate(items):
            first = jnp.bitwise_xor(me, mask) * tpd
            for t in range(tpd):
                taken = jnp.dot(
                    ref[at, :, t * chans : (t + 1) * chans], pick, preferred_element_type=jnp.float32
                )
                out_ref[first + t, rows, :] = taken.astype(jnp.bfloat16)


def extract(me, gathered, chans, tpd, share):
    pieces = [value for value, _, _ in gathered]
    masks = [(part_of, items) for _, part_of, items in gathered]
    taps = sum(len(items) for _, items in masks) // 2 * tpd
    vmem = pl.BlockSpec(memory_space=pltpu.VMEM)
    return pl.pallas_call(
        functools.partial(extract_kernel, chans, tpd, share, masks),
        out_shape=jax.ShapeDtypeStruct((taps, 2 * pieces[0].shape[1], -(-share // 128) * 128), jnp.bfloat16),
        in_specs=[pl.BlockSpec(memory_space=pltpu.SMEM)] + [vmem] * len(pieces),
        out_specs=vmem,
        compiler_params=params(14),
        cost_estimate=pl.CostEstimate(flops=4 * 10**8, bytes_accessed=4 * 10**6, transcendentals=0),
        name="extract",
    )(me, *pieces)


def correlate_kernel(chans, tpd, scale, masks, place_ref, *refs):
    count = len(masks)
    pieces, rest = refs[:count], refs[count:]
    mine_ref, early_ref, late_ref, out_ref, t_buf, e_buf, rhs, part, acc = rest
    half_rows = pieces[0].shape[1]
    lanes = tpd * chans
    blocks, panel, depth = t_buf.shape
    per = depth // lanes
    height = e_buf.shape[0] // 2
    keep = acc.shape[0] // 2
    shift = STRIDE * chans
    me, odd, pair = place_ref[0], place_ref[1], place_ref[2]
    early = early_ref.shape[0]
    e_buf[0:keep, :] = mine_ref[...]
    e_buf[keep:height, :] = late_ref[0 : height - keep, :]
    e_buf[height : height + early, :] = early_ref[...]
    e_buf[height + early :, :] = late_ref[height - keep :, :]
    for ref, (part_of, items) in zip(pieces, masks):
        rows = slice(part_of * half_rows, (part_of + 1) * half_rows)
        for at, mask in enumerate(items):
            chunk = jnp.bitwise_xor(me, mask)
            if per == 1:
                t_buf[chunk, rows, :] = ref[at]
            else:
                first = pl.multiple_of(chunk % per * lanes, 128)
                t_buf[chunk // per, rows, pl.ds(first, lanes)] = ref[at]
    for a in range(blocks + 1):
        used = depth if a < blocks else depth // 2
        for q in range(FOLD):
            rows = slice(q * panel, (q + 1) * panel)
            cut = q * shift
            low = min(cut, used)
            if low > 0:
                if a > 0:
                    rhs[rows, 0:low] = t_buf[a - 1, :, depth - cut : depth - cut + low]
                else:
                    rhs[rows, 0:low] = jnp.zeros((panel, low), jnp.bfloat16)
            if cut < used:
                if a < blocks:
                    rhs[rows, cut:used] = t_buf[a, :, 0 : used - cut]
                else:
                    rhs[rows, cut:used] = jnp.zeros((panel, used - cut), jnp.bfloat16)
        part[...] = lax.dot_general(
            e_buf[:, 0:used], rhs[:, 0:used], NT, preferred_element_type=jnp.float32
        )
        for h in range(2):
            found = part[h * height + a : h * height + a + keep, :]
            if a == 0:
                acc[h * keep : (h + 1) * keep, :] = found
            else:
                acc[h * keep : (h + 1) * keep, :] += found
    width = 128
    place = lax.broadcasted_iota(jnp.int32, (FOLD * width, FOLD * width), 0)
    lane = lax.broadcasted_iota(jnp.int32, (FOLD * width, FOLD * width), 1)
    weave = (lane == (place % width) * FOLD + place // width).astype(jnp.bfloat16)
    per_half = keep // width
    for h in range(2):
        side = odd if h == 0 else 1 - odd
        for b in range(per_half):
            first = h * keep + b * width
            turned = acc[first : first + width, :].T * scale
            row = jnp.concatenate([turned[q * panel : (q + 1) * panel] for q in range(FOLD)], axis=1)
            high = row.astype(jnp.bfloat16)
            found = jnp.dot(high, weave, preferred_element_type=jnp.float32)
            if out_ref.dtype == jnp.float32:
                rest = (row - high.astype(jnp.float32)).astype(jnp.bfloat16)
                found = found + jnp.dot(rest, weave, preferred_element_type=jnp.float32)
            at = ((2 * pair + side) * per_half + b) * (FOLD * width)
            at = pl.multiple_of(at, FOLD * width)
            out_ref[:, pl.ds(at, FOLD * width)] = found.astype(out_ref.dtype)


def correlate(place, gathered, windows, chans, tpd, scale, width, dtype):
    pieces = [value for value, _, _ in gathered]
    masks = [(part_of, items) for _, part_of, items in gathered]
    panel = 2 * pieces[0].shape[1]
    chunks = sum(len(items) for _, items in masks) // 2
    keep = windows[0].shape[0]
    height = keep + 16
    depth = ROWS * chans
    vmem = pl.BlockSpec(memory_space=pltpu.VMEM)
    return pl.pallas_call(
        functools.partial(correlate_kernel, chans, tpd, scale, masks),
        out_shape=jax.ShapeDtypeStruct((panel, width), dtype),
        in_specs=[pl.BlockSpec(memory_space=pltpu.SMEM)] + [vmem] * (len(pieces) + 3),
        out_specs=vmem,
        scratch_shapes=[
            pltpu.VMEM((chunks * tpd // ROWS, panel, depth), jnp.bfloat16),
            pltpu.VMEM((2 * height, depth), jnp.bfloat16),
            pltpu.VMEM((FOLD * panel, depth), jnp.bfloat16),
            pltpu.VMEM((2 * height, FOLD * panel), jnp.float32),
            pltpu.VMEM((2 * keep, FOLD * panel), jnp.float32),
        ],
        compiler_params=params(30),
        cost_estimate=pl.CostEstimate(flops=8 * 10**9, bytes_accessed=8 * 10**6, transcendentals=0),
        name="correlate",
    )(place, *pieces, *windows)


def swap(value, bit):
    size = lax.axis_size("tm")
    return lax.ppermute(value, "tm", [(i, i ^ bit) for i in range(size)])


def spread(value):
    bits = []
    while 2 << len(bits) < lax.axis_size("tm"):
        bits.append(2 << len(bits))
    rows = value.shape[0] // 2
    out = []
    for part_of, order in enumerate((bits[::-1], bits)):
        parts = [(value[part_of * rows : (part_of + 1) * rows][None], [0])]
        for bit in order:
            held = jnp.concatenate([v for v, _ in parts], axis=0) if len(parts) > 1 else parts[0][0]
            items = [m for _, ms in parts for m in ms]
            parts = [(held, items), (swap(held, bit), [m ^ bit for m in items])]
        out += [(v, part_of, ms) for v, ms in parts]
    return out


def across(parts):
    return parts + [(swap(v, 1), part_of, [m ^ 1 for m in ms]) for v, part_of, ms in parts]


def tie(parts, *beside):
    done = lax.optimization_barrier((*beside, *[v for v, _, _ in parts]))
    tied = [(v, n, ms) for v, (_, n, ms) in zip(done[len(beside) :], parts)]
    return tied, *done[: len(beside)]


def body(recording, spike_times, unit_labels, old_templates):
    sub_rows, chans = recording.shape
    panel, feat = old_templates.shape
    taps = feat // chans
    half = (taps - 1) // 2
    owners = lax.axis_size("unit")
    tm_count = lax.axis_size("tm")
    devices = owners * tm_count
    spikes = spike_times.shape[0]
    tm_pos = lax.axis_index("tm")
    unit_pos = lax.axis_index("unit")
    flat_pos = tm_pos * owners + unit_pos
    tpd = -(-taps // tm_count)
    padded = tpd * tm_count
    keep = sub_rows // ROWS
    scale = 1.0 / (float(feat) ** 0.5)

    base = (flat_pos * sub_rows + half).astype(jnp.int32).reshape(1)
    groups = padded // ROWS
    send = pack(spike_times, unit_labels, base, recording, taps, panel, owners, groups, ROWS)
    if tpd != ROWS:
        send = send.reshape(groups, owners, CAP, ROWS // tpd, tpd, chans)
        send = jnp.transpose(send, (0, 3, 1, 2, 4, 5))
    owner = unit_labels // panel
    hits = (owner[:, None] == jnp.arange(owners)[None, :]).astype(jnp.int32)
    rank = jnp.sum((jnp.cumsum(hits, axis=0) - hits) * hits, axis=1)
    placing = jnp.arange(owners * CAP)[:, None] == (owner * CAP + rank)[None, :]
    tags = jnp.sum(jnp.where(placing, (unit_labels % panel + 1)[None, :], 0), axis=1) - 1
    tags = jnp.broadcast_to(tags.reshape(1, owners, CAP), (tm_count, owners, CAP))
    tags = tags.reshape(devices, CAP)
    tags = lax.all_to_all(tags, AXES, split_axis=0, concat_axis=0, tiled=True)
    key = (tags[:, :, None] * tpd + jnp.arange(tpd)[None, None, :]).reshape(1, -1)
    send, key, before, ahead_rows = lax.optimization_barrier((send, key, old_templates, recording))
    pairs = [(i, i ^ 1) for i in range(owners)]
    unit_rows = 16 * ROWS
    cuts = [0, *(sub_rows * n // 16 // unit_rows * unit_rows for n in (4, 9)), sub_rows]
    ahead_rows = lax.ppermute(ahead_rows[: cuts[1]], "unit", pairs)
    got = lax.all_to_all(
        send.reshape(devices, CAP * tpd, chans), AXES, split_axis=0, concat_axis=0, tiled=True
    ).reshape(devices * CAP * tpd, chans)

    cube = before.reshape(panel, chans, taps)
    cube = jnp.pad(cube, ((0, 0), (0, 0), (0, padded - taps)))
    cube = lax.dynamic_slice_in_dim(cube, tm_pos * tpd, tpd, 2)
    old = jnp.transpose(cube, (0, 2, 1)).reshape(panel, tpd * chans)

    got, rest, old, ahead_rows = lax.optimization_barrier((got, recording, old, ahead_rows))
    head = rest[:padded]
    follow = lax.ppermute(head, AXES, [(i, i - 1) for i in range(1, devices)])
    skip = lax.ppermute(head, AXES, [(i, i - 2) for i in range(2, devices, 2)])
    early = lax.ppermute(rest[cuts[1] : cuts[2]], "unit", pairs)
    late = lax.ppermute(rest[cuts[2] :], "unit", pairs)
    odd = unit_pos % 2

    fresh = refine(key, got, old, tpd)
    rest, fresh = lax.optimization_barrier((rest, fresh))
    mine = fold(rest)
    own = spread(fresh)
    share = chans // tm_count
    width = 2 * keep * FOLD

    found = []
    for m in range(1, owners // 2):
        ahead = [(i, (i + 2 * m) % owners) for i in range(owners)]
        back = [(j, i) for i, j in ahead]
        chunk = lax.ppermute(fresh, "unit", ahead)
        if m == 1:
            own, chunk, mine, early, follow, skip = tie(own, chunk, mine, early, follow, skip)
            own = across(own)
            part = extract(tm_pos.astype(jnp.int32).reshape(1), own, chans, tpd, share)
            part = jnp.transpose(part[:taps, :, :share], (1, 2, 0)).reshape(panel, share * taps)
            other, late, part = tie(spread(chunk), late, part)
            windows = (mine, fold(ahead_rows, early), fold(follow, late, jnp.where(odd == 1, head, skip)))
        else:
            other = spread(chunk)
        other = across(other)
        place = jnp.stack([tm_pos, odd, 0 * odd]).astype(jnp.int32)
        out = correlate(place, other, windows, chans, tpd, scale, width, jnp.bfloat16)
        found.append((lax.ppermute(out, "unit", back), ((unit_pos + 2 * m) % owners) // 2))
    place = jnp.stack([tm_pos, odd, unit_pos // 2]).astype(jnp.int32)
    place, _ = lax.optimization_barrier((place, out))
    scores = correlate(place, own, windows, chans, tpd, scale, owners // 2 * width, jnp.float32)
    for out, pair in found:
        scores = lax.dynamic_update_slice_in_dim(
            scores, out.astype(jnp.float32), pair * width, 1
        )
    return (part, scores)


def solution(mesh):
    in_specs = (P(AXES, None), P(AXES), P(AXES), P("unit", None))
    out_specs = (P("unit", "tm"), P("unit", "tm"))
    return jax.shard_map(body, mesh=mesh, in_specs=in_specs, out_specs=out_specs, check_vma=False)
```

```python
import functools

import jax
import jax.numpy as jnp
from jax import lax
from jax.experimental import pallas as pl
from jax.experimental.pallas import tpu as pltpu
from jax.sharding import PartitionSpec as P

STRIDE = 2
CAP = 8
FOLD = 4
ROWS = STRIDE * FOLD
AXES = ("tm", "unit")
MIB = 1024 * 1024
NT = (((1,), (1,)), ((), ()))


def params(mib):
    return pltpu.CompilerParams(vmem_limit_bytes=mib * MIB)


def pack_kernel(
    taps, panel, owners, tm_count, tpd, times_ref, labels_ref, base_ref, rec_ref, send_ref, buf, cnt
):
    spikes = times_ref.shape[0]
    sub_rows = rec_ref.shape[0]
    padded = tm_count * tpd
    win = padded + 16
    base = base_ref[0]
    for o in range(owners):
        cnt[o] = 0
    if owners * CAP > spikes:
        buf[...] = jnp.zeros_like(buf)
    tap = lax.broadcasted_iota(jnp.int32, (padded, win), 0)
    col = lax.broadcasted_iota(jnp.int32, (padded, win), 1)
    gap = jnp.where(tap < taps, col - tap, -1)

    def one(s):
        first = times_ref[s] - base
        start = jnp.minimum((first // 16) * 16, sub_rows - win)
        owner = labels_ref[s] // panel
        slot = cnt[owner]
        cnt[owner] = slot + 1
        pick = (gap == first - start).astype(jnp.bfloat16)
        window = rec_ref[pl.ds(pl.multiple_of(start, 16), win), :]
        snip = jnp.dot(pick, window, preferred_element_type=jnp.float32)
        for t in range(tm_count):
            row = (t * owners + owner) * (CAP * tpd) + slot * tpd
            buf[pl.ds(pl.multiple_of(row, tpd), tpd), :] = snip[t * tpd : (t + 1) * tpd]

    def group(g, carry):
        for i in range(8):
            one(g * 8 + i)
        return carry

    lax.fori_loop(0, spikes // 8, group, 0)
    send_ref[...] = buf[...].astype(jnp.bfloat16)


def pack(times, labels, base, rec, taps, panel, owners, tm_count, tpd):
    chans = rec.shape[1]
    rows = owners * tm_count * CAP * tpd
    smem = pl.BlockSpec(memory_space=pltpu.SMEM)
    vmem = pl.BlockSpec(memory_space=pltpu.VMEM)
    return pl.pallas_call(
        functools.partial(pack_kernel, taps, panel, owners, tm_count, tpd),
        out_shape=jax.ShapeDtypeStruct((rows, chans), jnp.bfloat16),
        in_specs=[smem, smem, smem, vmem],
        out_specs=vmem,
        scratch_shapes=[
            pltpu.VMEM((rows, chans), jnp.float32),
            pltpu.SMEM((owners,), jnp.int32),
        ],
        compiler_params=params(16),
        cost_estimate=pl.CostEstimate(flops=10**8, bytes_accessed=4 * 10**6, transcendentals=0),
        name="pack",
    )(times, labels, base, rec)


def fold_kernel(*refs):
    out_ref = refs[-1]
    chans = refs[0].shape[1]
    block = 16 * ROWS
    new = lax.broadcasted_iota(jnp.int32, (block, block), 0)
    old = lax.broadcasted_iota(jnp.int32, (block, block), 1)
    perm = (old == (new % 16) * ROWS + new // 16).astype(jnp.bfloat16)
    at = 0
    for ref in refs[:-1]:
        for low in range(0, ref.shape[0], block):
            size = min(block, ref.shape[0] - low)
            part = jnp.dot(perm[:, :size], ref[low : low + size, :], preferred_element_type=jnp.float32)
            part = part.astype(jnp.bfloat16)
            for r in range(ROWS):
                out_ref[at : at + 16, r * chans : (r + 1) * chans] = part[r * 16 : (r + 1) * 16]
            at += 16


def fold(*parts):
    chans = parts[0].shape[1]
    blocks = sum(-(-p.shape[0] // (16 * ROWS)) for p in parts)
    vmem = pl.BlockSpec(memory_space=pltpu.VMEM)
    return pl.pallas_call(
        fold_kernel,
        out_shape=jax.ShapeDtypeStruct((blocks * 16, ROWS * chans), jnp.bfloat16),
        in_specs=[vmem] * len(parts),
        out_specs=vmem,
        compiler_params=params(14),
        cost_estimate=pl.CostEstimate(flops=2 * 10**8, bytes_accessed=4 * 10**6, transcendentals=0),
        name="fold",
    )(*parts)


def refine_kernel(tpd, key_ref, got_ref, old_ref, out_ref, sums):
    panel = old_ref.shape[0]
    rows, chans = got_ref.shape
    step = min(rows, 2048)
    count = jnp.zeros((panel, 1), jnp.float32)
    for b in range(rows // step):
        key = key_ref[:, b * step : (b + 1) * step]
        wanted = lax.broadcasted_iota(jnp.int32, (tpd * panel, step), 0)
        wanted = (wanted % panel) * tpd + wanted // panel
        hit = (wanted == key).astype(jnp.float32)
        count = count + jnp.sum(hit[:panel], axis=1, keepdims=True)
        part = jnp.dot(
            hit.astype(jnp.bfloat16),
            got_ref[b * step : (b + 1) * step, :],
            preferred_element_type=jnp.float32,
        )
        if b == 0:
            sums[...] = part
        else:
            sums[...] += part
    weight = count / (count + 4.0)
    most = jnp.maximum(count, 1.0)
    for t in range(tpd):
        base = old_ref[:, t * chans : (t + 1) * chans].astype(jnp.float32)
        mean = sums[t * panel : (t + 1) * panel, :] / most
        out_ref[:, t * chans : (t + 1) * chans] = (base + weight * (mean - base)).astype(jnp.bfloat16)


def refine(key, got, old, tpd):
    vmem = pl.BlockSpec(memory_space=pltpu.VMEM)
    panel = old.shape[0]
    return pl.pallas_call(
        functools.partial(refine_kernel, tpd),
        out_shape=jax.ShapeDtypeStruct(old.shape, jnp.bfloat16),
        in_specs=[vmem] * 3,
        out_specs=vmem,
        scratch_shapes=[pltpu.VMEM((tpd * panel, got.shape[1]), jnp.float32)],
        compiler_params=params(20),
        cost_estimate=pl.CostEstimate(flops=8 * 10**8, bytes_accessed=3 * 10**6, transcendentals=0),
        name="refine",
    )(key, got, old)


def extract_kernel(chans, tpd, share, masks, place_ref, *refs):
    pieces, out_ref = refs[:-1], refs[-1]
    half_rows = pieces[0].shape[1]
    wide = out_ref.shape[2]
    me = place_ref[0]
    channel = lax.broadcasted_iota(jnp.int32, (chans, wide), 0)
    lane = lax.broadcasted_iota(jnp.int32, (chans, wide), 1)
    pick = ((channel == me * share + lane) & (lane < share)).astype(jnp.bfloat16)
    for ref, (part_of, items) in zip(pieces, masks):
        rows = slice(part_of * half_rows, (part_of + 1) * half_rows)
        for at, mask in enumerate(items):
            first = jnp.bitwise_xor(me, mask) * tpd
            for t in range(tpd):
                taken = jnp.dot(
                    ref[at, :, t * chans : (t + 1) * chans], pick, preferred_element_type=jnp.float32
                )
                out_ref[first + t, rows, :] = taken.astype(jnp.bfloat16)


def extract(me, gathered, chans, tpd, share):
    pieces = [value for value, _, _ in gathered]
    masks = [(part_of, items) for _, part_of, items in gathered]
    taps = sum(len(items) for _, items in masks) // 2 * tpd
    vmem = pl.BlockSpec(memory_space=pltpu.VMEM)
    return pl.pallas_call(
        functools.partial(extract_kernel, chans, tpd, share, masks),
        out_shape=jax.ShapeDtypeStruct((taps, 2 * pieces[0].shape[1], -(-share // 128) * 128), jnp.bfloat16),
        in_specs=[pl.BlockSpec(memory_space=pltpu.SMEM)] + [vmem] * len(pieces),
        out_specs=vmem,
        compiler_params=params(14),
        cost_estimate=pl.CostEstimate(flops=4 * 10**8, bytes_accessed=4 * 10**6, transcendentals=0),
        name="extract",
    )(me, *pieces)


def correlate_kernel(chans, tpd, scale, masks, place_ref, *refs):
    count = len(masks)
    pieces, rest = refs[:count], refs[count:]
    mine_ref, early_ref, late_ref, out_ref, t_buf, e_buf, rhs, part, acc = rest
    half_rows = pieces[0].shape[1]
    lanes = tpd * chans
    blocks, panel, depth = t_buf.shape
    per = depth // lanes
    height = e_buf.shape[0] // 2
    keep = acc.shape[0] // 2
    shift = STRIDE * chans
    me, odd, pair = place_ref[0], place_ref[1], place_ref[2]
    early = early_ref.shape[0]
    e_buf[0:keep, :] = mine_ref[...]
    e_buf[keep:height, :] = late_ref[0 : height - keep, :]
    e_buf[height : height + early, :] = early_ref[...]
    e_buf[height + early :, :] = late_ref[height - keep :, :]
    for ref, (part_of, items) in zip(pieces, masks):
        rows = slice(part_of * half_rows, (part_of + 1) * half_rows)
        for at, mask in enumerate(items):
            chunk = jnp.bitwise_xor(me, mask)
            if per == 1:
                t_buf[chunk, rows, :] = ref[at]
            else:
                first = pl.multiple_of(chunk % per * lanes, 128)
                t_buf[chunk // per, rows, pl.ds(first, lanes)] = ref[at]
    for a in range(blocks + 1):
        used = depth if a < blocks else depth // 2
        for q in range(FOLD):
            rows = slice(q * panel, (q + 1) * panel)
            cut = q * shift
            low = min(cut, used)
            if low > 0:
                if a > 0:
                    rhs[rows, 0:low] = t_buf[a - 1, :, depth - cut : depth - cut + low]
                else:
                    rhs[rows, 0:low] = jnp.zeros((panel, low), jnp.bfloat16)
            if cut < used:
                if a < blocks:
                    rhs[rows, cut:used] = t_buf[a, :, 0 : used - cut]
                else:
                    rhs[rows, cut:used] = jnp.zeros((panel, used - cut), jnp.bfloat16)
        part[...] = lax.dot_general(
            e_buf[:, 0:used], rhs[:, 0:used], NT, preferred_element_type=jnp.float32
        )
        for h in range(2):
            found = part[h * height + a : h * height + a + keep, :]
            if a == 0:
                acc[h * keep : (h + 1) * keep, :] = found
            else:
                acc[h * keep : (h + 1) * keep, :] += found
    width = 128
    place = lax.broadcasted_iota(jnp.int32, (FOLD * width, FOLD * width), 0)
    lane = lax.broadcasted_iota(jnp.int32, (FOLD * width, FOLD * width), 1)
    weave = (lane == (place % width) * FOLD + place // width).astype(jnp.bfloat16)
    per_half = keep // width
    for h in range(2):
        side = odd if h == 0 else 1 - odd
        for b in range(per_half):
            first = h * keep + b * width
            turned = acc[first : first + width, :].T * scale
            row = jnp.concatenate([turned[q * panel : (q + 1) * panel] for q in range(FOLD)], axis=1)
            high = row.astype(jnp.bfloat16)
            found = jnp.dot(high, weave, preferred_element_type=jnp.float32)
            if out_ref.dtype == jnp.float32:
                rest = (row - high.astype(jnp.float32)).astype(jnp.bfloat16)
                found = found + jnp.dot(rest, weave, preferred_element_type=jnp.float32)
            at = ((2 * pair + side) * per_half + b) * (FOLD * width)
            at = pl.multiple_of(at, FOLD * width)
            out_ref[:, pl.ds(at, FOLD * width)] = found.astype(out_ref.dtype)


def correlate(place, gathered, windows, chans, tpd, scale, width, dtype):
    pieces = [value for value, _, _ in gathered]
    masks = [(part_of, items) for _, part_of, items in gathered]
    panel = 2 * pieces[0].shape[1]
    chunks = sum(len(items) for _, items in masks) // 2
    keep = windows[0].shape[0]
    height = keep + 16
    depth = ROWS * chans
    vmem = pl.BlockSpec(memory_space=pltpu.VMEM)
    return pl.pallas_call(
        functools.partial(correlate_kernel, chans, tpd, scale, masks),
        out_shape=jax.ShapeDtypeStruct((panel, width), dtype),
        in_specs=[pl.BlockSpec(memory_space=pltpu.SMEM)] + [vmem] * (len(pieces) + 3),
        out_specs=vmem,
        scratch_shapes=[
            pltpu.VMEM((chunks * tpd // ROWS, panel, depth), jnp.bfloat16),
            pltpu.VMEM((2 * height, depth), jnp.bfloat16),
            pltpu.VMEM((FOLD * panel, depth), jnp.bfloat16),
            pltpu.VMEM((2 * height, FOLD * panel), jnp.float32),
            pltpu.VMEM((2 * keep, FOLD * panel), jnp.float32),
        ],
        compiler_params=params(22),
        cost_estimate=pl.CostEstimate(flops=8 * 10**9, bytes_accessed=8 * 10**6, transcendentals=0),
        name="correlate",
    )(place, *pieces, *windows)


def swap(value, bit):
    size = lax.axis_size("tm")
    return lax.ppermute(value, "tm", [(i, i ^ bit) for i in range(size)])


def spread(value):
    bits = []
    while 2 << len(bits) < lax.axis_size("tm"):
        bits.append(2 << len(bits))
    rows = value.shape[0] // 2
    out = []
    for part_of, order in enumerate((bits[::-1], bits)):
        parts = [(value[part_of * rows : (part_of + 1) * rows][None], [0])]
        for bit in order:
            held = jnp.concatenate([v for v, _ in parts], axis=0) if len(parts) > 1 else parts[0][0]
            items = [m for _, ms in parts for m in ms]
            parts = [(held, items), (swap(held, bit), [m ^ bit for m in items])]
        out += [(v, part_of, ms) for v, ms in parts]
    return out


def across(parts):
    return parts + [(swap(v, 1), part_of, [m ^ 1 for m in ms]) for v, part_of, ms in parts]


def tie(parts, *beside):
    done = lax.optimization_barrier((*beside, *[v for v, _, _ in parts]))
    tied = [(v, n, ms) for v, (_, n, ms) in zip(done[len(beside) :], parts)]
    return tied, *done[: len(beside)]


def body(recording, spike_times, unit_labels, old_templates):
    sub_rows, chans = recording.shape
    panel, feat = old_templates.shape
    taps = feat // chans
    half = (taps - 1) // 2
    owners = lax.axis_size("unit")
    tm_count = lax.axis_size("tm")
    devices = owners * tm_count
    spikes = spike_times.shape[0]
    tm_pos = lax.axis_index("tm")
    unit_pos = lax.axis_index("unit")
    flat_pos = tm_pos * owners + unit_pos
    tpd = -(-taps // tm_count)
    padded = tpd * tm_count
    keep = sub_rows // ROWS
    scale = 1.0 / (float(feat) ** 0.5)

    base = (flat_pos * sub_rows + half).astype(jnp.int32).reshape(1)
    groups = padded // ROWS
    send = pack(spike_times, unit_labels, base, recording, taps, panel, owners, groups, ROWS)
    if tpd != ROWS:
        send = send.reshape(groups, owners, CAP, ROWS // tpd, tpd, chans)
        send = jnp.transpose(send, (0, 3, 1, 2, 4, 5))
    owner = unit_labels // panel
    hits = (owner[:, None] == jnp.arange(owners)[None, :]).astype(jnp.int32)
    rank = jnp.sum((jnp.cumsum(hits, axis=0) - hits) * hits, axis=1)
    placing = jnp.arange(owners * CAP)[:, None] == (owner * CAP + rank)[None, :]
    tags = jnp.sum(jnp.where(placing, (unit_labels % panel + 1)[None, :], 0), axis=1) - 1
    tags = jnp.broadcast_to(tags.reshape(1, owners, CAP), (tm_count, owners, CAP))
    tags = tags.reshape(devices, CAP)
    tags = lax.all_to_all(tags, AXES, split_axis=0, concat_axis=0, tiled=True)
    key = (tags[:, :, None] * tpd + jnp.arange(tpd)[None, None, :]).reshape(1, -1)
    send, key, before, ahead_rows = lax.optimization_barrier((send, key, old_templates, recording))
    pairs = [(i, i ^ 1) for i in range(owners)]
    unit_rows = 16 * ROWS
    cuts = [0, *(sub_rows * n // 16 // unit_rows * unit_rows for n in (4, 9)), sub_rows]
    ahead_rows = lax.ppermute(ahead_rows[: cuts[1]], "unit", pairs)
    got = lax.all_to_all(
        send.reshape(devices, CAP * tpd, chans), AXES, split_axis=0, concat_axis=0, tiled=True
    ).reshape(devices * CAP * tpd, chans)

    cube = before.reshape(panel, chans, taps)
    cube = jnp.pad(cube, ((0, 0), (0, 0), (0, padded - taps)))
    cube = lax.dynamic_slice_in_dim(cube, tm_pos * tpd, tpd, 2)
    old = jnp.transpose(cube, (0, 2, 1)).reshape(panel, tpd * chans)

    got, rest, old, ahead_rows = lax.optimization_barrier((got, recording, old, ahead_rows))
    odd = unit_pos % 2
    head, held = rest[:padded], ahead_rows[:padded]
    beyond = lax.ppermute(
        jnp.where(odd == 1, held, head), AXES, [(i, i - 2) for i in range(2, devices)]
    )
    early = lax.ppermute(rest[cuts[1] : cuts[2]], "unit", pairs)
    late = lax.ppermute(rest[cuts[2] :], "unit", pairs)

    fresh = refine(key, got, old, tpd)
    rest, fresh = lax.optimization_barrier((rest, fresh))
    mine = fold(rest)
    own = spread(fresh)
    share = chans // tm_count
    width = 2 * keep * FOLD

    found = []
    for m in range(1, owners // 2):
        ahead = [(i, (i + 2 * m) % owners) for i in range(owners)]
        back = [(j, i) for i, j in ahead]
        chunk = lax.ppermute(fresh, "unit", ahead)
        if m == 1:
            own, chunk, mine, early = tie(across(own), chunk, mine, early)
            part = extract(tm_pos.astype(jnp.int32).reshape(1), own, chans, tpd, share)
            part = jnp.transpose(part[:taps, :, :share], (1, 2, 0)).reshape(panel, share * taps)
            other, late, part, beyond = tie(spread(chunk), late, part, beyond)
            windows = (mine, fold(ahead_rows, early), fold(
                jnp.where(odd == 1, beyond, held), late, jnp.where(odd == 1, head, beyond)
            ))
        else:
            other = spread(chunk)
        other = across(other)
        place = jnp.stack([tm_pos, odd, 0 * odd]).astype(jnp.int32)
        out = correlate(place, other, windows, chans, tpd, scale, width, jnp.bfloat16)
        found.append((lax.ppermute(out, "unit", back), ((unit_pos + 2 * m) % owners) // 2))
    place = jnp.stack([tm_pos, odd, unit_pos // 2]).astype(jnp.int32)
    place, _ = lax.optimization_barrier((place, out))
    scores = correlate(place, own, windows, chans, tpd, scale, owners // 2 * width, jnp.float32)
    for out, pair in found:
        scores = lax.dynamic_update_slice_in_dim(
            scores, out.astype(jnp.float32), pair * width, 1
        )
    return (part, scores)


def solution(mesh):
    in_specs = (P(AXES, None), P(AXES), P(AXES), P("unit", None))
    out_specs = (P("unit", "tm"), P("unit", "tm"))
    return jax.shard_map(body, mesh=mesh, in_specs=in_specs, out_specs=out_specs, check_vma=False)
```

```python
import functools

import jax
import jax.numpy as jnp
from jax import lax
from jax.experimental import pallas as pl
from jax.experimental.pallas import tpu as pltpu
from jax.sharding import PartitionSpec as P

STRIDE = 2
CAP = 8
FOLD = 4
ROWS = STRIDE * FOLD
AXES = ("tm", "unit")
MIB = 1024 * 1024
NT = (((1,), (1,)), ((), ()))


def params(mib):
    return pltpu.CompilerParams(vmem_limit_bytes=mib * MIB)


def pack_kernel(
    taps, panel, owners, tm_count, tpd, times_ref, labels_ref, base_ref, rec_ref, send_ref, buf, cnt
):
    spikes = times_ref.shape[0]
    sub_rows = rec_ref.shape[0]
    padded = tm_count * tpd
    win = padded + 16
    base = base_ref[0]
    for o in range(owners):
        cnt[o] = 0
    if owners * CAP > spikes:
        buf[...] = jnp.zeros_like(buf)
    tap = lax.broadcasted_iota(jnp.int32, (padded, win), 0)
    col = lax.broadcasted_iota(jnp.int32, (padded, win), 1)
    gap = jnp.where(tap < taps, col - tap, -1)

    def one(s):
        first = times_ref[s] - base
        start = jnp.minimum((first // 16) * 16, sub_rows - win)
        owner = labels_ref[s] // panel
        slot = cnt[owner]
        cnt[owner] = slot + 1
        pick = (gap == first - start).astype(jnp.bfloat16)
        window = rec_ref[pl.ds(pl.multiple_of(start, 16), win), :]
        snip = jnp.dot(pick, window, preferred_element_type=jnp.float32)
        for t in range(tm_count):
            row = (t * owners + owner) * (CAP * tpd) + slot * tpd
            buf[pl.ds(pl.multiple_of(row, tpd), tpd), :] = snip[t * tpd : (t + 1) * tpd]

    def group(g, carry):
        for i in range(8):
            one(g * 8 + i)
        return carry

    lax.fori_loop(0, spikes // 8, group, 0)
    send_ref[...] = buf[...].astype(jnp.bfloat16)


def pack(times, labels, base, rec, taps, panel, owners, tm_count, tpd):
    chans = rec.shape[1]
    rows = owners * tm_count * CAP * tpd
    smem = pl.BlockSpec(memory_space=pltpu.SMEM)
    vmem = pl.BlockSpec(memory_space=pltpu.VMEM)
    return pl.pallas_call(
        functools.partial(pack_kernel, taps, panel, owners, tm_count, tpd),
        out_shape=jax.ShapeDtypeStruct((rows, chans), jnp.bfloat16),
        in_specs=[smem, smem, smem, vmem],
        out_specs=vmem,
        scratch_shapes=[
            pltpu.VMEM((rows, chans), jnp.float32),
            pltpu.SMEM((owners,), jnp.int32),
        ],
        compiler_params=params(16),
        cost_estimate=pl.CostEstimate(flops=10**8, bytes_accessed=4 * 10**6, transcendentals=0),
        name="pack",
    )(times, labels, base, rec)


def fold_kernel(*refs):
    out_ref = refs[-1]
    chans = refs[0].shape[1]
    block = 16 * ROWS
    new = lax.broadcasted_iota(jnp.int32, (block, block), 0)
    old = lax.broadcasted_iota(jnp.int32, (block, block), 1)
    perm = (old == (new % 16) * ROWS + new // 16).astype(jnp.bfloat16)
    at = 0
    for ref in refs[:-1]:
        for low in range(0, ref.shape[0], block):
            size = min(block, ref.shape[0] - low)
            part = jnp.dot(perm[:, :size], ref[low : low + size, :], preferred_element_type=jnp.float32)
            part = part.astype(jnp.bfloat16)
            for r in range(ROWS):
                out_ref[at : at + 16, r * chans : (r + 1) * chans] = part[r * 16 : (r + 1) * 16]
            at += 16


def fold(*parts):
    chans = parts[0].shape[1]
    blocks = sum(-(-p.shape[0] // (16 * ROWS)) for p in parts)
    vmem = pl.BlockSpec(memory_space=pltpu.VMEM)
    return pl.pallas_call(
        fold_kernel,
        out_shape=jax.ShapeDtypeStruct((blocks * 16, ROWS * chans), jnp.bfloat16),
        in_specs=[vmem] * len(parts),
        out_specs=vmem,
        compiler_params=params(14),
        cost_estimate=pl.CostEstimate(flops=2 * 10**8, bytes_accessed=4 * 10**6, transcendentals=0),
        name="fold",
    )(*parts)


def refine_kernel(tpd, key_ref, got_ref, old_ref, out_ref, sums):
    panel = old_ref.shape[0]
    rows, chans = got_ref.shape
    step = min(rows, 2048)
    count = jnp.zeros((panel, 1), jnp.float32)
    for b in range(rows // step):
        key = key_ref[:, b * step : (b + 1) * step]
        wanted = lax.broadcasted_iota(jnp.int32, (tpd * panel, step), 0)
        wanted = (wanted % panel) * tpd + wanted // panel
        hit = (wanted == key).astype(jnp.float32)
        count = count + jnp.sum(hit[:panel], axis=1, keepdims=True)
        part = jnp.dot(
            hit.astype(jnp.bfloat16),
            got_ref[b * step : (b + 1) * step, :],
            preferred_element_type=jnp.float32,
        )
        if b == 0:
            sums[...] = part
        else:
            sums[...] += part
    weight = count / (count + 4.0)
    most = jnp.maximum(count, 1.0)
    for t in range(tpd):
        base = old_ref[:, t * chans : (t + 1) * chans].astype(jnp.float32)
        mean = sums[t * panel : (t + 1) * panel, :] / most
        out_ref[:, t * chans : (t + 1) * chans] = (base + weight * (mean - base)).astype(jnp.bfloat16)


def refine(key, got, old, tpd):
    vmem = pl.BlockSpec(memory_space=pltpu.VMEM)
    panel = old.shape[0]
    return pl.pallas_call(
        functools.partial(refine_kernel, tpd),
        out_shape=jax.ShapeDtypeStruct(old.shape, jnp.bfloat16),
        in_specs=[vmem] * 3,
        out_specs=vmem,
        scratch_shapes=[pltpu.VMEM((tpd * panel, got.shape[1]), jnp.float32)],
        compiler_params=params(20),
        cost_estimate=pl.CostEstimate(flops=8 * 10**8, bytes_accessed=3 * 10**6, transcendentals=0),
        name="refine",
    )(key, got, old)


def extract_kernel(chans, tpd, share, masks, place_ref, *refs):
    pieces, out_ref = refs[:-1], refs[-1]
    half_rows = pieces[0].shape[1]
    wide = out_ref.shape[2]
    me = place_ref[0]
    channel = lax.broadcasted_iota(jnp.int32, (chans, wide), 0)
    lane = lax.broadcasted_iota(jnp.int32, (chans, wide), 1)
    pick = ((channel == me * share + lane) & (lane < share)).astype(jnp.bfloat16)
    for ref, (part_of, items) in zip(pieces, masks):
        rows = slice(part_of * half_rows, (part_of + 1) * half_rows)
        for at, mask in enumerate(items):
            first = jnp.bitwise_xor(me, mask) * tpd
            for t in range(tpd):
                taken = jnp.dot(
                    ref[at, :, t * chans : (t + 1) * chans], pick, preferred_element_type=jnp.float32
                )
                out_ref[first + t, rows, :] = taken.astype(jnp.bfloat16)


def extract(me, gathered, chans, tpd, share):
    pieces = [value for value, _, _ in gathered]
    masks = [(part_of, items) for _, part_of, items in gathered]
    taps = sum(len(items) for _, items in masks) // 2 * tpd
    vmem = pl.BlockSpec(memory_space=pltpu.VMEM)
    return pl.pallas_call(
        functools.partial(extract_kernel, chans, tpd, share, masks),
        out_shape=jax.ShapeDtypeStruct((taps, 2 * pieces[0].shape[1], -(-share // 128) * 128), jnp.bfloat16),
        in_specs=[pl.BlockSpec(memory_space=pltpu.SMEM)] + [vmem] * len(pieces),
        out_specs=vmem,
        compiler_params=params(14),
        cost_estimate=pl.CostEstimate(flops=4 * 10**8, bytes_accessed=4 * 10**6, transcendentals=0),
        name="extract",
    )(me, *pieces)


def correlate_kernel(chans, tpd, scale, masks, place_ref, *refs):
    count = len(masks)
    pieces, rest = refs[:count], refs[count:]
    mine_ref, early_ref, late_ref, out_ref, t_buf, e_buf, rhs, part, acc = rest
    half_rows = pieces[0].shape[1]
    lanes = tpd * chans
    blocks, panel, depth = t_buf.shape
    per = depth // lanes
    height = e_buf.shape[0] // 2
    keep = acc.shape[0] // 2
    shift = STRIDE * chans
    me, odd, pair = place_ref[0], place_ref[1], place_ref[2]
    early = early_ref.shape[0]
    e_buf[0:keep, :] = mine_ref[...]
    e_buf[keep:height, :] = late_ref[0 : height - keep, :]
    e_buf[height : height + early, :] = early_ref[...]
    e_buf[height + early :, :] = late_ref[height - keep :, :]
    for ref, (part_of, items) in zip(pieces, masks):
        rows = slice(part_of * half_rows, (part_of + 1) * half_rows)
        for at, mask in enumerate(items):
            chunk = jnp.bitwise_xor(me, mask)
            if per == 1:
                t_buf[chunk, rows, :] = ref[at]
            else:
                first = pl.multiple_of(chunk % per * lanes, 128)
                t_buf[chunk // per, rows, pl.ds(first, lanes)] = ref[at]
    for a in range(blocks + 1):
        used = depth if a < blocks else depth // 2
        for q in range(FOLD):
            rows = slice(q * panel, (q + 1) * panel)
            cut = q * shift
            low = min(cut, used)
            if low > 0:
                if a > 0:
                    rhs[rows, 0:low] = t_buf[a - 1, :, depth - cut : depth - cut + low]
                else:
                    rhs[rows, 0:low] = jnp.zeros((panel, low), jnp.bfloat16)
            if cut < used:
                if a < blocks:
                    rhs[rows, cut:used] = t_buf[a, :, 0 : used - cut]
                else:
                    rhs[rows, cut:used] = jnp.zeros((panel, used - cut), jnp.bfloat16)
        part[...] = lax.dot_general(
            e_buf[:, 0:used], rhs[:, 0:used], NT, preferred_element_type=jnp.float32
        )
        for h in range(2):
            found = part[h * height + a : h * height + a + keep, :]
            if a == 0:
                acc[h * keep : (h + 1) * keep, :] = found
            else:
                acc[h * keep : (h + 1) * keep, :] += found
    width = 128
    place = lax.broadcasted_iota(jnp.int32, (FOLD * width, FOLD * width), 0)
    lane = lax.broadcasted_iota(jnp.int32, (FOLD * width, FOLD * width), 1)
    weave = (lane == (place % width) * FOLD + place // width).astype(jnp.bfloat16)
    per_half = keep // width
    for h in range(2):
        side = odd if h == 0 else 1 - odd
        for b in range(per_half):
            first = h * keep + b * width
            turned = acc[first : first + width, :].T * scale
            row = jnp.concatenate([turned[q * panel : (q + 1) * panel] for q in range(FOLD)], axis=1)
            high = row.astype(jnp.bfloat16)
            found = jnp.dot(high, weave, preferred_element_type=jnp.float32)
            if out_ref.dtype == jnp.float32:
                rest = (row - high.astype(jnp.float32)).astype(jnp.bfloat16)
                found = found + jnp.dot(rest, weave, preferred_element_type=jnp.float32)
            at = ((2 * pair + side) * per_half + b) * (FOLD * width)
            at = pl.multiple_of(at, FOLD * width)
            out_ref[:, pl.ds(at, FOLD * width)] = found.astype(out_ref.dtype)


def correlate(place, gathered, windows, chans, tpd, scale, width, dtype):
    pieces = [value for value, _, _ in gathered]
    masks = [(part_of, items) for _, part_of, items in gathered]
    panel = 2 * pieces[0].shape[1]
    chunks = sum(len(items) for _, items in masks) // 2
    keep = windows[0].shape[0]
    height = keep + 16
    depth = ROWS * chans
    vmem = pl.BlockSpec(memory_space=pltpu.VMEM)
    return pl.pallas_call(
        functools.partial(correlate_kernel, chans, tpd, scale, masks),
        out_shape=jax.ShapeDtypeStruct((panel, width), dtype),
        in_specs=[pl.BlockSpec(memory_space=pltpu.SMEM)] + [vmem] * (len(pieces) + 3),
        out_specs=vmem,
        scratch_shapes=[
            pltpu.VMEM((chunks * tpd // ROWS, panel, depth), jnp.bfloat16),
            pltpu.VMEM((2 * height, depth), jnp.bfloat16),
            pltpu.VMEM((FOLD * panel, depth), jnp.bfloat16),
            pltpu.VMEM((2 * height, FOLD * panel), jnp.float32),
            pltpu.VMEM((2 * keep, FOLD * panel), jnp.float32),
        ],
        compiler_params=params(22),
        cost_estimate=pl.CostEstimate(flops=8 * 10**9, bytes_accessed=8 * 10**6, transcendentals=0),
        name="correlate",
    )(place, *pieces, *windows)


def swap(value, bit):
    size = lax.axis_size("tm")
    return lax.ppermute(value, "tm", [(i, i ^ bit) for i in range(size)])


def spread(value):
    bits = []
    while 2 << len(bits) < lax.axis_size("tm"):
        bits.append(2 << len(bits))
    rows = value.shape[0] // 2
    out = []
    for part_of, order in enumerate((bits[::-1], bits)):
        parts = [(value[part_of * rows : (part_of + 1) * rows][None], [0])]
        for bit in order:
            held = jnp.concatenate([v for v, _ in parts], axis=0) if len(parts) > 1 else parts[0][0]
            items = [m for _, ms in parts for m in ms]
            parts = [(held, items), (swap(held, bit), [m ^ bit for m in items])]
        out += [(v, part_of, ms) for v, ms in parts]
    return out


def across(parts):
    return parts + [(swap(v, 1), part_of, [m ^ 1 for m in ms]) for v, part_of, ms in parts]


def tie(parts, *beside):
    done = lax.optimization_barrier((*beside, *[v for v, _, _ in parts]))
    tied = [(v, n, ms) for v, (_, n, ms) in zip(done[len(beside) :], parts)]
    return tied, *done[: len(beside)]


def body(recording, spike_times, unit_labels, old_templates):
    sub_rows, chans = recording.shape
    panel, feat = old_templates.shape
    taps = feat // chans
    half = (taps - 1) // 2
    owners = lax.axis_size("unit")
    tm_count = lax.axis_size("tm")
    devices = owners * tm_count
    spikes = spike_times.shape[0]
    tm_pos = lax.axis_index("tm")
    unit_pos = lax.axis_index("unit")
    flat_pos = tm_pos * owners + unit_pos
    tpd = -(-taps // tm_count)
    padded = tpd * tm_count
    keep = sub_rows // ROWS
    scale = 1.0 / (float(feat) ** 0.5)

    base = (flat_pos * sub_rows + half).astype(jnp.int32).reshape(1)
    groups = padded // ROWS
    send = pack(spike_times, unit_labels, base, recording, taps, panel, owners, groups, ROWS)
    if tpd != ROWS:
        send = send.reshape(groups, owners, CAP, ROWS // tpd, tpd, chans)
        send = jnp.transpose(send, (0, 3, 1, 2, 4, 5))
    owner = unit_labels // panel
    hits = (owner[:, None] == jnp.arange(owners)[None, :]).astype(jnp.int32)
    rank = jnp.sum((jnp.cumsum(hits, axis=0) - hits) * hits, axis=1)
    placing = jnp.arange(owners * CAP)[:, None] == (owner * CAP + rank)[None, :]
    tags = jnp.sum(jnp.where(placing, (unit_labels % panel + 1)[None, :], 0), axis=1) - 1
    tags = jnp.broadcast_to(tags.reshape(1, owners, CAP), (tm_count, owners, CAP))
    tags = tags.reshape(devices, CAP)
    tags = lax.all_to_all(tags, AXES, split_axis=0, concat_axis=0, tiled=True)
    key = (tags[:, :, None] * tpd + jnp.arange(tpd)[None, None, :]).reshape(1, -1)
    send, key, before, ahead_rows = lax.optimization_barrier((send, key, old_templates, recording))
    pairs = [(i, i ^ 1) for i in range(owners)]
    unit_rows = 16 * ROWS
    first = sub_rows * 7 // 16 // unit_rows * unit_rows
    ahead_rows = lax.ppermute(ahead_rows[:first], "unit", pairs)
    got = lax.all_to_all(
        send.reshape(devices, CAP * tpd, chans), AXES, split_axis=0, concat_axis=0, tiled=True
    ).reshape(devices * CAP * tpd, chans)

    cube = before.reshape(panel, chans, taps)
    cube = jnp.pad(cube, ((0, 0), (0, 0), (0, padded - taps)))
    cube = lax.dynamic_slice_in_dim(cube, tm_pos * tpd, tpd, 2)
    old = jnp.transpose(cube, (0, 2, 1)).reshape(panel, tpd * chans)

    got, rest, old, ahead_rows = lax.optimization_barrier((got, recording, old, ahead_rows))
    odd = unit_pos % 2
    head, held = rest[:padded], ahead_rows[:padded]
    beyond = lax.ppermute(
        jnp.where(odd == 1, held, head), AXES, [(i, i - 2) for i in range(2, devices)]
    )
    late = lax.ppermute(rest[first:], "unit", pairs)

    fresh = refine(key, got, old, tpd)
    rest, fresh = lax.optimization_barrier((rest, fresh))
    mine = fold(rest)
    own = spread(fresh)
    share = chans // tm_count
    width = 2 * keep * FOLD

    found = []
    for m in range(1, owners // 2):
        ahead = [(i, (i + 2 * m) % owners) for i in range(owners)]
        back = [(j, i) for i, j in ahead]
        chunk = lax.ppermute(fresh, "unit", ahead)
        if m == 1:
            own, chunk, mine = tie(across(own), chunk, mine)
            part = extract(tm_pos.astype(jnp.int32).reshape(1), own, chans, tpd, share)
            part = jnp.transpose(part[:taps, :, :share], (1, 2, 0)).reshape(panel, share * taps)
            other, late, part, beyond = tie(spread(chunk), late, part, beyond)
            windows = (mine, fold(ahead_rows), fold(
                jnp.where(odd == 1, beyond, held), late, jnp.where(odd == 1, head, beyond)
            ))
        else:
            other = spread(chunk)
        other = across(other)
        place = jnp.stack([tm_pos, odd, 0 * odd]).astype(jnp.int32)
        out = correlate(place, other, windows, chans, tpd, scale, width, jnp.bfloat16)
        found.append((lax.ppermute(out, "unit", back), ((unit_pos + 2 * m) % owners) // 2))
    place = jnp.stack([tm_pos, odd, unit_pos // 2]).astype(jnp.int32)
    place, _ = lax.optimization_barrier((place, out))
    scores = correlate(place, own, windows, chans, tpd, scale, owners // 2 * width, jnp.float32)
    for out, pair in found:
        scores = lax.dynamic_update_slice_in_dim(
            scores, out.astype(jnp.float32), pair * width, 1
        )
    return (part, scores)


def solution(mesh):
    in_specs = (P(AXES, None), P(AXES), P(AXES), P("unit", None))
    out_specs = (P("unit", "tm"), P("unit", "tm"))
    return jax.shard_map(body, mesh=mesh, in_specs=in_specs, out_specs=out_specs, check_vma=False)
```
